32 devices in a mesh: dp: 8 (over y, x, core), tensor: 4 (over z).
Axes of the slice: x: 2, y: 2, z: 4, core: 2. Of those that a mesh axis runs over, the one named last changes fastest.
Arguments:
- tokens: bfloat16 [16384, 768], P('dp'), may hold values from -6 to 6
- w_query: bfloat16 [768, 768], P(None, 'tensor'), may hold values from -0.21875 to 0.21875
- b_query: bfloat16 [768], P('tensor'), may hold values from -3 to 3
- w_key: bfloat16 [768, 768], P(None, 'tensor'), may hold values from -0.21875 to 0.21875
- w_value: bfloat16 [768, 768], P(None, 'tensor'), may hold values from -0.21875 to 0.21875
- b_value: bfloat16 [768], P('tensor'), may hold values from -3 to 3
- w_attn_out: bfloat16 [768, 768], P('tensor'), may hold values from -0.875 to 0.875
- b_attn_out: bfloat16 [768], replicated, may hold values from -3 to 3
- gain_one: bfloat16 [768], replicated, may hold values from 0.5 to 1.5
- shift_one: bfloat16 [768], replicated, may hold values from -2 to 2
- w_inner: bfloat16 [768, 3072], P(None, 'tensor'), may hold values from -0.21875 to 0.21875
- b_inner: bfloat16 [3072], P('tensor'), may hold values from -3 to 3
- w_outer: bfloat16 [3072, 768], P('tensor'), may hold values from -0.109375 to 0.109375
- b_outer: bfloat16 [768], replicated, may hold values from -3 to 3
- gain_two: bfloat16 [768], replicated, may hold values from 0.5 to 1.5
- shift_two: bfloat16 [768], replicated, may hold values from -2 to 2
- cotangent: bfloat16 [16384, 768], P('dp'), may hold values from -6 to 6
- lengths: int32 [32], P('dp'), may hold values from 1 to 512, 12288 in all
- row_ids: int32 [32, 512], P('dp'), may hold values from 0 to 63
- col_ids: int32 [32, 512], P('dp'), may hold values from 0 to 7
Outputs:
- layer_out: bfloat16 [16384, 768], P('dp')
- grad_tokens: bfloat16 [16384, 768], P('dp')
- grad_w_query: float32 [768, 768], P(None, 'tensor')
- grad_b_query: float32 [768], P('tensor')
- grad_w_key: float32 [768, 768], P(None, 'tensor')
- grad_w_value: float32 [768, 768], P(None, 'tensor')
- grad_b_value: float32 [768], P('tensor')
- grad_w_attn_out: float32 [768, 768], P('tensor')
- grad_b_attn_out: float32 [768], replicated
- grad_gain_one: float32 [768], replicated
- grad_shift_one: float32 [768], replicated
- grad_w_inner: float32 [768, 3072], P(None, 'tensor')
- grad_b_inner: float32 [3072], P('tensor')
- grad_w_outer: float32 [3072, 768], P('tensor')
- grad_b_outer: float32 [768], replicated
- grad_gain_two: float32 [768], replicated
- grad_shift_two: float32 [768], replicated
The draws below stay inside these ranges and needn't reach their ends.
Inputs may be any that keep to these rules, and one draw needn't show every extreme that they name: `lengths`: the longest table in every draw has exactly 512 real tokens; positions from a table's length on are padding.
All inputs are finite; a program needn't handle non-finite values. No bound on the sum of `lengths` on one device may be relied on, other than what follows from the above.
Results may differ from the reference program's by a relative error of at most 0.022.
Values may be sent and summed in bfloat16 or wider, within the bound.
No kernel may reach another device: no remote copies, remote signals or barrier semaphores. Data moves between devices by JAX's collectives and lax.ppermute only.
A program may use at most 128 MiB of HBM per device.

```python
import math
import jax
import jax.numpy as jnp
import numpy as np
from jax import lax

D = 768
HEADS = 12
FF = 3072
SEQ = 512
HD = 64
TABLES = 32
TOKENS = 16384
N_DP = 8
N_TENSOR = 4


def set_ends(entries, rng, smallest, high):
    spot = [jax.random.randint(jax.random.fold_in(rng, axis), (), 0, length) for axis, length in enumerate(entries.shape)]
    widest = entries.shape.index(max(entries.shape))
    next_to = spot[:widest] + [(spot[widest] + 1) % entries.shape[widest]] + spot[widest + 1:]
    return entries.at[tuple(spot)].set(smallest).at[tuple(next_to)].set(high)


def block_scale(rng, extent, split, least, largest):
    def one(dim, shards_of):
        steps = jax.random.uniform(jax.random.fold_in(jax.random.fold_in(rng, 6), dim), (shards_of,), jnp.float32, least / len(split), largest / len(split))
        return jnp.repeat(jnp.exp(steps), extent[dim] // shards_of).reshape((-1,) + (1,) * (len(extent) - dim - 1))

    level = one(*split[0])
    for cut in split[1:]:
        level = level * one(*cut)
    return level


def split_up(number_of, total, most, lean):
    weights = [(1 << 20) // math.isqrt(rank ** lean) + 1 for rank in range(2, number_of + 1)]
    surplus, counts = total - most - (number_of - 1), [1] * (number_of - 1)
    while surplus > 0:
        movable = [i for i in range(number_of - 1) if counts[i] < most]
        whole, left = sum([weights[i] for i in movable]), surplus
        for i in movable:
            extra = min(most - counts[i], max(1, left * weights[i] // whole), surplus)
            counts[i] = counts[i] + extra
            surplus = surplus - extra
    return np.array([most] + counts)


def uneven_parts(stream_key, number_of, total, reach, slope):
    if number_of == 2:
        one = jax.random.randint(stream_key, (), max(1, total - reach), min(reach, total - 1) + 1)
        return jnp.stack([one, total - one])
    tallies = jnp.asarray(split_up(number_of, total, reach, slope), jnp.int32)
    pairs = (number_of - 1) // 2
    giver, taker = tallies[1:1 + 2 * pairs:2], tallies[2:2 + 2 * pairs:2]
    room = jnp.minimum(giver - 1, reach - taker)
    shifted = jax.random.randint(jax.random.fold_in(stream_key, 1), (pairs,), 0, 1 << 20) % (room + 1)
    tallies = tallies.at[1:1 + 2 * pairs:2].set(giver - shifted).at[2:2 + 2 * pairs:2].set(taker + shifted)
    return tallies[jax.random.permutation(jax.random.fold_in(stream_key, 2), number_of)]


def normal_values(stream_key, dims, deviation, most, shards=(), dtype=jnp.bfloat16):
    entries = deviation * jax.random.normal(stream_key, dims, jnp.float32)
    if shards:
        entries = entries * block_scale(stream_key, dims, shards, -0.22, 0.18)
    return jnp.clip(entries, -most, most).astype(dtype)


def setup_inputs(seed: int = 0) -> dict:
    seeds = jax.random.split(jax.random.key(seed), 21)
    tokens = normal_values(seeds[0], (TOKENS, D), 1.0, 6.0, ((0, 8),))
    w_query = normal_values(seeds[1], (D, D), D ** -0.5, 0.21875, ((1, 4),))
    b_query = normal_values(seeds[2], (D,), 0.5, 3.0, ((0, 4),))
    w_key = normal_values(seeds[3], (D, D), D ** -0.5, 0.21875, ((1, 4),))
    w_value = normal_values(seeds[4], (D, D), D ** -0.5, 0.21875, ((1, 4),))
    b_value = normal_values(seeds[5], (D,), 0.5, 3.0, ((0, 4),))
    w_attn_out = normal_values(seeds[6], (D, D), (D // 16) ** -0.5, 0.875, ((0, 4),))
    b_attn_out = normal_values(seeds[7], (D,), 0.5, 3.0)
    gain_one = jnp.clip(1.0 + 0.1 * jax.random.normal(seeds[8], (D,), jnp.float32), 0.5, 1.5).astype(jnp.bfloat16)
    shift_one = normal_values(seeds[9], (D,), 0.3, 2.0)
    w_inner = normal_values(seeds[10], (D, FF), D ** -0.5, 0.21875, ((1, 4),))
    b_inner = normal_values(seeds[11], (FF,), 0.5, 3.0, ((0, 4),))
    w_outer = normal_values(seeds[12], (FF, D), FF ** -0.5, 0.109375, ((0, 4),))
    b_outer = normal_values(seeds[13], (D,), 0.5, 3.0)
    gain_two = jnp.clip(1.0 + 0.1 * jax.random.normal(seeds[14], (D,), jnp.float32), 0.5, 1.5).astype(jnp.bfloat16)
    shift_two = normal_values(seeds[15], (D,), 0.3, 2.0)
    cotangent = normal_values(seeds[16], (TOKENS, D), 1.0, 6.0, ((0, 8),))
    lengths = uneven_parts(seeds[17], TABLES, 3 * TABLES * SEQ // 4, SEQ, 2).astype(jnp.int32)
    row_ids = set_ends(jax.random.randint(seeds[18], (TABLES, SEQ), 0, SEQ // 8), jax.random.fold_in(seeds[18], 1), 0, (SEQ // 8) - 1).astype(jnp.int32)
    col_ids = set_ends(jax.random.randint(seeds[19], (TABLES, SEQ), 0, max(SEQ // 64, 4)), jax.random.fold_in(seeds[19], 1), 0, (max(SEQ // 64, 4)) - 1).astype(jnp.int32)
    return dict(tokens=tokens, w_query=w_query, b_query=b_query, w_key=w_key, w_value=w_value, b_value=b_value, w_attn_out=w_attn_out, b_attn_out=b_attn_out, gain_one=gain_one, shift_one=shift_one, w_inner=w_inner, b_inner=b_inner, w_outer=w_outer, b_outer=b_outer, gain_two=gain_two, shift_two=shift_two, cotangent=cotangent, lengths=lengths, row_ids=row_ids, col_ids=col_ids)


@jax.custom_vjp
def low(v):
    return lax.optimization_barrier(v.astype(jnp.bfloat16)).astype(jnp.float32)

@jax.custom_vjp
def low_back(v):
    return v

def low_keep(v):
    return (low(v), None)

def low_pass(kept, grad):
    return (grad,)

def back_keep(v):
    return (v, None)

def back_low(kept, grad):
    return (low(grad),)
low.defvjp(low_keep, low_pass)
low_back.defvjp(back_keep, back_low)
epsilon = 1e-12
masked_value = -1e+30

def matmul_high(left_side, right_side):
    return jnp.dot(left_side, right_side, precision=lax.Precision.HIGHEST)

def normalize(residual, gain_vec, shift_vec):
    centre = residual - lax.optimization_barrier(jnp.mean(residual, axis=-1, keepdims=True))
    spread = lax.optimization_barrier(jnp.mean(centre * centre, axis=-1, keepdims=True))
    return centre * lax.rsqrt(spread + epsilon) * gain_vec + shift_vec

def visibility(length, row_tags, col_tags, head_type):
    position = jnp.arange(row_tags.shape[0])
    present = position[None, :] < length
    leading = position[None, :] == 0
    same_row = row_tags[:, None] == row_tags[None, :]
    same_col = col_tags[:, None] == col_tags[None, :]
    kinds = head_type[:, None, None]
    allowed = (kinds == 0) | (kinds == 1) & same_row[None] | (kinds == 2) & same_col[None]
    return present[None] & (allowed | leading[None])

def table_attention(pieces):
    queries, key_rows, values, length, row_tags, col_tags = pieces
    head_type = jnp.arange(HEADS) % 3
    logits = low_back(jnp.einsum('qhd,khd->hqk', queries, key_rows, precision=lax.Precision.HIGHEST))
    scores = jnp.where(visibility(length, row_tags, col_tags, head_type), logits * HD ** (-0.5), masked_value)
    chances = low(jax.nn.softmax(scores, axis=-1))
    return jnp.einsum('hqk,khd->qhd', chances, values, precision=lax.Precision.HIGHEST)

def layer(params, group_tokens, group_len, group_rows, group_cols):
    w_query, b_query, w_key, w_value, b_value, w_attn_out, b_attn_out, gain_one, shift_one, w_inner, b_inner, w_outer, b_outer, gain_two, shift_two = params
    shard_width = D // N_TENSOR
    hidden_width = FF // N_TENSOR
    parts_q, parts_k, parts_v = ([], [], [])
    for tensor_part in range(N_TENSOR):
        window = slice(tensor_part * shard_width, (tensor_part + 1) * shard_width)
        shard_input = low_back(group_tokens)
        parts_q.append(low(low_back(matmul_high(shard_input, w_query[:, window])) + b_query[window]))
        parts_k.append(low(low_back(matmul_high(shard_input, w_key[:, window]))))
        parts_v.append(low(low_back(matmul_high(shard_input, w_value[:, window])) + b_value[window]))
    head_shape = (group_len.shape[0], SEQ, HEADS, HD)
    queries = jnp.concatenate(parts_q, axis=1).reshape(head_shape)
    key_rows = jnp.concatenate(parts_k, axis=1).reshape(head_shape)
    values = jnp.concatenate(parts_v, axis=1).reshape(head_shape)
    blended = lax.map(jax.checkpoint(table_attention), (queries, key_rows, values, group_len, group_rows, group_cols))
    blended = low(low_back(blended.reshape(group_tokens.shape[0], D)))
    attn_terms = []
    for tensor_part in range(N_TENSOR):
        window = slice(tensor_part * shard_width, (tensor_part + 1) * shard_width)
        attn_terms.append(low(matmul_high(blended[:, window], w_attn_out[window, :])))
    attn_sum = attn_terms[0]
    for member in attn_terms[1:]:
        attn_sum = attn_sum + member
    resid_one = group_tokens + low_back(attn_sum) + b_attn_out
    hidden_one = normalize(resid_one, gain_one, shift_one)
    hidden_low = low(hidden_one)
    ffn_terms = []
    for tensor_part in range(N_TENSOR):
        window = slice(tensor_part * hidden_width, (tensor_part + 1) * hidden_width)
        shard_input = low_back(hidden_low)
        inner_pre = low_back(matmul_high(shard_input, w_inner[:, window])) + b_inner[window]
        activated = low(jax.nn.gelu(inner_pre, approximate=False))
        ffn_terms.append(low(matmul_high(activated, w_outer[window, :])))
    ffn_sum = ffn_terms[0]
    for member in ffn_terms[1:]:
        ffn_sum = ffn_sum + member
    resid_two = hidden_one + low_back(ffn_sum) + b_outer
    return normalize(resid_two, gain_two, shift_two)

def reference(tokens, w_query, b_query, w_key, w_value, b_value, w_attn_out, b_attn_out, gain_one, shift_one, w_inner, b_inner, w_outer, b_outer, gain_two, shift_two, cotangent, lengths, row_ids, col_ids):
    params = tuple((member.astype(jnp.float32) for member in (w_query, b_query, w_key, w_value, b_value, w_attn_out, b_attn_out, gain_one, shift_one, w_inner, b_inner, w_outer, b_outer, gain_two, shift_two)))
    per_group = lengths.shape[0] // N_DP
    rows_group = per_group * SEQ
    slabs = tokens.astype(jnp.float32).reshape(N_DP, rows_group, D)
    upstream = cotangent.astype(jnp.float32).reshape(N_DP, rows_group, D)

    def group_step(summed, pieces):
        group_tokens, pull_in, group_len, group_rows, group_cols = pieces

        def forward(weights, inputs):
            return layer(weights, inputs, group_len, group_rows, group_cols)
        result, pullback = jax.vjp(forward, params, group_tokens)
        grads, grad_group = pullback(pull_in)
        summed = jax.tree.map(jnp.add, summed, grads)
        return (summed, (result.astype(jnp.bfloat16), grad_group.astype(jnp.bfloat16)))
    zero_grads = jax.tree.map(jnp.zeros_like, params)
    summed, (results, grad_rows) = lax.scan(group_step, zero_grads, (slabs, upstream, lengths.reshape(N_DP, per_group), row_ids.reshape(N_DP, per_group, SEQ), col_ids.reshape(N_DP, per_group, SEQ)))
    return (results.reshape(-1, D), grad_rows.reshape(-1, D), summed[0], summed[1], summed[2], summed[3], summed[4], summed[5], summed[6], summed[7], summed[8], summed[9], summed[10], summed[11], summed[12], summed[13], summed[14])
```

```python
import functools

import jax
import jax.numpy as jnp
from jax import lax
from jax.experimental import pallas as pl
from jax.experimental.pallas import tpu as pltpu
from jax.sharding import PartitionSpec as P

F32 = jnp.float32
BF = jnp.bfloat16
HD = 64
D = 768
HALF = D // 2
BLOCKS = 4
QKV = 48
epsilon = 1e-12
masked_value = -1e30
CHUNK = 128

NN = (((1,), (0,)), ((), ()))
NT = (((1,), (1,)), ((), ()))
TN = (((0,), (0,)), ((), ()))


def product(left, right, dims):
    return lax.dot_general(left, right, dims, preferred_element_type=F32)


def shape_of(shape, dtype):
    return jax.ShapeDtypeStruct(shape, dtype)


def whole(shape):
    return pl.BlockSpec(shape, lambda r, *_: (0,) * len(shape))


def each(shape, shift=0):
    return pl.BlockSpec((1,) + shape, lambda r, *_: (r + shift,) + (0,) * len(shape))


def params():
    return pltpu.CompilerParams(vmem_limit_bytes=56 * 1024 * 1024)


def cost(flops, moved, exps=0):
    return pl.CostEstimate(flops=int(flops), bytes_accessed=int(moved), transcendentals=int(exps))


def rows_of(ref, kind):
    width = 3 * QKV
    return jnp.concatenate(
        [ref[0, width * j + QKV * kind : width * j + QKV * (kind + 1)] for j in range(BLOCKS)], axis=0
    )


class Masks:
    def __init__(self, length, row_q, col_q, row_k, col_k):
        position = lax.broadcasted_iota(jnp.int32, (row_k.shape[0], 1), 0)
        self.here = position < length
        self.leading = position == 0
        self.row_k = jnp.where(self.here, row_k, -1)
        self.col_k = jnp.where(self.here, col_k, -1)
        self.row_q, self.col_q = row_q, col_q

    def scores(self, logits, kind):
        if kind == 0:
            visible = self.here
        elif kind == 1:
            visible = (self.row_k == self.row_q) | self.leading
        else:
            visible = (self.col_k == self.col_q) | self.leading
        return jnp.where(visible, logits, masked_value)


def projection_rows(w_ref):
    return jnp.concatenate([w_ref[0, 4 * QKV * j : 4 * QKV * j + 3 * QKV] for j in range(BLOCKS)], axis=0)


def output_rows(w_ref, shard=0):
    return jnp.concatenate(
        [w_ref[shard, 4 * QKV * j + 3 * QKV : 4 * QKV * (j + 1)] for j in range(BLOCKS)], axis=0
    )


def as_column(row):
    return jnp.broadcast_to(row, (8, row.shape[1])).T[:, 0:1]


def attention_forward_kernel(
    scalars, x_ref, w_ref, b_ref, rq_ref, cq_ref, rk_ref, ck_ref, *rest
):
    qkv_ref, o_ref, lse_ref = rest[-3:]
    seq = x_ref.shape[0]
    qkv = product(projection_rows(w_ref), x_ref[...], NT) + as_column(b_ref[0])
    low = qkv.astype(BF)
    is_query = lax.broadcasted_iota(jnp.int32, (qkv.shape[0], 1), 0) % (3 * QKV) < QKV
    low = jnp.where(is_query, low * jnp.asarray(HD**-0.5, BF), low)
    qkv_ref[0] = low
    masks = Masks(scalars[0], rq_ref[...], cq_ref[...], rk_ref[...], ck_ref[...])
    q_t, k_t, v_t = rows_of(qkv_ref, 0), rows_of(qkv_ref, 1), rows_of(qkv_ref, 2)
    outs, logs = [], []
    for head in range(q_t.shape[0] // HD):
        rows = slice(HD * head, HD * (head + 1))
        scores = masks.scores(product(k_t[rows].T, q_t[rows], NN), head % 3)
        highest = jnp.max(scores, axis=0, keepdims=True)
        weights = jnp.exp(scores - highest).astype(BF)
        with_ones = jnp.concatenate([v_t[rows], jnp.ones((16, seq), BF)], axis=0)
        blended = product(with_ones, weights, NN)
        total = blended[HD : HD + 1]
        outs.append(blended[:HD] * (1.0 / total))
        logs.append(highest + jnp.log(total))
    o_ref[0] = jnp.concatenate(outs, axis=0).astype(BF)
    logs.append(jnp.zeros((8 - len(logs), seq), F32))
    lse_ref[0] = jnp.concatenate(logs, axis=0)


def attention_forward(scalars, x, weights, bias, ids, shards, first, carried=None):
    count, wide, seq = weights.shape[0] - (first if carried else 0), 3 * BLOCKS * QKV, x.shape[0]
    at = first if carried else 0
    out_shape = [
        shape_of((shards, wide, seq), BF),
        shape_of((shards, wide // 3, seq), BF),
        shape_of((shards, 8, seq), F32),
    ]
    kept = list(carried) if carried else []
    return pl.pallas_call(
        attention_forward_kernel,
        grid_spec=pltpu.PrefetchScalarGridSpec(
            num_scalar_prefetch=1,
            grid=(count,),
            in_specs=[
                whole((seq, D)),
                each((weights.shape[1], D), at),
                each((1, wide), first),
                whole((1, seq)),
                whole((1, seq)),
                whole((seq, 1)),
                whole((seq, 1)),
            ]
            + [pl.BlockSpec(memory_space=pl.ANY)] * len(kept),
            out_specs=[each(s.shape[1:], first) for s in out_shape],
        ),
        out_shape=out_shape,
        input_output_aliases={8 + i: i for i in range(len(kept))},
        compiler_params=params(),
        cost_estimate=cost(count * 4e9, count * 3e6),
    )(scalars, x, weights, bias, *ids, *kept)


def attention_backward_kernel(
    scalars, x_ref, w_ref, qkv_ref, o_ref, lse_ref, up_ref, start_ref, rq_ref, cq_ref, rk_ref, ck_ref,
    dx_ref, mine_ref, other_ref, db_ref, acc_ref, d_ref, low_ref,
):
    r, last = pl.program_id(0), pl.num_programs(0) - 1
    seq = x_ref.shape[0]

    @pl.when(r == 0)
    def _():
        acc_ref[...] = start_ref[...]
        low_ref[...] = up_ref[...].astype(BF)

    masks = Masks(scalars[0], rq_ref[...], cq_ref[...], rk_ref[...], ck_ref[...])
    q_t, k_t, v_t = rows_of(qkv_ref, 0), rows_of(qkv_ref, 1), rows_of(qkv_ref, 2)
    grad_heads = product(output_rows(w_ref), low_ref[...], NT).astype(BF)
    heads_out = o_ref[0]
    parts = [[], [], []]
    for head in range(q_t.shape[0] // HD):
        rows = slice(HD * head, HD * (head + 1))
        queries_t, keys_t, grad_t = q_t[rows], k_t[rows], grad_heads[rows]
        scores = masks.scores(product(keys_t.T, queries_t, NN), head % 3)
        chances = jnp.exp(scores - lse_ref[0, head : head + 1])
        grad_chances = product(v_t[rows].T, grad_t, NN)
        inner = jnp.sum(grad_t.astype(F32) * heads_out[rows].astype(F32), axis=0, keepdims=True)
        grad_logits = (chances * (grad_chances - inner)).astype(BF)
        parts[2].append(product(chances.astype(BF), grad_t.T, NN).T)
        parts[1].append(product(grad_logits, queries_t.T, NN).T)
        parts[0].append(product(keys_t, grad_logits, NN) * HD**-0.5)
    for kind in range(3):
        joined = jnp.concatenate(parts[kind], axis=0).astype(BF)
        for j in range(BLOCKS):
            base = 3 * QKV * j + QKV * kind
            d_ref[base : base + QKV, :] = joined[QKV * j : QKV * (j + 1)]
    grads_low = d_ref[...]
    db_ref[0] = product(jnp.ones((8, seq), BF), grads_low, NT)
    acc_ref[...] = acc_ref[...] + product(grads_low, projection_rows(w_ref), TN)
    c, my = scalars[1], scalars[2]
    for half, out_ref in enumerate((mine_ref, other_ref)):
        start = pl.multiple_of(jnp.where(c == half, 0, HALF), 128)
        grad_w = product(grads_low, x_ref[:, pl.ds(start, HALF)], NN).astype(BF)
        grad_wo = product(heads_out, low_ref[:, pl.ds(start, HALF)], NN).astype(BF)
        for j in range(BLOCKS):
            out_ref[j ^ my, 0, : 3 * QKV] = grad_w[3 * QKV * j : 3 * QKV * (j + 1)]
            out_ref[j ^ my, 0, 3 * QKV :] = grad_wo[QKV * j : QKV * (j + 1)]

    @pl.when(r == last)
    def _():
        dx_ref[...] = acc_ref[...].astype(dx_ref.dtype)


def attention_backward(scalars, x, weights, qkv, heads_out, lse, upstream, start, ids, first, count, dtype):
    wide, seq = qkv.shape[1], x.shape[0]
    piece = pl.BlockSpec((BLOCKS, 1, 4 * QKV, HALF), lambda r, *_: (0, r, 0, 0))
    return pl.pallas_call(
        attention_backward_kernel,
        grid_spec=pltpu.PrefetchScalarGridSpec(
            num_scalar_prefetch=1,
            grid=(count,),
            in_specs=[
                whole((seq, D)),
                each((weights.shape[1], D), first),
                each((wide, seq), first),
                each((wide // 3, seq), first),
                each((8, seq), first),
                whole((seq, D)),
                whole((seq, D)),
                whole((1, seq)),
                whole((1, seq)),
                whole((seq, 1)),
                whole((seq, 1)),
            ],
            out_specs=[whole((seq, D)), piece, piece, each((8, wide))],
            scratch_shapes=[pltpu.VMEM((seq, D), F32), pltpu.VMEM((wide, seq), BF), pltpu.VMEM((seq, D), BF)],
        ),
        out_shape=[
            shape_of((seq, D), dtype),
            shape_of((BLOCKS, count, 4 * QKV, HALF), BF),
            shape_of((BLOCKS, count, 4 * QKV, HALF), BF),
            shape_of((count, 8, wide), F32),
        ],
        compiler_params=params(),
        cost_estimate=cost(count * 6.5e9, count * 5e6),
    )(scalars, x, weights, qkv, heads_out, lse, upstream, start, *ids)


def gelu_pair(x):
    bell = jnp.exp(x * x * -0.5)
    t = 1.0 / (1.0 + (0.3275911 * 0.70710678118654752) * jnp.abs(x))
    series = 0.5 * 1.061405429
    for factor in (-1.453152027, 1.421413741, -0.284496736, 0.254829592):
        series = series * t + 0.5 * factor
    tail = series * t * bell
    below = jnp.where(x < 0, tail, 1.0 - tail)
    return x * below, below + x * (bell * 0.3989422804014327)


def normalize(residual):
    centre = residual - jnp.mean(residual, axis=-1, keepdims=True)
    inv_spread = lax.rsqrt(jnp.mean(centre * centre, axis=-1, keepdims=True) + epsilon)
    return centre * inv_spread, inv_spread


def norm_back(upstream, normed, inv_spread, gain):
    scaled = upstream * gain
    return inv_spread * (
        scaled
        - jnp.mean(scaled, axis=-1, keepdims=True)
        - normed * jnp.mean(scaled * normed, axis=-1, keepdims=True)
    )


def add_sums(sums, *terms):
    return [total + jnp.sum(term, axis=0, keepdims=True) for total, term in zip(sums, terms)]


def store_sums(ref, sums):
    ref[...] = jnp.concatenate(sums + [jnp.zeros((8 - len(sums), D), F32)], axis=0)


def inner_kernel(
    o_ref, wo_ref, x_ref, vec_ref, wi_ref, bi_ref, normed_ref, inv_ref, hidden_ref, low_ref, act_ref, slope_ref
):
    seq = x_ref.shape[0]

    @pl.when(pl.program_id(0) == 0)
    def _():
        for start in range(0, seq, CHUNK):
            rows = slice(start, start + CHUNK)
            residual = vec_ref[0:1] + x_ref[rows].astype(F32)
            for shard in range(o_ref.shape[0]):
                residual = residual + product(o_ref[shard, :, rows], output_rows(wo_ref, shard), TN)
            normed, inv_spread = normalize(residual)
            hidden = normed * vec_ref[1:2] + vec_ref[2:3]
            normed_ref[rows], inv_ref[rows], hidden_ref[rows] = normed, inv_spread, hidden
            low_ref[rows] = hidden.astype(BF)

    for start in range(0, seq, CHUNK):
        rows = slice(start, start + CHUNK)
        act, slope = gelu_pair(product(low_ref[rows], wi_ref[0], NT) + bi_ref[0])
        act_ref[0, rows] = act.astype(BF)
        slope_ref[0, rows] = slope.astype(BF)


def inner_half(heads_out, w_out, x, vectors, w_inner, b_inner):
    shards, wide, seq = w_inner.shape[0], w_inner.shape[1], x.shape[0]
    return pl.pallas_call(
        inner_kernel,
        grid=(shards,),
        in_specs=[
            whole(heads_out.shape),
            whole(w_out.shape),
            whole((seq, D)),
            whole(vectors.shape),
            each((wide, D)),
            each((1, wide)),
        ],
        out_specs=[
            whole((seq, D)),
            whole((seq, 1)),
            whole((seq, D)),
            whole((seq, D)),
            each((seq, wide)),
            each((seq, wide)),
        ],
        out_shape=[
            shape_of((seq, D), F32),
            shape_of((seq, 1), F32),
            shape_of((seq, D), F32),
            shape_of((seq, D), BF),
            shape_of((shards, seq, wide), BF),
            shape_of((shards, seq, wide), BF),
        ],
        compiler_params=params(),
        cost_estimate=cost(14e9, 20e6),
    )(heads_out, w_out, x, vectors, w_inner, b_inner)


def outer_kernel(act_ref, wu_ref, hidden_ref, cot_ref, vec_ref, out_ref, grad_ref, sums_ref, acc_ref):
    r, last, seq = pl.program_id(0), pl.num_programs(0) - 1, hidden_ref.shape[0]

    @pl.when(r == 0)
    def _():
        acc_ref[...] = hidden_ref[...] + vec_ref[0:1]

    acc_ref[...] = acc_ref[...] + product(act_ref[0], wu_ref[0], NN)

    @pl.when(r == last)
    def _():
        sums = [jnp.zeros((1, D), F32)] * 3
        gain = vec_ref[1:2]
        for start in range(0, seq, CHUNK):
            rows = slice(start, start + CHUNK)
            normed, inv_spread = normalize(acc_ref[rows])
            out_ref[rows] = (normed * gain + vec_ref[2:3]).astype(BF)
            upstream = cot_ref[rows].astype(F32)
            grad = norm_back(upstream, normed, inv_spread, gain)
            grad_ref[rows] = grad
            sums = add_sums(sums, upstream * normed, upstream, grad)
        store_sums(sums_ref, sums)


def outer_half(act, w_outer, hidden, cotangent, vectors):
    shards, seq, wide = act.shape
    return pl.pallas_call(
        outer_kernel,
        grid=(shards,),
        in_specs=[each((seq, wide)), each((wide, D)), whole((seq, D)), whole((seq, D)), whole(vectors.shape)],
        out_specs=[whole((seq, D)), whole((seq, D)), whole((8, D))],
        out_shape=[shape_of((seq, D), BF), shape_of((seq, D), F32), shape_of((8, D), F32)],
        scratch_shapes=[pltpu.VMEM((seq, D), F32)],
        compiler_params=params(),
        cost_estimate=cost(8e9, 14e6),
    )(act, w_outer, hidden, cotangent, vectors)


def ffn_back_kernel(
    scalars, up_ref, start_ref, act_ref, slope_ref, wu_ref, wi_ref, low_ref, *refs, final
):
    r, last = pl.program_id(0), pl.num_programs(0) - 1
    if final:
        normed_ref, inv_ref, vec_ref, *refs = refs
        *refs, sums_ref, acc_ref, up_low_ref, inner_ref = refs
    else:
        *refs, acc_ref, up_low_ref, inner_ref = refs
    grad_ref, mine_ref, other_ref, db_ref = refs
    seq, wide = up_ref.shape[0], wi_ref.shape[1]
    block = wide // BLOCKS

    @pl.when(r == 0)
    def _():
        acc_ref[...] = start_ref[...]
        up_low_ref[...] = up_ref[...].astype(BF)

    db = jnp.zeros((1, wide), F32)
    for start in range(0, seq, CHUNK):
        rows = slice(start, start + CHUNK)
        grad_inner = product(up_low_ref[rows], wu_ref[0], NT) * slope_ref[0, rows].astype(F32)
        db = db + jnp.sum(grad_inner, axis=0, keepdims=True)
        inner_ref[rows] = grad_inner.astype(BF)
    db_ref[0] = db
    acc_ref[...] = acc_ref[...] + product(inner_ref[...], wi_ref[0], NN)
    c, my = scalars[1], scalars[2]
    for half, out_ref in enumerate((mine_ref, other_ref)):
        start = pl.multiple_of(jnp.where(c == half, 0, HALF), 128)
        columns = pl.ds(start, HALF)
        grad_wi = product(inner_ref[...], low_ref[:, columns], TN).astype(BF)
        grad_wu = product(act_ref[0], up_low_ref[:, columns], TN).astype(BF)
        for j in range(BLOCKS):
            out_ref[j ^ my, 0, :block] = grad_wi[block * j : block * (j + 1)]
            out_ref[j ^ my, 0, block:] = grad_wu[block * j : block * (j + 1)]

    @pl.when(r == last)
    def _():
        if not final:
            grad_ref[...] = acc_ref[...]
            return
        sums = [jnp.zeros((1, D), F32)] * 3
        for start in range(0, seq, CHUNK):
            rows = slice(start, start + CHUNK)
            upstream, normed = acc_ref[rows], normed_ref[rows]
            grad = norm_back(upstream, normed, inv_ref[rows], vec_ref[1:2])
            grad_ref[rows] = grad
            sums = add_sums(sums, upstream * normed, upstream, grad)
        store_sums(sums_ref, sums)


def ffn_back(scalars, upstream, start, act, slope, w_outer, w_inner, low, norm, first, count):
    _, seq, wide = act.shape
    rows = 2 * wide // BLOCKS
    piece = pl.BlockSpec((BLOCKS, 1, rows, HALF), lambda r, *_: (0, r, 0, 0))
    pieces = shape_of((BLOCKS, count, rows, HALF), BF)
    final = bool(norm)
    return pl.pallas_call(
        functools.partial(ffn_back_kernel, final=final),
        grid_spec=pltpu.PrefetchScalarGridSpec(
            num_scalar_prefetch=1,
            grid=(count,),
            in_specs=[
                whole((seq, D)),
                whole((seq, D)),
                each((seq, wide), first),
                each((seq, wide), first),
                each((wide, D), first),
                each((wide, D), first),
                whole((seq, D)),
            ]
            + [whole(array.shape) for array in norm],
            out_specs=[whole((seq, D)), piece, piece, each((1, wide))] + [whole((8, D))] * final,
            scratch_shapes=[pltpu.VMEM((seq, D), F32), pltpu.VMEM((seq, D), BF), pltpu.VMEM((seq, wide), BF)],
        ),
        out_shape=[shape_of((seq, D), F32), pieces, pieces, shape_of((count, 1, wide), F32)]
        + [shape_of((8, D), F32)] * final,
        compiler_params=params(),
        cost_estimate=cost(count * 6.5e9, count * 7e6),
    )(scalars, upstream, start, act, slope, w_outer, w_inner, low, *norm)


def run_copies(copies, sems):
    started = [pltpu.make_async_copy(source, target, sems.at[i]) for i, (source, target) in enumerate(copies)]
    for copy in started:
        copy.start()
    for copy in started:
        copy.wait()


def assemble(scalars, near, far, own):
    count, rows = near.shape[1:3]

    def kernel(scalars, near_ref, far_ref, own_ref, out_ref, sems):
        c, my = scalars[1], scalars[2]
        copies = [(own_ref, out_ref.at[0])]
        for m in range(BLOCKS):
            for source, side in ((near_ref, c), (far_ref, 1 - c)):
                target = out_ref.at[
                    pl.ds(1, count),
                    pl.ds(pl.multiple_of((m ^ my) * rows, 16), rows),
                    pl.ds(pl.multiple_of(side * HALF, 128), HALF),
                ]
                copies.append((source.at[m], target))
        run_copies(copies, sems)

    shape = (1 + count, BLOCKS * rows, D)
    return pl.pallas_call(
        kernel,
        grid_spec=pltpu.PrefetchScalarGridSpec(
            num_scalar_prefetch=1,
            grid=(1,),
            in_specs=[pl.BlockSpec(memory_space=pl.ANY)] * 3,
            out_specs=whole(shape),
            scratch_shapes=[pltpu.SemaphoreType.DMA((2 * BLOCKS + 1,))],
        ),
        out_shape=shape_of(shape, near.dtype),
        compiler_params=params(),
        cost_estimate=cost(0, 4 * near.size * 2 * 2),
    )(scalars, near, far, own)


def place_rows(scalars, own, left, right):
    count, seq = len(left) + 1, own.shape[0]

    def kernel(scalars, own_ref, *refs):
        left_refs, right_refs, out_ref, sems = refs[: count - 1], refs[count - 1 : -2], refs[-2], refs[-1]
        z = scalars[3]

        def copy(source, place, index):
            target = out_ref.at[pl.ds(pl.multiple_of(place * seq, 128), seq)]
            return pltpu.make_async_copy(source, target, sems.at[index])

        def every(action):
            action(copy(own_ref, z, 0))
            for k in range(1, count):
                pl.when(z >= k)(lambda k=k: action(copy(left_refs[k - 1], z - k, k)))
                pl.when(z + k < count)(lambda k=k: action(copy(right_refs[k - 1], z + k, count - 1 + k)))

        every(lambda step: step.start())
        every(lambda step: step.wait())

    return pl.pallas_call(
        kernel,
        grid_spec=pltpu.PrefetchScalarGridSpec(
            num_scalar_prefetch=1,
            grid=(1,),
            in_specs=[pl.BlockSpec(memory_space=pl.ANY)] * (2 * count - 1),
            out_specs=whole((count * seq, D)),
            scratch_shapes=[pltpu.SemaphoreType.DMA((2 * count,))],
        ),
        out_shape=shape_of((count * seq, D), own.dtype),
        compiler_params=params(),
        cost_estimate=cost(0, 4 * count * own.size),
    )(scalars, own, *left, *right)


def finish_kernel(scalars, near_ref, far_ref, *refs, kinds, flipped):
    *outs, held, sems = refs
    c, my = scalars[1], scalars[2]
    rows = near_ref.shape[1]
    copies = []
    for m in range(BLOCKS):
        for source, side in ((near_ref, c), (far_ref, 1 - c)):
            copies.append((source.at[m], held.at[m ^ my, :, pl.ds(pl.multiple_of(side * HALF, 128), HALF)]))
    run_copies(copies, sems)
    each_rows = rows // kinds
    for kind, out in enumerate(outs):
        for j in range(BLOCKS):
            part = held[j, each_rows * kind : each_rows * (kind + 1)].astype(F32)
            if not flipped[kind]:
                out[each_rows * j : each_rows * (j + 1)] = part
            elif each_rows % 128 == 0:
                out[:, each_rows * j : each_rows * (j + 1)] = part.T
        if flipped[kind] and each_rows % 128:
            whole_kind = jnp.concatenate(
                [held[j, each_rows * kind : each_rows * (kind + 1)] for j in range(BLOCKS)], axis=0
            )
            out[...] = whole_kind.astype(F32).T


def finish(scalars, near, far, flipped):
    rows, kinds = near.shape[1], len(flipped)
    wide = BLOCKS * rows // kinds
    shapes = [(D, wide) if flip else (wide, D) for flip in flipped]
    return pl.pallas_call(
        functools.partial(finish_kernel, kinds=kinds, flipped=flipped),
        grid_spec=pltpu.PrefetchScalarGridSpec(
            num_scalar_prefetch=1,
            grid=(1,),
            in_specs=[pl.BlockSpec(memory_space=pl.ANY)] * 2,
            out_specs=[whole(shape) for shape in shapes],
            scratch_shapes=[pltpu.VMEM((BLOCKS, rows, D), BF), pltpu.SemaphoreType.DMA((2 * BLOCKS,))],
        ),
        out_shape=[shape_of(shape, F32) for shape in shapes],
        compiler_params=params(),
        cost_estimate=cost(0, 8 * near.size),
    )(scalars, near, far)


def tie(array, *before):
    return lax.optimization_barrier((array,) + before)[0]


def build(n_dp, n_tensor):
    flip = {bit: [(i, i ^ bit) for i in range(n_dp)] for bit in (1, 2, 4)}
    f32 = lambda array: array.astype(F32)

    def across(array, bit):
        return lax.ppermute(array, "dp", flip[bit])

    def along(array, r):
        return lax.ppermute(array, "tensor", [(i, i ^ r) for i in range(n_tensor)])

    def plane_gather(mine, first, then):
        from_first, from_then = across(mine, first), across(mine, then)
        diagonal = across(from_first, then)
        from_x, from_y = (from_first, from_then) if first == 2 else (from_then, from_first)
        near = jnp.stack([mine, from_x, from_y, diagonal])
        return near, across(near, 1)

    def plane_reduce(mine, other):
        summed = (f32(mine) + f32(across(other, 1))).astype(BF)
        via_y, via_x = across(summed[3, :1], 4), across(summed[3, 1:], 2)
        for_x = jnp.concatenate([(f32(summed[1, :1]) + f32(via_y)).astype(BF), summed[1, 1:]])
        for_y = jnp.concatenate([summed[2, :1], (f32(summed[2, 1:]) + f32(via_x)).astype(BF)])
        return f32(summed[0]) + f32(across(for_x, 2)) + f32(across(for_y, 4))

    def line_reduce(far):
        ends = lax.ppermute(far.astype(BF), "tensor", [(0, 1), (3, 2)])
        middle = lax.ppermute((far + f32(ends[::-1])).astype(BF), "tensor", [(1, 2), (2, 1)])
        return f32(middle[::-1])

    def reduce(near_pieces, far_pieces):
        far = line_reduce(plane_reduce(*far_pieces))
        near = plane_reduce(*near_pieces) + far
        total = near[0] + f32(along(near[1].astype(BF), 1))
        step = 8
        while step < n_dp:
            total = total + lax.ppermute(total, "dp", [(i, i ^ step) for i in range(n_dp)])
            step *= 2
        return total.astype(BF)

    def rows_gather(own):
        left, right, going_up, going_down = [], [], own, own
        for k in range(1, n_tensor):
            going_up = lax.ppermute(going_up, "tensor", [(i, i + 1) for i in range(k - 1, n_tensor - 1)])
            going_down = lax.ppermute(going_down, "tensor", [(i + 1, i) for i in range(n_tensor - k)])
            left.append(going_up)
            right.append(going_down)
        return left, right

    def sum_everywhere(by_shard, shared):
        count = by_shard.shape[0]
        both = jnp.concatenate([by_shard, shared])
        step = 1
        while step < n_dp:
            both = both + lax.ppermute(both, "dp", [(i, i ^ step) for i in range(n_dp)])
            step *= 2
        step = 1
        while step < n_tensor:
            other = along(both, step)
            order = [r ^ step for r in range(count)]
            both = both + jnp.concatenate([other[r : r + 1] for r in order] + [other[count:]])
            step *= 2
        return both[0], both[count:]

    def body(
        tokens, w_query, b_query, w_key, w_value, b_value, w_attn_out, b_attn_out, gain_one, shift_one,
        w_inner, b_inner, w_outer, b_outer, gain_two, shift_two, cotangent, lengths, row_ids, col_ids,
    ):
        seq = row_ids.shape[1]
        wide = w_inner.shape[1]
        block = wide // BLOCKS
        heads = BLOCKS * QKV
        index = lax.axis_index("dp")
        z = lax.axis_index("tensor")
        c, my = index & 1, (index >> 1) & 3
        scalars = jnp.stack([lax.dynamic_index_in_dim(lengths, z, keepdims=False), c, my, z]).astype(jnp.int32)

        def cut(array, rows):
            return lax.dynamic_slice(array, (my * rows, c * HALF), (rows, HALF))

        def cut_t(array, rows):
            return lax.dynamic_slice(array, (c * HALF, my * rows), (HALF, rows)).T

        bias = jnp.concatenate([b_query, b_value, b_inner]).reshape(-1, HALF)
        bias_rows = bias.shape[0]
        piece_a = jnp.concatenate(
            [cut_t(w, QKV) for w in (w_query, w_key, w_value)]
            + [cut(w_attn_out, QKV), bias, jnp.zeros((16 - bias_rows, HALF), BF)]
        )
        shards_a = [along(piece_a, r) for r in range(1, n_tensor)]
        piece_i = tie(cut_t(w_inner, block), *shards_a)
        shards_i = [along(piece_i, r) for r in range(1, n_tensor)]
        piece_u = tie(cut(w_outer, block), *shards_i)
        shards_u = [along(piece_u, r) for r in range(1, n_tensor)]

        slab = jnp.stack(
            [w.T.reshape(BLOCKS, QKV, D) for w in (w_query, w_key, w_value)]
            + [w_attn_out.reshape(BLOCKS, QKV, D)],
            axis=1,
        ).reshape(4 * heads, D)
        near_a, far_a = plane_gather(jnp.stack([s[: 4 * QKV] for s in shards_a]), 2, 4)
        near_i, far_i = plane_gather(jnp.stack(shards_i), 4, 2)
        near_u, far_u = plane_gather(jnp.stack(shards_u), 2, 4)

        biases = f32(jnp.stack([bias] + [s[4 * QKV : 4 * QKV + bias_rows] for s in shards_a]))
        biases = biases.reshape(n_tensor, -1)
        of_kind = lambda kind: biases[:, kind * heads : (kind + 1) * heads].reshape(n_tensor, BLOCKS, QKV)
        bias_qkv = jnp.stack([of_kind(0), jnp.zeros((n_tensor, BLOCKS, QKV), F32), of_kind(1)], axis=2)
        bias_qkv = bias_qkv.reshape(n_tensor, 1, 3 * heads)
        bias_inner = biases[:, None, 2 * heads :]

        own_rows = lambda array: lax.dynamic_slice(array, (z * seq, 0), (seq, D))
        x, upstream = own_rows(tokens), own_rows(cotangent)
        row_tags = lax.dynamic_index_in_dim(row_ids, z, keepdims=False)
        col_tags = lax.dynamic_index_in_dim(col_ids, z, keepdims=False)
        ids = (row_tags[None, :], col_tags[None, :], row_tags[:, None], col_tags[:, None])

        first = attention_forward(scalars, x, slab[None], bias_qkv, ids, n_tensor, 0)
        w_attn = assemble(scalars, near_a, far_a, slab)
        qkv, heads_out, lse = attention_forward(scalars, x, w_attn, bias_qkv, ids, n_tensor, 1, first)

        w_in = assemble(scalars, near_i, far_i, w_inner.T)
        vectors_one = f32(jnp.stack([b_attn_out, gain_one, shift_one]))
        vectors_two = f32(jnp.stack([b_outer, gain_two, shift_two]))
        normed, inv_spread, hidden, low, act, slope = inner_half(
            heads_out, w_attn, x, vectors_one, w_in, bias_inner
        )
        w_up = assemble(scalars, near_u, far_u, w_outer)
        out_rows, grad_two, sums_two = outer_half(act, w_up, hidden, upstream, vectors_two)
        out_left, out_right = rows_gather(out_rows)

        half = n_tensor // 2
        shared = (scalars, grad_two)
        rest = (act, slope, w_up, w_in, low)
        partial, far_mine, far_other, db_far = ffn_back(*shared, grad_two, *rest, (), half, half)
        grad_one, near_mine, near_other, db_near, sums_one = ffn_back(
            *shared, partial, *rest, (normed, inv_spread, vectors_one), 0, half
        )
        done_f = reduce((near_mine, near_other), (far_mine, far_other))
        db_inner = jnp.concatenate([db_near, db_far])

        rest = (qkv, heads_out, lse, grad_one)
        partial, far_mine, far_other, db_far = attention_backward(
            scalars, x, w_attn, *rest, grad_one, ids, half, half, F32
        )
        grad_rows, near_mine, near_other, db_near = attention_backward(
            scalars, x, w_attn, *rest, partial, ids, 0, half, BF
        )
        grad_left, grad_right = rows_gather(grad_rows)
        done_a = reduce((near_mine, near_other), (far_mine, far_other))
        db_qkv = jnp.concatenate([db_near, db_far])[:, 0].reshape(n_tensor, BLOCKS, 3, QKV)

        layer_out = place_rows(scalars, out_rows, out_left, out_right)
        grad_tokens = place_rows(scalars, grad_rows, grad_left, grad_right)
        near_g, far_g = plane_gather(jnp.concatenate([done_a, done_f])[None], 2, 4)
        split = 4 * QKV
        grad_wq, grad_wk, grad_wv, grad_wo = finish(
            scalars, near_g[:, 0, :split], far_g[:, 0, :split], (True, True, True, False)
        )
        grad_wi, grad_wu = finish(scalars, near_g[:, 0, split:], far_g[:, 0, split:], (True, False))

        by_shard = jnp.concatenate(
            [db_qkv[:, :, i].reshape(n_tensor, -1) for i in (0, 2)] + [db_inner[:, 0]], axis=1
        )
        summed = jnp.concatenate([sums_one[:3], sums_two[:3]]).reshape(-1, by_shard.shape[1])
        mine, summed = sum_everywhere(by_shard, summed)
        summed = summed.reshape(6, D)

        return (
            layer_out,
            grad_tokens,
            grad_wq,
            mine[:heads],
            grad_wk,
            grad_wv,
            mine[heads : 2 * heads],
            grad_wo,
            summed[2],
            summed[0],
            summed[1],
            grad_wi,
            mine[2 * heads :],
            grad_wu,
            summed[5],
            summed[3],
            summed[4],
        )

    return body


def solution(mesh):
    rows, columns, out = P("dp", None), P(None, "tensor"), P("tensor", None)
    one = P("tensor")
    in_specs = (
        rows, columns, one, columns, columns, one, out, P(), P(), P(), columns, one, out, P(), P(), P(),
        rows, P("dp"), rows, rows,
    )
    out_specs = (
        rows, rows, columns, one, columns, columns, one, out, P(), P(), P(), columns, one, out, P(), P(), P(),
    )
    body = build(mesh.shape["dp"], mesh.shape["tensor"])
    return jax.shard_map(body, mesh=mesh, in_specs=in_specs, out_specs=out_specs, check_vma=False)
```

```python
import functools

import jax
import jax.numpy as jnp
from jax import lax
from jax.experimental import pallas as pl
from jax.experimental.pallas import tpu as pltpu
from jax.sharding import PartitionSpec as P

F32 = jnp.float32
BF = jnp.bfloat16
HD = 64
D = 768
HALF = D // 2
BLOCKS = 4
QKV = 48
epsilon = 1e-12
masked_value = -1e30
CHUNK = 128
SCALE = 0.05
VECTORS = 16

NN = (((1,), (0,)), ((), ()))
NT = (((1,), (1,)), ((), ()))
TN = (((0,), (0,)), ((), ()))


def product(left, right, dims):
    return lax.dot_general(left, right, dims, preferred_element_type=F32)


def shape_of(shape, dtype):
    return jax.ShapeDtypeStruct(shape, dtype)


def whole(shape):
    return pl.BlockSpec(shape, lambda r, *_: (0,) * len(shape))


def each(shape, shift=0):
    return pl.BlockSpec((1,) + shape, lambda r, *_: (r + shift,) + (0,) * len(shape))


def params():
    return pltpu.CompilerParams(vmem_limit_bytes=24 * 1024 * 1024)


def cost(flops, moved, exps=0):
    return pl.CostEstimate(flops=int(flops * SCALE), bytes_accessed=int(moved * SCALE), transcendentals=int(exps))


def rows_of(ref, kind):
    width = 3 * QKV
    return jnp.concatenate(
        [ref[0, width * j + QKV * kind : width * j + QKV * (kind + 1)] for j in range(BLOCKS)], axis=0
    )


class Masks:
    def __init__(self, scalars, row_ref, col_ref):
        length, table = scalars[0], scalars[3]
        row_q = row_ref[pl.ds(table, 1), :].astype(F32)
        col_q = col_ref[pl.ds(table, 1), :].astype(F32)
        row_k, col_k = as_column(row_q), as_column(col_q)
        position = lax.broadcasted_iota(jnp.int32, row_k.shape, 0)
        self.here = position < length
        self.leading = position == 0
        self.row_k = jnp.where(self.here, row_k, -1.0)
        self.col_k = jnp.where(self.here, col_k, -1.0)
        self.row_q, self.col_q = row_q, col_q

    def scores(self, logits, kind):
        if kind == 0:
            visible = self.here
        elif kind == 1:
            visible = (self.row_k == self.row_q) | self.leading
        else:
            visible = (self.col_k == self.col_q) | self.leading
        return jnp.where(visible, logits, masked_value)


def as_column(row):
    return jnp.broadcast_to(row, (8, row.shape[1])).T[:, 0:1]


def projection_rows(w_ref):
    return jnp.concatenate([w_ref[0, 4 * QKV * j : 4 * QKV * j + 3 * QKV] for j in range(BLOCKS)], axis=0)


def output_rows(w_ref, shard=0):
    return jnp.concatenate(
        [w_ref[shard, 4 * QKV * j + 3 * QKV : 4 * QKV * (j + 1)] for j in range(BLOCKS)], axis=0
    )


def attention_forward_kernel(scalars, x_ref, w_ref, b_ref, row_ref, col_ref, *rest):
    qkv_ref, o_ref, lse_ref = rest[-3:]
    seq = x_ref.shape[0]
    bias = b_ref[0].astype(F32)
    bias = jnp.concatenate([bias[0:1], bias[1:2, : 3 * BLOCKS * QKV - HALF]], axis=1)
    qkv = product(projection_rows(w_ref), x_ref[...], NT) + as_column(bias)
    low = qkv.astype(BF)
    is_query = lax.broadcasted_iota(jnp.int32, (qkv.shape[0], 1), 0) % (3 * QKV) < QKV
    low = jnp.where(is_query, low * jnp.asarray(HD**-0.5, BF), low)
    qkv_ref[0] = low
    masks = Masks(scalars, row_ref, col_ref)
    q_t, k_t, v_t = rows_of(qkv_ref, 0), rows_of(qkv_ref, 1), rows_of(qkv_ref, 2)
    outs, logs = [], []
    for head in range(q_t.shape[0] // HD):
        rows = slice(HD * head, HD * (head + 1))
        scores = masks.scores(product(k_t[rows].T, q_t[rows], NN), head % 3)
        highest = jnp.max(scores, axis=0, keepdims=True)
        weights = jnp.exp(scores - highest).astype(BF)
        with_ones = jnp.concatenate([v_t[rows], jnp.ones((16, seq), BF)], axis=0)
        blended = product(with_ones, weights, NN)
        total = blended[HD : HD + 1]
        outs.append(blended[:HD] * (1.0 / total))
        logs.append(highest + jnp.log(total))
    o_ref[0] = jnp.concatenate(outs, axis=0).astype(BF)
    logs.append(jnp.zeros((8 - len(logs), seq), F32))
    lse_ref[0] = jnp.concatenate(logs, axis=0)


def in_hbm():
    return pl.BlockSpec(memory_space=pltpu.HBM)


def table_rows(seq):
    return pl.BlockSpec((seq, D), lambda r, scalars: (scalars[3], 0))


def bias_rows(shift=0):
    return pl.BlockSpec((1, VECTORS, HALF), lambda r, *_: (r + shift, 4 * QKV // VECTORS, 0))


def attention_forward(scalars, tokens, weights, pieces, tags, shards, first, carried=None):
    wide, seq = 3 * BLOCKS * QKV, tags[0].shape[1]
    count, at = pieces.shape[0], first if carried else 0
    out_shape = [
        shape_of((shards, wide, seq), BF),
        shape_of((shards, wide // 3, seq), BF),
        shape_of((shards, 8, seq), F32),
    ]
    kept = list(carried) if carried else []
    return pl.pallas_call(
        attention_forward_kernel,
        grid_spec=pltpu.PrefetchScalarGridSpec(
            num_scalar_prefetch=1,
            grid=(count,),
            in_specs=[
                table_rows(seq),
                each((weights.shape[1], D), at),
                bias_rows(),
                whole(tags[0].shape),
                whole(tags[1].shape),
            ]
            + [pl.BlockSpec(memory_space=pl.ANY)] * len(kept),
            out_specs=[each(s.shape[1:], first) for s in out_shape],
        ),
        out_shape=out_shape,
        input_output_aliases={6 + i: i for i in range(len(kept))},
        compiler_params=params(),
        cost_estimate=cost(count * 3e9, count * 3e6),
    )(scalars, tokens, weights, pieces, *tags, *kept)


def attention_backward_kernel(
    scalars, x_hbm, w_hbm, qkv_hbm, o_hbm, lse_hbm, up_hbm, start_hbm, row_ref, col_ref, dbi_ref, one_ref, two_ref,
    *refs, shard, carried,
):
    dx_ref, mine_ref, other_ref, d_ref, x_ref, w_ref, qkv_ref, o_ref, lse_ref, low_ref, start_ref, sems = refs[carried:]
    seq = x_ref.shape[0]
    at = pl.ds(shard, 1)
    copies = [
        (w_hbm.at[at], w_ref),
        (up_hbm, low_ref),
        (qkv_hbm.at[at], qkv_ref),
        (o_hbm.at[at], o_ref),
        (lse_hbm.at[at], lse_ref),
        (x_hbm.at[pl.ds(pl.multiple_of(scalars[3] * seq, 128), seq)], x_ref),
        (start_hbm, start_ref),
    ]
    started = [pltpu.make_async_copy(source, target, sems.at[i]) for i, (source, target) in enumerate(copies)]
    for copy in started:
        copy.start()
    for copy in started[:5]:
        copy.wait()
    masks = Masks(scalars, row_ref, col_ref)
    q_t, k_t, v_t = rows_of(qkv_ref, 0), rows_of(qkv_ref, 1), rows_of(qkv_ref, 2)
    grad_heads = product(output_rows(w_ref), low_ref[...], NT).astype(BF)
    heads_out = o_ref[0]
    parts = [[], [], []]
    for head in range(q_t.shape[0] // HD):
        rows = slice(HD * head, HD * (head + 1))
        queries_t, keys_t, grad_t = q_t[rows], k_t[rows], grad_heads[rows]
        scores = masks.scores(product(keys_t.T, queries_t, NN), head % 3)
        chances = jnp.exp(scores - lse_ref[0, head : head + 1])
        grad_chances = product(v_t[rows].T, grad_t, NN)
        inner = jnp.sum(grad_t.astype(F32) * heads_out[rows].astype(F32), axis=0, keepdims=True)
        grad_logits = (chances * (grad_chances - inner)).astype(BF)
        parts[2].append(product(chances.astype(BF), grad_t.T, NN).T)
        parts[1].append(product(grad_logits, queries_t.T, NN).T)
        parts[0].append(product(keys_t, grad_logits, NN) * HD**-0.5)
    for kind in range(3):
        joined = jnp.concatenate(parts[kind], axis=0).astype(BF)
        for j in range(BLOCKS):
            base = 3 * QKV * j + QKV * kind
            d_ref[base : base + QKV, :] = joined[QKV * j : QKV * (j + 1)]
    grads_low = d_ref[...]
    for copy in started[5:]:
        copy.wait()
    dx_ref[...] = (start_ref[...] + product(grads_low, projection_rows(w_ref), TN)).astype(dx_ref.dtype)
    db = product(jnp.ones((8, seq), BF), grads_low, NT)[:1]
    vectors = [dbi_ref[0, :, :HALF], dbi_ref[0, :, HALF:], db[:, :HALF]]
    vectors.append(jnp.concatenate([db[:, HALF:], jnp.zeros((1, 2 * HALF - db.shape[1]), F32)], axis=1))
    for sums_ref in (one_ref, two_ref):
        for i in range(3):
            vectors += [sums_ref[i : i + 1, :HALF], sums_ref[i : i + 1, HALF:]]
    vectors = jnp.concatenate(vectors, axis=0).astype(BF)
    c, my = scalars[1], scalars[2]
    for half, out_ref in enumerate((mine_ref, other_ref)):
        start = pl.multiple_of(jnp.where(c == half, 0, HALF), 128)
        grad_w = product(grads_low, x_ref[:, pl.ds(start, HALF)], NN).astype(BF)
        grad_wo = product(heads_out, low_ref[:, pl.ds(start, HALF)], NN).astype(BF)
        for j in range(BLOCKS):
            out_ref[j ^ my, 0, : 3 * QKV] = grad_w[3 * QKV * j : 3 * QKV * (j + 1)]
            out_ref[j ^ my, 0, 3 * QKV : 4 * QKV] = grad_wo[QKV * j : QKV * (j + 1)]
            here = jnp.where(c == half, 1.0, 0.0).astype(BF) if j == 0 else jnp.zeros((), BF)
            out_ref[j ^ my, 0, 4 * QKV :] = vectors * here


def attention_backward(
    scalars, tokens, weights, qkv, heads_out, lse, upstream, start, tags, vectors, shard, dtype, carried
):
    shards, wide, seq = qkv.shape
    rows = 4 * QKV + VECTORS
    pieces = shape_of((BLOCKS, shards, rows, HALF), BF)
    piece = pl.BlockSpec((BLOCKS, 1, rows, HALF), lambda r, *_: (0, shard, 0, 0))
    return pl.pallas_call(
        functools.partial(attention_backward_kernel, shard=shard, carried=len(carried)),
        grid_spec=pltpu.PrefetchScalarGridSpec(
            num_scalar_prefetch=1,
            grid=(1,),
            in_specs=[in_hbm()] * 7
            + [whole(tags[0].shape), whole(tags[1].shape), each(vectors[0].shape[1:], shard)]
            + [whole((8, D)), whole((8, D))]
            + [in_hbm()] * len(carried),
            out_specs=[whole((seq, D)), piece, piece],
            scratch_shapes=[
                pltpu.VMEM((wide, seq), BF),
                pltpu.VMEM((seq, D), BF),
                pltpu.VMEM((1,) + weights.shape[1:], BF),
                pltpu.VMEM((1, wide, seq), BF),
                pltpu.VMEM((1, wide // 3, seq), BF),
                pltpu.VMEM((1, 8, seq), F32),
                pltpu.VMEM((seq, D), BF),
                pltpu.VMEM((seq, D), F32),
                pltpu.SemaphoreType.DMA((7,)),
            ],
        ),
        out_shape=[shape_of((seq, D), dtype), pieces, pieces],
        input_output_aliases={13 + i: 1 + i for i in range(len(carried))},
        compiler_params=params(),
        cost_estimate=cost(5e9, 5e6),
    )(scalars, tokens, weights, qkv, heads_out, lse, upstream, start, *tags, *vectors, *carried)


def gelu_pair(x):
    bell = jnp.exp(x * x * -0.5)
    t = 1.0 / (1.0 + (0.3275911 * 0.70710678118654752) * jnp.abs(x))
    series = 0.5 * 1.061405429
    for factor in (-1.453152027, 1.421413741, -0.284496736, 0.254829592):
        series = series * t + 0.5 * factor
    tail = series * t * bell
    below = jnp.where(x < 0, tail, 1.0 - tail)
    return x * below, below + x * (bell * 0.3989422804014327)


def normalize(residual):
    centre = residual - jnp.mean(residual, axis=-1, keepdims=True)
    inv_spread = lax.rsqrt(jnp.mean(centre * centre, axis=-1, keepdims=True) + epsilon)
    return centre * inv_spread, inv_spread


def norm_back(upstream, normed, inv_spread, gain):
    scaled = upstream * gain
    return inv_spread * (
        scaled
        - jnp.mean(scaled, axis=-1, keepdims=True)
        - normed * jnp.mean(scaled * normed, axis=-1, keepdims=True)
    )


def add_sums(sums, *terms):
    return [total + jnp.sum(term, axis=0, keepdims=True) for total, term in zip(sums, terms)]


def store_sums(ref, sums):
    ref[...] = jnp.concatenate(sums + [jnp.zeros((8 - len(sums), D), F32)], axis=0)


def inner_kernel(
    scalars, o_ref, wo_ref, x_ref, vec_ref, wi_ref, own_ref, others_ref,
    normed_ref, inv_ref, hidden_ref, low_ref, act_ref, slope_ref,
):
    seq, r = x_ref.shape[0], pl.program_id(0)
    bias = jnp.where(r == 0, own_ref[0].astype(F32), others_ref[jnp.maximum(r - 1, 0)].astype(F32))
    bias = jnp.concatenate([bias[2:3], bias[3:4]], axis=1)

    @pl.when(r == 0)
    def _():
        for start in range(0, seq, CHUNK):
            rows = slice(start, start + CHUNK)
            residual = vec_ref[0:1] + x_ref[rows].astype(F32)
            for shard in range(o_ref.shape[0]):
                residual = residual + product(o_ref[shard, :, rows], output_rows(wo_ref, shard), TN)
            normed, inv_spread = normalize(residual)
            hidden = normed * vec_ref[1:2] + vec_ref[2:3]
            normed_ref[rows], inv_ref[rows], hidden_ref[rows] = normed, inv_spread, hidden
            low_ref[rows] = hidden.astype(BF)

    for start in range(0, seq, CHUNK):
        rows = slice(start, start + CHUNK)
        act, slope = gelu_pair(product(low_ref[rows], wi_ref[0], NT) + bias)
        act_ref[0, rows] = act.astype(BF)
        slope_ref[0, rows] = slope.astype(BF)


def inner_half(scalars, heads_out, w_out, tokens, vectors, w_inner, own_piece, pieces):
    shards, wide, seq = w_inner.shape[0], w_inner.shape[1], heads_out.shape[2]
    return pl.pallas_call(
        inner_kernel,
        grid_spec=pltpu.PrefetchScalarGridSpec(
            num_scalar_prefetch=1,
            grid=(shards,),
            in_specs=[
                whole(heads_out.shape),
                whole(w_out.shape),
                table_rows(seq),
                whole(vectors.shape),
                each((wide, D)),
                pl.BlockSpec((1, VECTORS, HALF), lambda r, *_: (0, 4 * QKV // VECTORS, 0)),
                pl.BlockSpec((shards - 1, VECTORS, HALF), lambda r, *_: (0, 4 * QKV // VECTORS, 0)),
            ],
            out_specs=[
                whole((seq, D)),
                whole((seq, 1)),
                whole((seq, D)),
                whole((seq, D)),
                each((seq, wide)),
                each((seq, wide)),
            ],
        ),
        out_shape=[
            shape_of((seq, D), F32),
            shape_of((seq, 1), F32),
            shape_of((seq, D), F32),
            shape_of((seq, D), BF),
            shape_of((shards, seq, wide), BF),
            shape_of((shards, seq, wide), BF),
        ],
        compiler_params=params(),
        cost_estimate=cost(12e9, 20e6),
    )(scalars, heads_out, w_out, tokens, vectors, w_inner, own_piece, pieces)


def outer_kernel(scalars, act_ref, wu_ref, hidden_ref, cot_ref, vec_ref, out_ref, grad_ref, sums_ref, acc_ref):
    r, last, seq = pl.program_id(0), pl.num_programs(0) - 1, hidden_ref.shape[0]

    @pl.when(r == 0)
    def _():
        acc_ref[...] = hidden_ref[...] + vec_ref[0:1]

    acc_ref[...] = acc_ref[...] + product(act_ref[0], wu_ref[0], NN)

    @pl.when(r == last)
    def _():
        sums = [jnp.zeros((1, D), F32)] * 3
        gain = vec_ref[1:2]
        for start in range(0, seq, CHUNK):
            rows = slice(start, start + CHUNK)
            normed, inv_spread = normalize(acc_ref[rows])
            out_ref[rows] = (normed * gain + vec_ref[2:3]).astype(BF)
            upstream = cot_ref[rows].astype(F32)
            grad = norm_back(upstream, normed, inv_spread, gain)
            grad_ref[rows] = grad
            sums = add_sums(sums, upstream * normed, upstream, grad)
        store_sums(sums_ref, sums)


def outer_half(scalars, act, w_outer, hidden, cotangent, vectors):
    shards, seq, wide = act.shape
    return pl.pallas_call(
        outer_kernel,
        grid_spec=pltpu.PrefetchScalarGridSpec(
            num_scalar_prefetch=1,
            grid=(shards,),
            in_specs=[
                each((seq, wide)),
                each((wide, D)),
                whole((seq, D)),
                table_rows(seq),
                whole(vectors.shape),
            ],
            out_specs=[whole((seq, D)), whole((seq, D)), whole((8, D))],
            scratch_shapes=[pltpu.VMEM((seq, D), F32)],
        ),
        out_shape=[shape_of((seq, D), BF), shape_of((seq, D), F32), shape_of((8, D), F32)],
        compiler_params=params(),
        cost_estimate=cost(5e9, 14e6),
    )(scalars, act, w_outer, hidden, cotangent, vectors)


def ffn_back_kernel(
    up_ref, slope_ref, wu_ref, wi_ref, normed_ref, inv_ref, vec_ref, grad_ref, grad_low_ref, inner_ref, db_ref, sums_ref,
    acc_ref, low_ref,
):
    r, last = pl.program_id(0), pl.num_programs(0) - 1
    seq, wide = up_ref.shape[0], wi_ref.shape[1]

    @pl.when(r == 0)
    def _():
        acc_ref[...] = up_ref[...]
        low_ref[...] = up_ref[...].astype(BF)

    db = jnp.zeros((1, wide), F32)
    for start in range(0, seq, CHUNK):
        rows = slice(start, start + CHUNK)
        grad_inner = product(low_ref[rows], wu_ref[0], NT) * slope_ref[0, rows].astype(F32)
        db = db + jnp.sum(grad_inner, axis=0, keepdims=True)
        inner_ref[0, rows] = grad_inner.astype(BF)
    db_ref[0] = db
    acc_ref[...] = acc_ref[...] + product(inner_ref[0], wi_ref[0], NN)

    @pl.when(r == last)
    def _():
        sums = [jnp.zeros((1, D), F32)] * 3
        for start in range(0, seq, CHUNK):
            rows = slice(start, start + CHUNK)
            upstream, normed = acc_ref[rows], normed_ref[rows]
            grad = norm_back(upstream, normed, inv_ref[rows], vec_ref[1:2])
            grad_ref[rows] = grad
            grad_low_ref[rows] = grad.astype(BF)
            sums = add_sums(sums, upstream * normed, upstream, grad)
        store_sums(sums_ref, sums)


def ffn_back(upstream, slope, w_outer, w_inner, normed, inv_spread, vectors):
    shards, seq, wide = slope.shape
    return pl.pallas_call(
        ffn_back_kernel,
        grid=(shards,),
        in_specs=[
            whole((seq, D)),
            each((seq, wide)),
            each((wide, D)),
            each((wide, D)),
            whole((seq, D)),
            whole((seq, 1)),
            whole(vectors.shape),
        ],
        out_specs=[whole((seq, D)), whole((seq, D)), each((seq, wide)), each((1, wide)), whole((8, D))],
        out_shape=[
            shape_of((seq, D), F32),
            shape_of((seq, D), BF),
            shape_of((shards, seq, wide), BF),
            shape_of((shards, 1, wide), F32),
            shape_of((8, D), F32),
        ],
        scratch_shapes=[pltpu.VMEM((seq, D), F32), pltpu.VMEM((seq, D), BF)],
        compiler_params=params(),
        cost_estimate=cost(shards * 3e9, shards * 4e6),
    )(upstream, slope, w_outer, w_inner, normed, inv_spread, vectors)


def weight_grad_kernel(scalars, left_ref, right_ref, mine_ref, other_ref, low_ref):
    @pl.when(pl.program_id(0) == 0)
    def _():
        low_ref[...] = right_ref[...].astype(BF)

    c, my = scalars[1], scalars[2]
    rows = mine_ref.shape[2]
    for half, out_ref in enumerate((mine_ref, other_ref)):
        start = pl.multiple_of(jnp.where(c == half, 0, HALF), 128)
        grad = product(left_ref[0], low_ref[:, pl.ds(start, HALF)], TN).astype(BF)
        for j in range(BLOCKS):
            out_ref[j ^ my, 0] = grad[rows * j : rows * (j + 1)]


def weight_grad(scalars, left, right):
    shards, seq, wide = left.shape
    piece = pl.BlockSpec((BLOCKS, 1, wide // BLOCKS, HALF), lambda r, *_: (0, r, 0, 0))
    pieces = shape_of((BLOCKS, shards, wide // BLOCKS, HALF), BF)
    return pl.pallas_call(
        weight_grad_kernel,
        grid_spec=pltpu.PrefetchScalarGridSpec(
            num_scalar_prefetch=1,
            grid=(shards,),
            in_specs=[each((seq, wide)), whole((seq, D))],
            out_specs=[piece, piece],
            scratch_shapes=[pltpu.VMEM((seq, D), BF)],
        ),
        out_shape=[pieces, pieces],
        compiler_params=params(),
        cost_estimate=cost(shards * 1.5e9, shards * 2e6),
    )(scalars, left, right)


def run_copies(copies, sems):
    started = [pltpu.make_async_copy(source, target, sems.at[i]) for i, (source, target) in enumerate(copies)]
    for copy in started:
        copy.start()
    for copy in started:
        copy.wait()


def any_place():
    return pl.BlockSpec(memory_space=pl.ANY)


def slab_places(first, columns):
    col = lax.broadcasted_iota(jnp.int32, (columns, BLOCKS * QKV), 0) + first
    feature = lax.broadcasted_iota(jnp.int32, (columns, BLOCKS * QKV), 1)
    block = sum((feature >= QKV * j).astype(jnp.int32) for j in range(1, BLOCKS))
    return lambda kind: (col == feature + block * 2 * QKV + QKV * kind).astype(BF)


def attention_piece(scalars, w_query, w_key, w_value, w_out, bias):
    heads = BLOCKS * QKV

    def kernel(scalars, *refs):
        *w_refs, bias_ref, slab_ref, piece_ref = refs
        for j in range(BLOCKS):
            for kind, w_ref in enumerate(w_refs):
                base = QKV * (4 * j + kind)
                slab_ref[0, base : base + QKV] = w_ref[QKV * j : QKV * (j + 1)]
        c, my = scalars[1], scalars[2]
        rows = pl.ds(pl.multiple_of(my * 4 * QKV, 16), 4 * QKV)
        piece_ref[0, : 4 * QKV] = slab_ref[0, rows, pl.ds(pl.multiple_of(c * HALF, 128), HALF)]
        every = jnp.broadcast_to(bias_ref[...], (16, bias_ref.shape[1]))
        of_query, of_value = every[:, :heads], every[:, heads : 2 * heads]
        low = []
        for first in (0, HALF):
            places = slab_places(first, HALF)
            low.append(product(of_query, places(0), NT) + product(of_value, places(2), NT))
        inner = every[:, 2 * heads :].astype(F32)
        rows = [low[0], low[1], inner[:, :HALF], inner[:, HALF:]]
        at = lax.broadcasted_iota(jnp.int32, (16, HALF), 0)
        piece_ref[0, 4 * QKV :] = sum(jnp.where(at == i, row, 0.0) for i, row in enumerate(rows)).astype(BF)

    weights = (w_query.T, w_key.T, w_value.T, w_out)
    return pl.pallas_call(
        kernel,
        grid_spec=pltpu.PrefetchScalarGridSpec(
            num_scalar_prefetch=1,
            grid=(1,),
            in_specs=[whole(w.shape) for w in weights] + [whole(bias.shape)],
            out_specs=[whole((1, 4 * heads, D)), whole((1, 4 * QKV + VECTORS, HALF))],
        ),
        out_shape=[shape_of((1, 4 * heads, D), BF), shape_of((1, 4 * QKV + VECTORS, HALF), BF)],
        compiler_params=params(),
        cost_estimate=cost(2e9, 0),
    )(scalars, *weights, bias)


def ffn_pieces(scalars, w_inner, w_outer):
    wide = w_inner.shape[1]
    rows = wide // BLOCKS

    def kernel(scalars, wi_ref, wu_ref, wt_ref, i_ref, u_ref):
        wt_ref[...] = wi_ref[...].T
        c, my = scalars[1], scalars[2]
        block = pl.ds(pl.multiple_of(my * rows, 16), rows)
        columns = pl.ds(pl.multiple_of(c * HALF, 128), HALF)
        i_ref[...] = wt_ref[block, columns]
        u_ref[...] = wu_ref[block, columns]

    return pl.pallas_call(
        kernel,
        grid_spec=pltpu.PrefetchScalarGridSpec(
            num_scalar_prefetch=1,
            grid=(1,),
            in_specs=[whole(w_inner.shape), whole(w_outer.shape)],
            out_specs=[whole((wide, D)), whole((rows, HALF)), whole((rows, HALF))],
        ),
        out_shape=[shape_of((wide, D), BF), shape_of((rows, HALF), BF), shape_of((rows, HALF), BF)],
        compiler_params=params(),
        cost_estimate=cost(2e9, 0),
    )(scalars, w_inner, w_outer)


def assemble(scalars, near, far, own, rows):
    count = near.shape[1]

    def kernel(scalars, near_ref, far_ref, own_ref, out_ref, sems):
        c, my = scalars[1], scalars[2]
        copies = [(own_ref, out_ref.at[0])]
        for m in range(BLOCKS):
            for source, side in ((near_ref, c), (far_ref, 1 - c)):
                target = out_ref.at[
                    pl.ds(1, count),
                    pl.ds(pl.multiple_of((m ^ my) * rows, 16), rows),
                    pl.ds(pl.multiple_of(side * HALF, 128), HALF),
                ]
                copies.append((source.at[m, :, pl.ds(0, rows)], target))
        run_copies(copies, sems)

    shape = (1 + count, BLOCKS * rows, D)
    return pl.pallas_call(
        kernel,
        grid_spec=pltpu.PrefetchScalarGridSpec(
            num_scalar_prefetch=1,
            grid=(1,),
            in_specs=[any_place()] * 3,
            out_specs=whole(shape),
            scratch_shapes=[pltpu.SemaphoreType.DMA((2 * BLOCKS + 1,))],
        ),
        out_shape=shape_of(shape, own.dtype),
        compiler_params=params(),
        cost_estimate=cost(2e9, 0),
    )(scalars, near, far, own)


def finish(scalars, near, far, wide, narrow):
    total, base = near.shape[1], 4 * narrow

    def kernel(scalars, near_ref, far_ref, *refs):
        *outs, held, sems = refs
        c, my = scalars[1], scalars[2]
        copies = []
        for m in range(BLOCKS):
            for source, side in ((near_ref, c), (far_ref, 1 - c)):
                copies.append((source.at[m], held.at[m ^ my, :, pl.ds(pl.multiple_of(side * HALF, 128), HALF)]))
        run_copies(copies, sems)
        for kind in range(4):
            for j in range(BLOCKS):
                outs[kind][narrow * j : narrow * (j + 1)] = held[j, narrow * kind : narrow * (kind + 1)].astype(F32)
        for j in range(BLOCKS):
            at = base + VECTORS
            outs[4][wide * j : wide * (j + 1)] = held[j, at : at + wide].astype(F32)
        last = jnp.concatenate([held[j, base + VECTORS + wide :] for j in range(BLOCKS)], axis=0)
        outs[5][...] = last.astype(F32).T
        low = held[0, base : base + VECTORS, :HALF]
        vectors = low.astype(F32)
        for out, kind in zip(outs[6:8], (0, 2)):
            halves = [product(low, slab_places(first, HALF)(kind), NN) for first in (0, HALF)]
            out[...] = halves[0][2:3] + halves[1][3:4]
        for out, i in zip(outs[8:], (0, 4, 6, 8, 10, 12, 14)):
            out[...] = jnp.concatenate([vectors[i : i + 1], vectors[i + 1 : i + 2]], axis=1)

    heads = BLOCKS * narrow
    shapes = [(heads, D)] * 4 + [(BLOCKS * wide, D), (D, BLOCKS * wide)] + [(1, heads)] * 2 + [(1, D)] * 7
    return pl.pallas_call(
        kernel,
        grid_spec=pltpu.PrefetchScalarGridSpec(
            num_scalar_prefetch=1,
            grid=(1,),
            in_specs=[any_place()] * 2,
            out_specs=[whole(shape) for shape in shapes],
            scratch_shapes=[pltpu.VMEM((BLOCKS, total, D), BF), pltpu.SemaphoreType.DMA((2 * BLOCKS,))],
        ),
        out_shape=[shape_of(shape, F32) for shape in shapes],
        compiler_params=params(),
        cost_estimate=cost(2e9, 0),
    )(scalars, near, far)


def core_add(mine, theirs):
    _, shards, rows, columns = mine.shape
    half = shards // 2

    def kernel(mine_ref, theirs_ref, own_ref, x_ref, y_ref, first_ref, second_ref):
        r = pl.program_id(0)
        total = lambda m: (mine_ref[m, 0].astype(F32) + theirs_ref[m, 0].astype(F32)).astype(BF)
        own_ref[0], x_ref[0], y_ref[0] = total(0), total(1), total(2)

        @pl.when(r < half)
        def _():
            first_ref[0] = total(3)

        @pl.when(r >= half)
        def _():
            second_ref[0] = total(3)

    blocks = pl.BlockSpec((BLOCKS, 1, rows, columns), lambda r: (0, r, 0, 0))
    block = lambda index: pl.BlockSpec((1, rows, columns), lambda r: (index(r), 0, 0))
    return pl.pallas_call(
        kernel,
        grid=(shards,),
        in_specs=[blocks, blocks],
        out_specs=[block(lambda r: r)] * 3
        + [block(lambda r: jnp.minimum(r, half - 1)), block(lambda r: jnp.maximum(r - half, 0))],
        out_shape=[shape_of((shards, rows, columns), BF)] * 3 + [shape_of((half, rows, columns), BF)] * 2,
        compiler_params=params(),
        cost_estimate=cost(1e9, 0),
    )(mine, theirs)


def plane_add(for_x, for_y, via_y, via_x):
    half, rows, columns = via_y.shape

    def kernel(x_ref, y_ref, via_y_ref, via_x_ref, x_out, y_out):
        x_out[...] = (x_ref[...].astype(F32) + via_y_ref[...].astype(F32)).astype(BF)
        y_out[...] = (y_ref[...].astype(F32) + via_x_ref[...].astype(F32)).astype(BF)

    block = lambda shift: pl.BlockSpec((1, rows, columns), lambda r: (r + shift, 0, 0))
    return pl.pallas_call(
        kernel,
        grid=(half,),
        in_specs=[block(0), block(half), block(0), block(0)],
        out_specs=[block(0), block(half)],
        out_shape=[shape_of(for_x.shape, BF)] * 2,
        input_output_aliases={0: 0, 1: 1},
        compiler_params=params(),
        cost_estimate=cost(1e9, 0),
    )(for_x, for_y, via_y, via_x)


def tie(array, *before):
    return lax.optimization_barrier((array,) + before)[0]


def build(n_dp, n_tensor):
    flip = {bit: [(i, i ^ bit) for i in range(n_dp)] for bit in (1, 2, 4, 6)}
    f32 = lambda array: array.astype(F32)
    half = n_tensor // 2

    def across(array, bit):
        return lax.ppermute(array, "dp", flip[bit])

    def along(array, r):
        return lax.ppermute(array, "tensor", [(i, i ^ r) for i in range(n_tensor)])

    def from_all(array):
        return [along(array, r) for r in range(1, n_tensor)]

    def from_all_by_steps(array):
        two = along(array, 2)
        one, three = along(jnp.stack([array, two]), 1)
        return [one, two, three]

    def plane(array):
        return [across(array, bit) for bit in (2, 4, 6)]

    def rows_round(k, up, down):
        up = lax.ppermute(up, "tensor", [(i, i + 1) for i in range(k - 1, n_tensor - 1)])
        return up, lax.ppermute(down, "tensor", [(i + 1, i) for i in range(n_tensor - k)])

    def place_rows(z, own, ups, downs):
        seq = own.shape[0]
        rows = jnp.zeros((n_tensor * seq, D), own.dtype)
        rows = lax.dynamic_update_slice(rows, own, (z * seq, 0))
        for k in (2, 1, 3):
            got = jnp.where(z >= k, ups[k - 1], downs[n_tensor - 1 - k])
            rows = lax.dynamic_update_slice(rows, got, (((z - k) & (n_tensor - 1)) * seq, 0))
        return rows

    def add(*terms):
        return sum(f32(term) for term in terms).astype(BF)

    def plane_one(diagonal_y, diagonal_x):
        return across(diagonal_y, 4), across(diagonal_x, 2)

    def plane_two(for_x, for_y):
        return across(for_x, 2), across(for_y, 4)

    def line_ends(far):
        return lax.ppermute(far, "tensor", [(0, 1), (3, 2)])

    def line_middle(far):
        return lax.ppermute(far, "tensor", [(1, 2), (2, 1)])

    def line_end(own, last):
        total = own + f32(last)
        step = 8
        while step < n_dp:
            total = total + lax.ppermute(total, "dp", [(i, i ^ step) for i in range(n_dp)])
            step *= 2
        return total.astype(BF)

    def body(
        tokens, w_query, b_query, w_key, w_value, b_value, w_attn_out, b_attn_out, gain_one, shift_one,
        w_inner, b_inner, w_outer, b_outer, gain_two, shift_two, cotangent, lengths, row_ids, col_ids,
    ):
        block = w_inner.shape[1] // BLOCKS
        index = lax.axis_index("dp")
        z = lax.axis_index("tensor")
        c, my = index & 1, (index >> 1) & 3
        scalars = jnp.stack([lax.dynamic_index_in_dim(lengths, z, keepdims=False), c, my, z]).astype(jnp.int32)
        tags = (row_ids, col_ids)
        vectors_one = f32(jnp.stack([b_attn_out, gain_one, shift_one]))
        vectors_two = f32(jnp.stack([b_outer, gain_two, shift_two]))

        bias = jnp.concatenate([b_query, b_value, b_inner])[None]
        slab, piece_a = attention_piece(scalars, w_query, w_key, w_value, w_attn_out, bias)
        with jax.named_scope("line attention weights"):
            line_a = from_all(piece_a)
        first = attention_forward(scalars, tokens, slab, piece_a, tags, n_tensor, 0)
        w_inner_t, piece_i, piece_u = ffn_pieces(tie(scalars, slab), w_inner, w_outer)

        with jax.named_scope("line inner weights"):
            line_i = from_all(tie(piece_i, *line_a, first[2]))
        own_a = jnp.concatenate([tie(line_a[0], piece_i, first[2])] + line_a[1:])
        with jax.named_scope("plane attention weights"):
            plane_a = plane(own_a)

        own_i = jnp.stack([tie(line_i[0], *plane_a)] + line_i[1:])
        near_a = jnp.stack([tie(own_a, *line_i), *plane_a])
        with jax.named_scope("core attention weights"):
            far_a = across(near_a, 1)
        with jax.named_scope("plane inner weights"):
            plane_i = plane(own_i)
        with jax.named_scope("line outer weights"):
            line_u = from_all(tie(piece_u, *line_i, far_a))

        w_attn = assemble(scalars, near_a, far_a, slab[0], 4 * QKV)
        qkv, heads_out, lse = attention_forward(scalars, tokens, w_attn, own_a, tags, n_tensor, 1, first)
        own_u = jnp.stack([tie(line_u[0], lse, *plane_i)] + line_u[1:])
        near_i = jnp.stack([tie(own_i, *line_u, lse), *plane_i])
        with jax.named_scope("core inner weights"):
            far_i = across(near_i, 1)
        with jax.named_scope("plane outer weights"):
            plane_u = plane(own_u)

        w_in = assemble(scalars, near_i, far_i, w_inner_t, block)
        normed, inv_spread, hidden, low, act, slope = inner_half(
            scalars, heads_out, w_attn, tokens, vectors_one, w_in, piece_a, own_a
        )
        near_u = jnp.stack([tie(own_u, inv_spread), *plane_u])
        with jax.named_scope("core outer weights"):
            far_u = across(near_u, 1)
        w_up = assemble(scalars, near_u, far_u, w_outer, block)
        out_rows, grad_two, sums_two = outer_half(scalars, act, w_up, hidden, cotangent, vectors_two)

        barrier = lambda *arrays: lax.optimization_barrier(arrays)
        with jax.named_scope("rows 1"):
            up_1, down_1 = rows_round(1, out_rows, out_rows)
        mine_u, other_u = weight_grad(scalars, act, grad_two)
        with jax.named_scope("core outer grad"):
            theirs_u = across(other_u, 1)
        grad_one, grad_one_low, grad_inner, db_inner, sums_one = ffn_back(
            tie(grad_two, mine_u), slope, w_up, w_in, normed, inv_spread, vectors_one
        )
        grad_one, grad_inner, theirs_u, up_1, down_1 = barrier(grad_one, grad_inner, theirs_u, up_1, down_1)
        with jax.named_scope("rows 2"):
            up_2, down_2 = rows_round(2, up_1, down_1)
        own_u, x_u, y_u, *via_u = core_add(mine_u, theirs_u)
        with jax.named_scope("plane one outer grad"):
            via_u = plane_one(*via_u)
        mine_i, other_i = weight_grad(scalars, tie(grad_inner, own_u), low)
        vectors = (db_inner, sums_one, sums_two)
        pieces = ()

        def shard_back(start, r):
            dtype = F32 if r else BF
            return attention_backward(
                scalars, tokens, w_attn, qkv, heads_out, lse, grad_one_low, start, tags, vectors, r, dtype, pieces
            )

        start, *pieces = shard_back(tie(grad_one, mine_i), 3)
        start, *via_u = barrier(start, *via_u)
        x_u, y_u = plane_add(x_u, y_u, *via_u)
        with jax.named_scope("plane two outer grad"):
            plane_u = plane_two(x_u, y_u)
        start, *pieces = shard_back(tie(start, x_u), 2)
        with jax.named_scope("core inner grad"):
            theirs_i = across(tie(other_i, start), 1)
        start, up_2, down_2 = barrier(start, up_2, down_2)
        with jax.named_scope("rows 3"):
            up_3, down_3 = rows_round(3, up_2, down_2)
        start, *pieces = shard_back(start, 1)
        start, theirs_i, *plane_u = barrier(start, theirs_i, *plane_u)
        own_i, x_i, y_i, *via_i = core_add(mine_i, theirs_i)
        with jax.named_scope("plane one inner grad"):
            via_i = plane_one(*via_i)
        grad_rows, mine_a, other_a = shard_back(tie(start, own_i), 0)
        grad_rows, mine_a, other_a, up_3, down_3, *via_i = barrier(grad_rows, mine_a, other_a, up_3, down_3, *via_i)

        with jax.named_scope("grad rows 1"):
            go_1, back_1 = rows_round(1, grad_rows, grad_rows)
        with jax.named_scope("core attention grad"):
            theirs_a = across(other_a, 1)
        x_i, y_i = plane_add(x_i, y_i, *via_i)
        with jax.named_scope("plane two inner grad"):
            plane_i = plane_two(x_i, y_i)
        own_a, x_a, y_a, *via_a = core_add(mine_a, theirs_a)
        *via_a, plane_i_x, plane_i_y = barrier(*via_a, *plane_i)
        with jax.named_scope("plane one attention grad"):
            via_a = plane_one(*via_a)
        groups = ((own_u, *plane_u), (own_i, plane_i_x, plane_i_y))
        near_f = jnp.concatenate([sum(f32(a[:half]) for a in group) for group in groups], axis=1)
        far_f = jnp.concatenate([add(*[a[half:] for a in group]) for group in groups], axis=1)
        with jax.named_scope("line ends ffn grad"):
            ends_f = line_ends(far_f)
        go_1, back_1, *via_a = barrier(go_1, back_1, *via_a)
        with jax.named_scope("grad rows 2"):
            go_2, back_2 = rows_round(2, go_1, back_1)
        x_a, y_a = plane_add(x_a, y_a, *via_a)
        with jax.named_scope("plane two attention grad"):
            plane_a = plane_two(x_a, y_a)
        layer_out = place_rows(z, tie(out_rows, *via_a), (up_1, up_2, up_3), (down_1, down_2, down_3))
        go_2, back_2, ends_f, layer_out, *plane_a = barrier(go_2, back_2, ends_f, layer_out, *plane_a)
        with jax.named_scope("grad rows 3"):
            go_3, back_3 = rows_round(3, go_2, back_2)
        with jax.named_scope("line middle ffn grad"):
            middle_f = line_middle(add(far_f, ends_f[::-1]))
        group = (own_a, *plane_a)
        odd_a = add(*[a[1::2] for a in group])
        with jax.named_scope("line one attention grad"):
            odd_a = along(odd_a, 1)
        even_a = sum(f32(a[0::2]) for a in group)
        odd_a, middle_f = barrier(odd_a, middle_f)
        near_f = near_f + f32(middle_f[::-1])
        with jax.named_scope("line pair ffn grad"):
            pair_f = along(near_f[1].astype(BF), 1)
        even_a = even_a + f32(odd_a)
        with jax.named_scope("line two attention grad"):
            last_a = along(even_a[1].astype(BF), 2)
        last_a, pair_f = barrier(last_a, pair_f)
        done = jnp.concatenate([line_end(even_a[0], last_a), line_end(near_f[0], pair_f)])
        done, go_3, back_3 = barrier(done, go_3, back_3)
        with jax.named_scope("plane result"):
            found = plane(done)
        grad_tokens = place_rows(z, grad_rows, (go_1, go_2, go_3), (back_1, back_2, back_3))
        near = jnp.stack([done, *found])
        with jax.named_scope("core result"):
            far = across(near, 1)
        grads = finish(scalars, near, far, block, QKV)
        grad_wq, grad_wk, grad_wv, grad_wo, grad_wu, grad_wi, *vectors = grads
        grad_bq, grad_bv, grad_bi, gain_1, shift_1, b_1, gain_2, shift_2, b_2 = [v.reshape(-1) for v in vectors]

        return (
            layer_out,
            grad_tokens,
            grad_wq.T,
            grad_bq,
            grad_wk.T,
            grad_wv.T,
            grad_bv,
            grad_wo,
            b_1,
            gain_1,
            shift_1,
            grad_wi,
            grad_bi,
            grad_wu,
            b_2,
            gain_2,
            shift_2,
        )

    return body


def solution(mesh):
    rows, columns, out = P("dp", None), P(None, "tensor"), P("tensor", None)
    one = P("tensor")
    in_specs = (
        rows, columns, one, columns, columns, one, out, P(), P(), P(), columns, one, out, P(), P(), P(),
        rows, P("dp"), rows, rows,
    )
    out_specs = (
        rows, rows, columns, one, columns, columns, one, out, P(), P(), P(), columns, one, out, P(), P(), P(),
    )
    body = build(mesh.shape["dp"], mesh.shape["tensor"])
    return jax.shard_map(body, mesh=mesh, in_specs=in_specs, out_specs=out_specs, check_vma=False)
```

```python
import functools

import jax
import jax.numpy as jnp
from jax import lax
from jax.experimental import pallas as pl
from jax.experimental.pallas import tpu as pltpu
from jax.sharding import PartitionSpec as P

F32 = jnp.float32
BF = jnp.bfloat16
HD = 64
D = 768
HALF = D // 2
BLOCKS = 4
QKV = 48
epsilon = 1e-12
masked_value = -1e30
CHUNK = 128
SCALE = 0.05
VECTORS = 16

NN = (((1,), (0,)), ((), ()))
NT = (((1,), (1,)), ((), ()))
TN = (((0,), (0,)), ((), ()))


def product(left, right, dims):
    return lax.dot_general(left, right, dims, preferred_element_type=F32)


def shape_of(shape, dtype):
    return jax.ShapeDtypeStruct(shape, dtype)


def whole(shape):
    return pl.BlockSpec(shape, lambda r, *_: (0,) * len(shape))


def each(shape, shift=0):
    return pl.BlockSpec((1,) + shape, lambda r, *_: (r + shift,) + (0,) * len(shape))


def params(mebibytes=16):
    return pltpu.CompilerParams(vmem_limit_bytes=mebibytes * 1024 * 1024)


def cost(flops, moved, exps=0):
    return pl.CostEstimate(flops=int(flops * SCALE), bytes_accessed=int(moved * SCALE), transcendentals=int(exps))


def rows_of(ref, kind):
    width = 3 * QKV
    return jnp.concatenate(
        [ref[0, width * j + QKV * kind : width * j + QKV * (kind + 1)] for j in range(BLOCKS)], axis=0
    )


class Masks:
    def __init__(self, scalars, lengths, row_ref, col_ref):
        table = scalars[2]
        length = lengths[table]
        row_q = row_ref[pl.ds(table, 1), :].astype(F32)
        col_q = col_ref[pl.ds(table, 1), :].astype(F32)
        row_k, col_k = as_column(row_q), as_column(col_q)
        position = lax.broadcasted_iota(jnp.int32, row_k.shape, 0)
        self.here = position < length
        self.leading = position == 0
        self.row_k = jnp.where(self.here, row_k, -1.0)
        self.col_k = jnp.where(self.here, col_k, -1.0)
        self.row_q, self.col_q = row_q, col_q

    def scores(self, logits, kind):
        if kind == 0:
            visible = self.here
        elif kind == 1:
            visible = (self.row_k == self.row_q) | self.leading
        else:
            visible = (self.col_k == self.col_q) | self.leading
        return jnp.where(visible, logits, masked_value)


def as_column(row):
    return jnp.broadcast_to(row, (8, row.shape[1])).T[:, 0:1]


def projection_rows(w_ref):
    return jnp.concatenate([w_ref[0, 4 * QKV * j : 4 * QKV * j + 3 * QKV] for j in range(BLOCKS)], axis=0)


def output_rows(w_ref, shard=0):
    return jnp.concatenate(
        [w_ref[shard, 4 * QKV * j + 3 * QKV : 4 * QKV * (j + 1)] for j in range(BLOCKS)], axis=0
    )


def attention_forward_kernel(scalars, lengths, x_ref, w_ref, b_ref, row_ref, col_ref, *rest):
    qkv_ref, o_ref, lse_ref = rest[-3:]
    seq = x_ref.shape[0]
    bias = b_ref[0].astype(F32)
    bias = jnp.concatenate([bias[0:1], bias[1:2, : 3 * BLOCKS * QKV - HALF]], axis=1)
    qkv = product(projection_rows(w_ref), x_ref[...], NT) + as_column(bias)
    low = qkv.astype(BF)
    is_query = lax.broadcasted_iota(jnp.int32, (qkv.shape[0], 1), 0) % (3 * QKV) < QKV
    low = jnp.where(is_query, low * jnp.asarray(HD**-0.5, BF), low)
    qkv_ref[0] = low
    masks = Masks(scalars, lengths, row_ref, col_ref)
    q_t, k_t, v_t = rows_of(qkv_ref, 0), rows_of(qkv_ref, 1), rows_of(qkv_ref, 2)
    outs, logs = [], []
    for head in range(q_t.shape[0] // HD):
        rows = slice(HD * head, HD * (head + 1))
        scores = masks.scores(product(k_t[rows].T, q_t[rows], NN), head % 3)
        highest = jnp.max(scores, axis=0, keepdims=True)
        weights = jnp.exp(scores - highest).astype(BF)
        with_ones = jnp.concatenate([v_t[rows], jnp.ones((16, seq), BF)], axis=0)
        blended = product(with_ones, weights, NN)
        total = blended[HD : HD + 1]
        outs.append(blended[:HD] * (1.0 / total))
        logs.append(highest + jnp.log(total))
    o_ref[0] = jnp.concatenate(outs, axis=0).astype(BF)
    logs.append(jnp.zeros((8 - len(logs), seq), F32))
    lse_ref[0] = jnp.concatenate(logs, axis=0)


def in_hbm():
    return pl.BlockSpec(memory_space=pltpu.HBM)


def table_rows(seq):
    return pl.BlockSpec((seq, D), lambda r, scalars, *_: (scalars[2], 0))


def bias_rows(shift=0):
    return pl.BlockSpec((1, VECTORS, HALF), lambda r, *_: (r + shift, 4 * QKV // VECTORS, 0))


def attention_forward(scalars, lengths, tokens, weights, pieces, tags, shards, first, carried=None):
    wide, seq = 3 * BLOCKS * QKV, tags[0].shape[1]
    count, at = pieces.shape[0], first if carried else 0
    out_shape = [
        shape_of((shards, wide, seq), BF),
        shape_of((shards, wide // 3, seq), BF),
        shape_of((shards, 8, seq), F32),
    ]
    kept = list(carried) if carried else []
    return pl.pallas_call(
        attention_forward_kernel,
        grid_spec=pltpu.PrefetchScalarGridSpec(
            num_scalar_prefetch=2,
            grid=(count,),
            in_specs=[
                table_rows(seq),
                each((weights.shape[1], D), at),
                bias_rows(),
                whole(tags[0].shape),
                whole(tags[1].shape),
            ]
            + [pl.BlockSpec(memory_space=pl.ANY)] * len(kept),
            out_specs=[each(s.shape[1:], first) for s in out_shape],
        ),
        out_shape=out_shape,
        input_output_aliases={7 + i: i for i in range(len(kept))},
        compiler_params=params(),
        cost_estimate=cost(count * 3e9, count * 3e6),
    )(scalars, lengths, tokens, weights, pieces, *tags, *kept)


def attention_backward_kernel(
    scalars, lengths, x_hbm, w_hbm, qkv_hbm, o_hbm, lse_hbm, up_hbm, start_hbm, row_ref, col_ref, dbi_ref, one_ref, two_ref,
    *refs, shard, carried,
):
    dx_ref, mine_ref, other_ref, d_ref, x_ref, w_ref, qkv_ref, o_ref, lse_ref, low_ref, start_ref, sems = refs[carried:]
    seq = x_ref.shape[0]
    at = pl.ds(shard, 1)
    copies = [
        (w_hbm.at[at], w_ref),
        (up_hbm, low_ref),
        (qkv_hbm.at[at], qkv_ref),
        (o_hbm.at[at], o_ref),
        (lse_hbm.at[at], lse_ref),
        (x_hbm.at[pl.ds(pl.multiple_of(scalars[2] * seq, 128), seq)], x_ref),
        (start_hbm, start_ref),
    ]
    started = [pltpu.make_async_copy(source, target, sems.at[i]) for i, (source, target) in enumerate(copies)]
    for copy in started:
        copy.start()
    for copy in started[:5]:
        copy.wait()
    masks = Masks(scalars, lengths, row_ref, col_ref)
    q_t, k_t, v_t = rows_of(qkv_ref, 0), rows_of(qkv_ref, 1), rows_of(qkv_ref, 2)
    grad_heads = product(output_rows(w_ref), low_ref[...], NT).astype(BF)
    heads_out = o_ref[0]
    parts = [[], [], []]
    for head in range(q_t.shape[0] // HD):
        rows = slice(HD * head, HD * (head + 1))
        queries_t, keys_t, grad_t = q_t[rows], k_t[rows], grad_heads[rows]
        scores = masks.scores(product(keys_t.T, queries_t, NN), head % 3)
        chances = jnp.exp(scores - lse_ref[0, head : head + 1])
        grad_chances = product(v_t[rows].T, grad_t, NN)
        inner = jnp.sum(grad_t.astype(F32) * heads_out[rows].astype(F32), axis=0, keepdims=True)
        grad_logits = (chances * (grad_chances - inner)).astype(BF)
        parts[2].append(product(chances.astype(BF), grad_t.T, NN).T)
        parts[1].append(product(grad_logits, queries_t.T, NN).T)
        parts[0].append(product(keys_t, grad_logits, NN) * HD**-0.5)
    for kind in range(3):
        joined = jnp.concatenate(parts[kind], axis=0).astype(BF)
        for j in range(BLOCKS):
            base = 3 * QKV * j + QKV * kind
            d_ref[base : base + QKV, :] = joined[QKV * j : QKV * (j + 1)]
    grads_low = d_ref[...]
    for copy in started[5:]:
        copy.wait()
    dx_ref[...] = (start_ref[...] + product(grads_low, projection_rows(w_ref), TN)).astype(dx_ref.dtype)
    db = product(jnp.ones((8, seq), BF), grads_low, NT)[:1]
    vectors = [dbi_ref[0, :, :HALF], dbi_ref[0, :, HALF:], db[:, :HALF]]
    vectors.append(jnp.concatenate([db[:, HALF:], jnp.zeros((1, 2 * HALF - db.shape[1]), F32)], axis=1))
    for sums_ref in (one_ref, two_ref):
        for i in range(3):
            vectors += [sums_ref[i : i + 1, :HALF], sums_ref[i : i + 1, HALF:]]
    vectors = jnp.concatenate(vectors, axis=0).astype(BF)
    c, my = scalars[0], scalars[1]
    for half, out_ref in enumerate((mine_ref, other_ref)):
        start = pl.multiple_of(jnp.where(c == half, 0, HALF), 128)
        grad_w = product(grads_low, x_ref[:, pl.ds(start, HALF)], NN).astype(BF)
        grad_wo = product(heads_out, low_ref[:, pl.ds(start, HALF)], NN).astype(BF)
        for j in range(BLOCKS):
            out_ref[j ^ my, 0, : 3 * QKV] = grad_w[3 * QKV * j : 3 * QKV * (j + 1)]
            out_ref[j ^ my, 0, 3 * QKV : 4 * QKV] = grad_wo[QKV * j : QKV * (j + 1)]
            here = jnp.where(c == half, 1.0, 0.0).astype(BF) if j == 0 else jnp.zeros((), BF)
            out_ref[j ^ my, 0, 4 * QKV :] = vectors * here


def attention_backward(
    scalars, lengths, tokens, weights, qkv, heads_out, lse, upstream, start, tags, vectors, shard, dtype, carried
):
    shards, wide, seq = qkv.shape
    rows = 4 * QKV + VECTORS
    pieces = shape_of((BLOCKS, shards, rows, HALF), BF)
    piece = pl.BlockSpec((BLOCKS, 1, rows, HALF), lambda r, *_: (0, shard, 0, 0))
    return pl.pallas_call(
        functools.partial(attention_backward_kernel, shard=shard, carried=len(carried)),
        grid_spec=pltpu.PrefetchScalarGridSpec(
            num_scalar_prefetch=2,
            grid=(1,),
            in_specs=[in_hbm()] * 7
            + [whole(tags[0].shape), whole(tags[1].shape), each(vectors[0].shape[1:], shard)]
            + [whole((8, D)), whole((8, D))]
            + [in_hbm()] * len(carried),
            out_specs=[whole((seq, D)), piece, piece],
            scratch_shapes=[
                pltpu.VMEM((wide, seq), BF),
                pltpu.VMEM((seq, D), BF),
                pltpu.VMEM((1,) + weights.shape[1:], BF),
                pltpu.VMEM((1, wide, seq), BF),
                pltpu.VMEM((1, wide // 3, seq), BF),
                pltpu.VMEM((1, 8, seq), F32),
                pltpu.VMEM((seq, D), BF),
                pltpu.VMEM((seq, D), F32),
                pltpu.SemaphoreType.DMA((7,)),
            ],
        ),
        out_shape=[shape_of((seq, D), dtype), pieces, pieces],
        input_output_aliases={14 + i: 1 + i for i in range(len(carried))},
        compiler_params=params(),
        cost_estimate=cost(5e9, 5e6),
    )(scalars, lengths, tokens, weights, qkv, heads_out, lse, upstream, start, *tags, *vectors, *carried)


def gelu_pair(x):
    bell = jnp.exp(x * x * -0.5)
    t = 1.0 / (1.0 + (0.3275911 * 0.70710678118654752) * jnp.abs(x))
    series = 0.5 * 1.061405429
    for factor in (-1.453152027, 1.421413741, -0.284496736, 0.254829592):
        series = series * t + 0.5 * factor
    tail = series * t * bell
    below = jnp.where(x < 0, tail, 1.0 - tail)
    return x * below, below + x * (bell * 0.3989422804014327)


def normalize(residual):
    centre = residual - jnp.mean(residual, axis=-1, keepdims=True)
    inv_spread = lax.rsqrt(jnp.mean(centre * centre, axis=-1, keepdims=True) + epsilon)
    return centre * inv_spread, inv_spread


def norm_back(upstream, normed, inv_spread, gain):
    scaled = upstream * gain
    return inv_spread * (
        scaled
        - jnp.mean(scaled, axis=-1, keepdims=True)
        - normed * jnp.mean(scaled * normed, axis=-1, keepdims=True)
    )


def add_sums(sums, *terms):
    return [total + jnp.sum(term, axis=0, keepdims=True) for total, term in zip(sums, terms)]


def store_sums(ref, sums):
    ref[...] = jnp.concatenate(sums + [jnp.zeros((8 - len(sums), D), F32)], axis=0)


def inner_kernel(
    scalars, o_ref, wo_ref, x_ref, vec_ref, wi_ref, own_ref, others_ref,
    normed_ref, inv_ref, hidden_ref, low_ref, act_ref, slope_ref,
):
    seq, r = x_ref.shape[0], pl.program_id(0)
    bias = jnp.where(r == 0, own_ref[0].astype(F32), others_ref[jnp.maximum(r - 1, 0)].astype(F32))
    bias = jnp.concatenate([bias[2:3], bias[3:4]], axis=1)

    @pl.when(r == 0)
    def _():
        for start in range(0, seq, CHUNK):
            rows = slice(start, start + CHUNK)
            residual = vec_ref[0:1] + x_ref[rows].astype(F32)
            for shard in range(o_ref.shape[0]):
                residual = residual + product(o_ref[shard, :, rows], output_rows(wo_ref, shard), TN)
            normed, inv_spread = normalize(residual)
            hidden = normed * vec_ref[1:2] + vec_ref[2:3]
            normed_ref[rows], inv_ref[rows], hidden_ref[rows] = normed, inv_spread, hidden
            low_ref[rows] = hidden.astype(BF)

    for start in range(0, seq, CHUNK):
        rows = slice(start, start + CHUNK)
        act, slope = gelu_pair(product(low_ref[rows], wi_ref[0], NT) + bias)
        act_ref[0, rows] = act.astype(BF)
        slope_ref[0, rows] = slope.astype(BF)


def inner_half(scalars, heads_out, w_out, tokens, vectors, w_inner, own_piece, pieces):
    shards, wide, seq = w_inner.shape[0], w_inner.shape[1], heads_out.shape[2]
    return pl.pallas_call(
        inner_kernel,
        grid_spec=pltpu.PrefetchScalarGridSpec(
            num_scalar_prefetch=1,
            grid=(shards,),
            in_specs=[
                whole(heads_out.shape),
                whole(w_out.shape),
                table_rows(seq),
                whole(vectors.shape),
                each((wide, D)),
                pl.BlockSpec((1, VECTORS, HALF), lambda r, *_: (0, 4 * QKV // VECTORS, 0)),
                pl.BlockSpec((shards - 1, VECTORS, HALF), lambda r, *_: (0, 4 * QKV // VECTORS, 0)),
            ],
            out_specs=[
                whole((seq, D)),
                whole((seq, 1)),
                whole((seq, D)),
                whole((seq, D)),
                each((seq, wide)),
                each((seq, wide)),
            ],
        ),
        out_shape=[
            shape_of((seq, D), F32),
            shape_of((seq, 1), F32),
            shape_of((seq, D), F32),
            shape_of((seq, D), BF),
            shape_of((shards, seq, wide), BF),
            shape_of((shards, seq, wide), BF),
        ],
        compiler_params=params(),
        cost_estimate=cost(12e9, 20e6),
    )(scalars, heads_out, w_out, tokens, vectors, w_inner, own_piece, pieces)


def outer_kernel(scalars, act_ref, wu_ref, hidden_ref, cot_ref, vec_ref, out_ref, grad_ref, sums_ref, acc_ref):
    r, last, seq = pl.program_id(0), pl.num_programs(0) - 1, hidden_ref.shape[0]

    @pl.when(r == 0)
    def _():
        acc_ref[...] = hidden_ref[...] + vec_ref[0:1]

    acc_ref[...] = acc_ref[...] + product(act_ref[0], wu_ref[0], NN)

    @pl.when(r == last)
    def _():
        sums = [jnp.zeros((1, D), F32)] * 3
        gain = vec_ref[1:2]
        for start in range(0, seq, CHUNK):
            rows = slice(start, start + CHUNK)
            normed, inv_spread = normalize(acc_ref[rows])
            out_ref[rows] = (normed * gain + vec_ref[2:3]).astype(BF)
            upstream = cot_ref[rows].astype(F32)
            grad = norm_back(upstream, normed, inv_spread, gain)
            grad_ref[rows] = grad
            sums = add_sums(sums, upstream * normed, upstream, grad)
        store_sums(sums_ref, sums)


def outer_half(scalars, act, w_outer, hidden, cotangent, vectors):
    shards, seq, wide = act.shape
    return pl.pallas_call(
        outer_kernel,
        grid_spec=pltpu.PrefetchScalarGridSpec(
            num_scalar_prefetch=1,
            grid=(shards,),
            in_specs=[
                each((seq, wide)),
                each((wide, D)),
                whole((seq, D)),
                table_rows(seq),
                whole(vectors.shape),
            ],
            out_specs=[whole((seq, D)), whole((seq, D)), whole((8, D))],
            scratch_shapes=[pltpu.VMEM((seq, D), F32)],
        ),
        out_shape=[shape_of((seq, D), BF), shape_of((seq, D), F32), shape_of((8, D), F32)],
        compiler_params=params(),
        cost_estimate=cost(5e9, 14e6),
    )(scalars, act, w_outer, hidden, cotangent, vectors)


def ffn_back_kernel(up_ref, start_ref, slope_ref, wu_ref, wi_ref, *refs, final):
    if final:
        normed_ref, inv_ref, vec_ref, *refs = refs[:3] + refs[5:]
        grad_ref, inner_ref, db_ref, grad_low_ref, sums_ref, acc_ref, low_ref = refs
    else:
        grad_ref, inner_ref, db_ref, acc_ref, low_ref = refs
    r, last = pl.program_id(0), pl.num_programs(0) - 1
    seq, wide = up_ref.shape[0], wi_ref.shape[1]

    @pl.when(r == 0)
    def _():
        acc_ref[...] = start_ref[...]
        low_ref[...] = up_ref[...].astype(BF)

    db = jnp.zeros((1, wide), F32)
    for start in range(0, seq, CHUNK):
        rows = slice(start, start + CHUNK)
        grad_inner = product(low_ref[rows], wu_ref[0], NT) * slope_ref[0, rows].astype(F32)
        db = db + jnp.sum(grad_inner, axis=0, keepdims=True)
        inner_ref[0, rows] = grad_inner.astype(BF)
    db_ref[0] = db
    acc_ref[...] = acc_ref[...] + product(inner_ref[0], wi_ref[0], NN)

    @pl.when(r == last)
    def _():
        if not final:
            grad_ref[...] = acc_ref[...]
            return
        sums = [jnp.zeros((1, D), F32)] * 3
        for start in range(0, seq, CHUNK):
            rows = slice(start, start + CHUNK)
            upstream, normed = acc_ref[rows], normed_ref[rows]
            grad = norm_back(upstream, normed, inv_ref[rows], vec_ref[1:2])
            grad_ref[rows] = grad
            grad_low_ref[rows] = grad.astype(BF)
            sums = add_sums(sums, upstream * normed, upstream, grad)
        store_sums(sums_ref, sums)


def ffn_back(upstream, start, slope, w_outer, w_inner, first, count, norm=(), carried=()):
    shards, seq, wide = slope.shape
    final = bool(norm)
    out_specs = [whole((seq, D)), each((seq, wide), first), each((1, wide), first)]
    out_shape = [shape_of((seq, D), F32), shape_of((shards, seq, wide), BF), shape_of((shards, 1, wide), F32)]
    if final:
        out_specs += [whole((seq, D)), whole((8, D))]
        out_shape += [shape_of((seq, D), BF), shape_of((8, D), F32)]
    return pl.pallas_call(
        functools.partial(ffn_back_kernel, final=final),
        grid=(count,),
        in_specs=[
            whole((seq, D)),
            whole((seq, D)),
            each((seq, wide), first),
            each((wide, D), first),
            each((wide, D), first),
        ]
        + [whole(array.shape) for array in norm]
        + [any_place()] * len(carried),
        out_specs=out_specs,
        out_shape=out_shape,
        input_output_aliases={8 + i: 1 + i for i in range(len(carried))},
        scratch_shapes=[pltpu.VMEM((seq, D), F32), pltpu.VMEM((seq, D), BF)],
        compiler_params=params(),
        cost_estimate=cost(count * 3e9, count * 4e6),
    )(upstream, start, slope, w_outer, w_inner, *norm, *carried)


def weight_grad_kernel(scalars, left_ref, right_ref, mine_ref, other_ref, low_ref):
    @pl.when(pl.program_id(0) == 0)
    def _():
        low_ref[...] = right_ref[...].astype(BF)

    c, my = scalars[0], scalars[1]
    rows = mine_ref.shape[2]
    for half, out_ref in enumerate((mine_ref, other_ref)):
        start = pl.multiple_of(jnp.where(c == half, 0, HALF), 128)
        grad = product(left_ref[0], low_ref[:, pl.ds(start, HALF)], TN).astype(BF)
        for j in range(BLOCKS):
            out_ref[j ^ my, 0] = grad[rows * j : rows * (j + 1)]


def weight_grad(scalars, left, right):
    shards, seq, wide = left.shape
    piece = pl.BlockSpec((BLOCKS, 1, wide // BLOCKS, HALF), lambda r, *_: (0, r, 0, 0))
    pieces = shape_of((BLOCKS, shards, wide // BLOCKS, HALF), BF)
    return pl.pallas_call(
        weight_grad_kernel,
        grid_spec=pltpu.PrefetchScalarGridSpec(
            num_scalar_prefetch=1,
            grid=(shards,),
            in_specs=[each((seq, wide)), whole((seq, D))],
            out_specs=[piece, piece],
            scratch_shapes=[pltpu.VMEM((seq, D), BF)],
        ),
        out_shape=[pieces, pieces],
        compiler_params=params(),
        cost_estimate=cost(shards * 1.5e9, shards * 2e6),
    )(scalars, left, right)


def run_copies(copies, sems):
    started = [pltpu.make_async_copy(source, target, sems.at[i]) for i, (source, target) in enumerate(copies)]
    for copy in started:
        copy.start()
    for copy in started:
        copy.wait()


def any_place():
    return pl.BlockSpec(memory_space=pl.ANY)


def slab_places(first, columns):
    col = lax.broadcasted_iota(jnp.int32, (columns, BLOCKS * QKV), 0) + first
    feature = lax.broadcasted_iota(jnp.int32, (columns, BLOCKS * QKV), 1)
    block = sum((feature >= QKV * j).astype(jnp.int32) for j in range(1, BLOCKS))
    return lambda kind: (col == feature + block * 2 * QKV + QKV * kind).astype(BF)


def attention_piece(scalars, w_query, w_key, w_value, w_out, biases):
    heads = BLOCKS * QKV

    def kernel(scalars, *refs):
        w_refs, (query_ref, value_ref, inner_ref, slab_ref, piece_ref, sems) = refs[:4], refs[4:]
        copies = []
        for j in range(BLOCKS):
            for kind, w_ref in enumerate(w_refs):
                base = QKV * (4 * j + kind)
                copies.append((w_ref.at[pl.ds(QKV * j, QKV)], slab_ref.at[0, pl.ds(base, QKV)]))
        started = [pltpu.make_async_copy(source, target, sems.at[i]) for i, (source, target) in enumerate(copies)]
        for copy in started:
            copy.start()
        every = lambda ref: jnp.broadcast_to(ref[...].astype(F32).reshape(1, -1), (16, ref.shape[0]))
        of_query, of_value, inner = every(query_ref), every(value_ref), every(inner_ref)
        low = []
        for first in (0, HALF):
            places = slab_places(first, HALF)
            low.append(product(of_query.astype(BF), places(0), NT) + product(of_value.astype(BF), places(2), NT))
        rows = [low[0], low[1], inner[:, :HALF], inner[:, HALF:]]
        at = lax.broadcasted_iota(jnp.int32, (16, HALF), 0)
        piece_ref[0, 4 * QKV :] = sum(jnp.where(at == i, row, 0.0) for i, row in enumerate(rows)).astype(BF)
        for copy in started:
            copy.wait()
        c, my = scalars[0], scalars[1]
        rows = pl.ds(pl.multiple_of(my * 4 * QKV, 16), 4 * QKV)
        piece_ref[0, : 4 * QKV] = slab_ref[0, rows, pl.ds(pl.multiple_of(c * HALF, 128), HALF)]

    weights = (w_query.T, w_key.T, w_value.T, w_out)
    return pl.pallas_call(
        kernel,
        grid_spec=pltpu.PrefetchScalarGridSpec(
            num_scalar_prefetch=1,
            grid=(1,),
            in_specs=[in_hbm()] * 4 + [whole(bias.shape) for bias in biases],
            out_specs=[whole((1, 4 * heads, D)), whole((1, 4 * QKV + VECTORS, HALF))],
            scratch_shapes=[pltpu.SemaphoreType.DMA((4 * BLOCKS,))],
        ),
        out_shape=[shape_of((1, 4 * heads, D), BF), shape_of((1, 4 * QKV + VECTORS, HALF), BF)],
        compiler_params=params(58),
        cost_estimate=cost(2e9, 0),
    )(scalars, *weights, *biases)


def ffn_pieces(scalars, w_inner, w_outer):
    wide = w_inner.shape[1]
    rows = wide // BLOCKS

    def kernel(scalars, wi_hbm, wu_hbm, wt_ref, i_ref, u_ref, wi_ref, sems):
        c, my = scalars[0], scalars[1]
        block = pl.ds(pl.multiple_of(my * rows, 16), rows)
        columns = pl.ds(pl.multiple_of(c * HALF, 128), HALF)
        run_copies([(wi_hbm, wi_ref), (wu_hbm.at[block, columns], u_ref)], sems)
        wt_ref[...] = wi_ref[...].T
        i_ref[...] = wt_ref[block, columns]

    return pl.pallas_call(
        kernel,
        grid_spec=pltpu.PrefetchScalarGridSpec(
            num_scalar_prefetch=1,
            grid=(1,),
            in_specs=[in_hbm()] * 2,
            out_specs=[whole((wide, D)), whole((rows, HALF)), whole((rows, HALF))],
            scratch_shapes=[pltpu.VMEM(w_inner.shape, BF), pltpu.SemaphoreType.DMA((2,))],
        ),
        out_shape=[shape_of((wide, D), BF), shape_of((rows, HALF), BF), shape_of((rows, HALF), BF)],
        compiler_params=params(58),
        cost_estimate=cost(2e9, 0),
    )(scalars, w_inner, w_outer)


def assemble(scalars, near, far, own, rows):
    count = near.shape[1]

    def kernel(scalars, near_ref, far_ref, own_ref, out_ref, sems):
        c, my = scalars[0], scalars[1]
        copies = [(own_ref, out_ref.at[0])]
        for m in range(BLOCKS):
            for source, side in ((near_ref, c), (far_ref, 1 - c)):
                target = out_ref.at[
                    pl.ds(1, count),
                    pl.ds(pl.multiple_of((m ^ my) * rows, 16), rows),
                    pl.ds(pl.multiple_of(side * HALF, 128), HALF),
                ]
                copies.append((source.at[m, :, pl.ds(0, rows)], target))
        run_copies(copies, sems)

    shape = (1 + count, BLOCKS * rows, D)
    return pl.pallas_call(
        kernel,
        grid_spec=pltpu.PrefetchScalarGridSpec(
            num_scalar_prefetch=1,
            grid=(1,),
            in_specs=[any_place()] * 3,
            out_specs=whole(shape),
            scratch_shapes=[pltpu.SemaphoreType.DMA((2 * BLOCKS + 1,))],
        ),
        out_shape=shape_of(shape, own.dtype),
        compiler_params=params(),
        cost_estimate=cost(2e9, 0),
    )(scalars, near, far, own)


def finish(scalars, near, far, wide, narrow):
    total, base = near.shape[1], 4 * narrow

    def kernel(scalars, near_ref, far_ref, *refs):
        *outs, held, sems = refs
        c, my = scalars[0], scalars[1]
        copies = []
        for m in range(BLOCKS):
            for source, side in ((near_ref, c), (far_ref, 1 - c)):
                copies.append((source.at[m], held.at[m ^ my, :, pl.ds(pl.multiple_of(side * HALF, 128), HALF)]))
        run_copies(copies, sems)
        for kind in range(4):
            for j in range(BLOCKS):
                outs[kind][narrow * j : narrow * (j + 1)] = held[j, narrow * kind : narrow * (kind + 1)].astype(F32)
        for j in range(BLOCKS):
            at = base + VECTORS
            outs[4][wide * j : wide * (j + 1)] = held[j, at : at + wide].astype(F32)
        last = jnp.concatenate([held[j, base + VECTORS + wide :] for j in range(BLOCKS)], axis=0)
        outs[5][...] = last.astype(F32).T
        low = held[0, base : base + VECTORS, :HALF]
        vectors = low.astype(F32)
        for out, kind in zip(outs[6:8], (0, 2)):
            halves = [product(low, slab_places(first, HALF)(kind), NN) for first in (0, HALF)]
            out[...] = (halves[0][2:3] + halves[1][3:4])[0]
        for out, i in zip(outs[8:], (0, 4, 6, 8, 10, 12, 14)):
            out[...] = jnp.concatenate([vectors[i : i + 1], vectors[i + 1 : i + 2]], axis=1)[0]

    heads = BLOCKS * narrow
    shapes = [(heads, D)] * 4 + [(BLOCKS * wide, D), (D, BLOCKS * wide)] + [(heads,)] * 2 + [(D,)] * 7
    return pl.pallas_call(
        kernel,
        grid_spec=pltpu.PrefetchScalarGridSpec(
            num_scalar_prefetch=1,
            grid=(1,),
            in_specs=[any_place()] * 2,
            out_specs=[whole(shape) for shape in shapes],
            scratch_shapes=[pltpu.VMEM((BLOCKS, total, D), BF), pltpu.SemaphoreType.DMA((2 * BLOCKS,))],
        ),
        out_shape=[shape_of(shape, F32) for shape in shapes],
        compiler_params=params(),
        cost_estimate=cost(2e9, 0),
    )(scalars, near, far)


def core_add(mine, theirs):
    _, shards, rows, columns = mine.shape
    half = shards // 2

    def kernel(mine_ref, theirs_ref, own_ref, x_ref, y_ref, first_ref, second_ref):
        r = pl.program_id(0)
        total = lambda m: (mine_ref[m, 0].astype(F32) + theirs_ref[m, 0].astype(F32)).astype(BF)
        own_ref[0], x_ref[0], y_ref[0] = total(0), total(1), total(2)

        @pl.when(r < half)
        def _():
            first_ref[0] = total(3)

        @pl.when(r >= half)
        def _():
            second_ref[0] = total(3)

    blocks = pl.BlockSpec((BLOCKS, 1, rows, columns), lambda r: (0, r, 0, 0))
    block = lambda index: pl.BlockSpec((1, rows, columns), lambda r: (index(r), 0, 0))
    return pl.pallas_call(
        kernel,
        grid=(shards,),
        in_specs=[blocks, blocks],
        out_specs=[block(lambda r: r)] * 3
        + [block(lambda r: jnp.minimum(r, half - 1)), block(lambda r: jnp.maximum(r - half, 0))],
        out_shape=[shape_of((shards, rows, columns), BF)] * 3 + [shape_of((half, rows, columns), BF)] * 2,
        compiler_params=params(),
        cost_estimate=cost(1e9, 0),
    )(mine, theirs)


def plane_add(for_x, for_y, via_y, via_x):
    half, rows, columns = via_y.shape

    def kernel(x_ref, y_ref, via_y_ref, via_x_ref, x_out, y_out):
        x_out[...] = (x_ref[...].astype(F32) + via_y_ref[...].astype(F32)).astype(BF)
        y_out[...] = (y_ref[...].astype(F32) + via_x_ref[...].astype(F32)).astype(BF)

    block = lambda shift: pl.BlockSpec((1, rows, columns), lambda r: (r + shift, 0, 0))
    return pl.pallas_call(
        kernel,
        grid=(half,),
        in_specs=[block(0), block(half), block(0), block(0)],
        out_specs=[block(0), block(half)],
        out_shape=[shape_of(for_x.shape, BF)] * 2,
        input_output_aliases={0: 0, 1: 1},
        compiler_params=params(),
        cost_estimate=cost(1e9, 0),
    )(for_x, for_y, via_y, via_x)


def tie(array, *before):
    return lax.optimization_barrier((array,) + before)[0]


def build(n_dp, n_tensor):
    flip = {bit: [(i, i ^ bit) for i in range(n_dp)] for bit in (1, 2, 4, 6)}
    f32 = lambda array: array.astype(F32)
    half = n_tensor // 2

    def across(array, bit):
        return lax.ppermute(array, "dp", flip[bit])

    def along(array, r):
        return lax.ppermute(array, "tensor", [(i, i ^ r) for i in range(n_tensor)])

    def from_all(array):
        return [along(array, r) for r in range(1, n_tensor)]

    def from_all_by_steps(array):
        two = along(array, 2)
        one, three = along(jnp.stack([array, two]), 1)
        return [one, two, three]

    def plane(array):
        return [across(array, bit) for bit in (2, 4, 6)]

    def rows_round(k, up, down):
        up = lax.ppermute(up, "tensor", [(i, i + 1) for i in range(k - 1, n_tensor - 1)])
        return up, lax.ppermute(down, "tensor", [(i + 1, i) for i in range(n_tensor - k)])

    def place_rows(z, own, ups, downs):
        seq = own.shape[0]
        rows = jnp.zeros((n_tensor * seq, D), own.dtype)
        rows = lax.dynamic_update_slice(rows, own, (z * seq, 0))
        for k in (2, 1, 3):
            got = jnp.where(z >= k, ups[k - 1], downs[n_tensor - 1 - k])
            rows = lax.dynamic_update_slice(rows, got, (((z - k) & (n_tensor - 1)) * seq, 0))
        return rows

    def add(*terms):
        return sum(f32(term) for term in terms).astype(BF)

    def plane_one(diagonal_y, diagonal_x):
        return across(diagonal_y, 4), across(diagonal_x, 2)

    def plane_two(for_x, for_y):
        return across(for_x, 2), across(for_y, 4)

    def line_sums(group):
        return sum(f32(a[:half]) for a in group), add(*[a[half:] for a in group])

    def line_ends(far):
        return lax.ppermute(far, "tensor", [(0, 1), (3, 2)])

    def line_middle(far):
        return lax.ppermute(far, "tensor", [(1, 2), (2, 1)])

    def line_end(own, last):
        total = own + f32(last)
        step = 8
        while step < n_dp:
            total = total + lax.ppermute(total, "dp", [(i, i ^ step) for i in range(n_dp)])
            step *= 2
        return total.astype(BF)

    def body(
        tokens, w_query, b_query, w_key, w_value, b_value, w_attn_out, b_attn_out, gain_one, shift_one,
        w_inner, b_inner, w_outer, b_outer, gain_two, shift_two, cotangent, lengths, row_ids, col_ids,
    ):
        block = w_inner.shape[1] // BLOCKS
        index = lax.axis_index("dp")
        z = lax.axis_index("tensor")
        c, my = index & 1, (index >> 1) & 3
        scalars = jnp.stack([c, my, z]).astype(jnp.int32)
        tags = (row_ids, col_ids)
        vectors_one = f32(jnp.stack([b_attn_out, gain_one, shift_one]))
        vectors_two = f32(jnp.stack([b_outer, gain_two, shift_two]))

        slab, piece_a = attention_piece(
            scalars, w_query, w_key, w_value, w_attn_out, (b_query, b_value, b_inner)
        )
        with jax.named_scope("line attention weights"):
            line_a = from_all(piece_a)
        first = attention_forward(scalars, lengths, tokens, slab, piece_a, tags, n_tensor, 0)
        w_inner_t, piece_i, piece_u = ffn_pieces(tie(scalars, slab), w_inner, w_outer)

        with jax.named_scope("line inner weights"):
            line_i = from_all(tie(piece_i, *line_a, first[2]))
        own_a = jnp.concatenate([tie(line_a[0], piece_i, first[2])] + line_a[1:])
        with jax.named_scope("plane attention weights"):
            plane_a = plane(own_a)

        own_i = jnp.stack([tie(line_i[0], *plane_a)] + line_i[1:])
        near_a = jnp.stack([tie(own_a, *line_i), *plane_a])
        with jax.named_scope("core attention weights"):
            far_a = across(near_a, 1)
        with jax.named_scope("plane inner weights"):
            plane_i = plane(own_i)
        with jax.named_scope("line outer weights"):
            line_u = from_all(tie(piece_u, *line_i, far_a))

        w_attn = assemble(scalars, near_a, far_a, slab[0], 4 * QKV)
        qkv, heads_out, lse = attention_forward(scalars, lengths, tokens, w_attn, own_a, tags, n_tensor, 1, first)
        own_u = jnp.stack([tie(line_u[0], lse, *plane_i)] + line_u[1:])
        near_i = jnp.stack([tie(own_i, *line_u, lse), *plane_i])
        with jax.named_scope("core inner weights"):
            far_i = across(near_i, 1)
        with jax.named_scope("plane outer weights"):
            plane_u = plane(own_u)

        w_in = assemble(scalars, near_i, far_i, w_inner_t, block)
        normed, inv_spread, hidden, low, act, slope = inner_half(
            scalars, heads_out, w_attn, tokens, vectors_one, w_in, piece_a, own_a
        )
        near_u = jnp.stack([tie(own_u, inv_spread), *plane_u])
        with jax.named_scope("core outer weights"):
            far_u = across(near_u, 1)
        w_up = assemble(scalars, near_u, far_u, w_outer, block)
        out_rows, grad_two, sums_two = outer_half(scalars, act, w_up, hidden, cotangent, vectors_two)

        barrier = lambda *arrays: lax.optimization_barrier(arrays)
        with jax.named_scope("rows 1"):
            up_1, down_1 = rows_round(1, out_rows, out_rows)
        mine_u, other_u = weight_grad(scalars, act, grad_two)
        with jax.named_scope("core outer grad"):
            theirs_u = across(other_u, 1)
        partial, *carried = ffn_back(tie(grad_two, mine_u), grad_two, slope, w_up, w_in, 0, half)
        partial, theirs_u = barrier(partial, theirs_u)
        own_u, x_u, y_u, *via_u = core_add(mine_u, theirs_u)
        with jax.named_scope("plane one outer grad"):
            via_u = plane_one(*via_u)
        grad_one, grad_inner, db_inner, grad_one_low, sums_one = ffn_back(
            grad_two, tie(partial, own_u), slope, w_up, w_in, half, half, (normed, inv_spread, vectors_one), carried
        )
        grad_one, grad_inner, up_1, down_1, *via_u = barrier(grad_one, grad_inner, up_1, down_1, *via_u)
        with jax.named_scope("rows 2"):
            up_2, down_2 = rows_round(2, up_1, down_1)
        x_u, y_u = plane_add(x_u, y_u, *via_u)
        with jax.named_scope("plane two outer grad"):
            plane_u = plane_two(x_u, y_u)
        mine_i, other_i = weight_grad(scalars, tie(grad_inner, x_u), low)
        with jax.named_scope("core inner grad"):
            theirs_i = across(other_i, 1)
        vectors = (db_inner, sums_one, sums_two)
        pieces = ()

        def shard_back(start, r):
            dtype = F32 if r else BF
            return attention_backward(
                scalars, lengths, tokens, w_attn, qkv, heads_out, lse, grad_one_low, start, tags, vectors, r, dtype, pieces
            )

        start, *pieces = shard_back(tie(grad_one, mine_i), 3)
        start, theirs_i = barrier(start, theirs_i)
        own_i, x_i, y_i, *via_i = core_add(mine_i, theirs_i)
        start, *pieces = shard_back(tie(start, own_i), 2)
        start, up_2, down_2, *plane_u = barrier(start, up_2, down_2, *plane_u)
        with jax.named_scope("rows 3"):
            up_3, down_3 = rows_round(3, up_2, down_2)
        with jax.named_scope("plane one inner grad"):
            via_i = plane_one(*[tie(v, *plane_u) for v in via_i])
        near_u, far_u = line_sums((own_u, *plane_u))
        with jax.named_scope("line ends outer grad"):
            ends_u = line_ends(far_u)
        start, *pieces = shard_back(tie(start, far_u), 1)
        start, *via_i = barrier(start, *via_i)
        x_i, y_i = plane_add(x_i, y_i, *via_i)
        with jax.named_scope("plane two inner grad"):
            plane_i = plane_two(x_i, y_i)
        grad_rows, mine_a, other_a = shard_back(tie(start, x_i), 0)
        grad_rows, mine_a, other_a, ends_u, up_3, down_3 = barrier(grad_rows, mine_a, other_a, ends_u, up_3, down_3)
        far_u = add(far_u, ends_u[::-1])
        with jax.named_scope("line middle outer grad"):
            middle_u = line_middle(far_u)

        with jax.named_scope("core attention grad"):
            theirs_a = across(other_a, 1)
        with jax.named_scope("grad rows 1"):
            go_1, back_1 = rows_round(1, grad_rows, grad_rows)
        own_a, x_a, y_a, *via_a = core_add(mine_a, theirs_a)
        *via_a, middle_u, plane_i_x, plane_i_y = barrier(*via_a, middle_u, *plane_i)
        with jax.named_scope("plane one attention grad"):
            via_a = plane_one(*via_a)
        near_i, far_i = line_sums((own_i, plane_i_x, plane_i_y))
        with jax.named_scope("line ends inner grad"):
            ends_i = line_ends(far_i)
        go_1, back_1, ends_i, *via_a = barrier(go_1, back_1, ends_i, *via_a)
        with jax.named_scope("grad rows 2"):
            go_2, back_2 = rows_round(2, go_1, back_1)
        x_a, y_a = plane_add(x_a, y_a, *via_a)
        with jax.named_scope("plane two attention grad"):
            plane_a = plane_two(x_a, y_a)
        layer_out = place_rows(z, tie(out_rows, *via_a), (up_1, up_2, up_3), (down_1, down_2, down_3))
        far_i = add(far_i, ends_i[::-1])
        with jax.named_scope("line middle inner grad"):
            middle_i = line_middle(far_i)
        layer_out, _, *plane_a = barrier(layer_out, far_i, *plane_a)
        group = (own_a, *plane_a)
        low_a = [add(*[a[r] for a in group]) for r in range(1, n_tensor)]
        with jax.named_scope("line attention grad"):
            got_a = [along(a, r) for r, a in enumerate(low_a, 1)]
        near_u, near_i, go_2, back_2, *_ = barrier(near_u, near_i, go_2, back_2, *plane_a)
        near_f = [near_u + f32(middle_u[::-1]), near_i + f32(middle_i[::-1])]
        with jax.named_scope("line pair ffn grad"):
            pair_f = [along(near[1].astype(BF), 1) for near in near_f]
        pair_u, pair_i, *got_a = barrier(*pair_f, *got_a)
        own_a = sum(f32(a[0]) for a in group) + f32(got_a[0]) + f32(got_a[1])
        done = [line_end(own_a, got_a[2]), line_end(near_f[0][0], pair_u), line_end(near_f[1][0], pair_i)]
        done = jnp.concatenate(done)
        with jax.named_scope("plane result"):
            found = plane(done)
        with jax.named_scope("grad rows 3"):
            go_3, back_3 = rows_round(3, go_2, back_2)
        go_3, back_3, *found = barrier(go_3, back_3, *found)
        near = jnp.stack([done, *found])
        with jax.named_scope("core result"):
            far = across(near, 1)
        grad_tokens = place_rows(z, grad_rows, (go_1, go_2, go_3), (back_1, back_2, back_3))
        grads = finish(scalars, near, far, block, QKV)
        grad_wq, grad_wk, grad_wv, grad_wo, grad_wu, grad_wi, *vectors = grads
        grad_bq, grad_bv, grad_bi, gain_1, shift_1, b_1, gain_2, shift_2, b_2 = vectors

        return (
            layer_out,
            grad_tokens,
            grad_wq.T,
            grad_bq,
            grad_wk.T,
            grad_wv.T,
            grad_bv,
            grad_wo,
            b_1,
            gain_1,
            shift_1,
            grad_wi,
            grad_bi,
            grad_wu,
            b_2,
            gain_2,
            shift_2,
        )

    return body


def solution(mesh):
    rows, columns, out = P("dp", None), P(None, "tensor"), P("tensor", None)
    one = P("tensor")
    in_specs = (
        rows, columns, one, columns, columns, one, out, P(), P(), P(), columns, one, out, P(), P(), P(),
        rows, P("dp"), rows, rows,
    )
    out_specs = (
        rows, rows, columns, one, columns, columns, one, out, P(), P(), P(), columns, one, out, P(), P(), P(),
    )
    body = build(mesh.shape["dp"], mesh.shape["tensor"])
    return jax.shard_map(body, mesh=mesh, in_specs=in_specs, out_specs=out_specs, check_vma=False)
```

```python
import functools

import jax
import jax.numpy as jnp
from jax import lax
from jax.experimental import pallas as pl
from jax.experimental.pallas import tpu as pltpu
from jax.sharding import PartitionSpec as P

F32 = jnp.float32
BF = jnp.bfloat16
HD = 64
D = 768
HALF = D // 2
BLOCKS = 4
QKV = 48
epsilon = 1e-12
masked_value = -1e30
CHUNK = 128
SCALE = 0.05
VECTORS = 16

NN = (((1,), (0,)), ((), ()))
NT = (((1,), (1,)), ((), ()))
TN = (((0,), (0,)), ((), ()))


def product(left, right, dims):
    return lax.dot_general(left, right, dims, preferred_element_type=F32)


def shape_of(shape, dtype):
    return jax.ShapeDtypeStruct(shape, dtype)


def whole(shape):
    return pl.BlockSpec(shape, lambda r, *_: (0,) * len(shape))


def each(shape, shift=0):
    return pl.BlockSpec((1,) + shape, lambda r, *_: (r + shift,) + (0,) * len(shape))


def params(mebibytes=16):
    return pltpu.CompilerParams(vmem_limit_bytes=mebibytes * 1024 * 1024)


def cost(flops, moved, exps=0):
    return pl.CostEstimate(flops=int(flops * SCALE), bytes_accessed=int(moved * SCALE), transcendentals=int(exps))


def rows_of(ref, kind):
    width = 3 * QKV
    return jnp.concatenate(
        [ref[0, width * j + QKV * kind : width * j + QKV * (kind + 1)] for j in range(BLOCKS)], axis=0
    )


class Masks:
    def __init__(self, scalars, lengths, row_ref, col_ref):
        table = scalars[2]
        length = lengths[table]
        row_q = row_ref[pl.ds(table, 1), :].astype(F32)
        col_q = col_ref[pl.ds(table, 1), :].astype(F32)
        row_k, col_k = as_column(row_q), as_column(col_q)
        position = lax.broadcasted_iota(jnp.int32, row_k.shape, 0)
        self.here = position < length
        self.leading = position == 0
        self.row_k = jnp.where(self.here, row_k, -1.0)
        self.col_k = jnp.where(self.here, col_k, -1.0)
        self.row_q, self.col_q = row_q, col_q

    def scores(self, logits, kind):
        if kind == 0:
            visible = self.here
        elif kind == 1:
            visible = (self.row_k == self.row_q) | self.leading
        else:
            visible = (self.col_k == self.col_q) | self.leading
        return jnp.where(visible, logits, masked_value)


def as_column(row):
    return jnp.broadcast_to(row, (8, row.shape[1])).T[:, 0:1]


def projection_rows(w_ref):
    return jnp.concatenate([w_ref[0, 4 * QKV * j : 4 * QKV * j + 3 * QKV] for j in range(BLOCKS)], axis=0)


def output_rows(w_ref, shard=0):
    return jnp.concatenate(
        [w_ref[shard, 4 * QKV * j + 3 * QKV : 4 * QKV * (j + 1)] for j in range(BLOCKS)], axis=0
    )


def attention_forward_kernel(scalars, lengths, x_ref, w_ref, b_ref, row_ref, col_ref, *rest):
    qkv_ref, o_ref, lse_ref = rest[-3:]
    seq = x_ref.shape[0]
    bias = b_ref[0].astype(F32)
    bias = jnp.concatenate([bias[0:1], bias[1:2, : 3 * BLOCKS * QKV - HALF]], axis=1)
    qkv = product(projection_rows(w_ref), x_ref[...], NT) + as_column(bias)
    low = qkv.astype(BF)
    is_query = lax.broadcasted_iota(jnp.int32, (qkv.shape[0], 1), 0) % (3 * QKV) < QKV
    low = jnp.where(is_query, low * jnp.asarray(HD**-0.5, BF), low)
    qkv_ref[0] = low
    masks = Masks(scalars, lengths, row_ref, col_ref)
    q_t, k_t, v_t = rows_of(qkv_ref, 0), rows_of(qkv_ref, 1), rows_of(qkv_ref, 2)
    outs, logs = [], []
    for head in range(q_t.shape[0] // HD):
        rows = slice(HD * head, HD * (head + 1))
        scores = masks.scores(product(k_t[rows].T, q_t[rows], NN), head % 3)
        highest = jnp.max(scores, axis=0, keepdims=True)
        weights = jnp.exp(scores - highest).astype(BF)
        with_ones = jnp.concatenate([v_t[rows], jnp.ones((16, seq), BF)], axis=0)
        blended = product(with_ones, weights, NN)
        total = blended[HD : HD + 1]
        outs.append(blended[:HD] * (1.0 / total))
        logs.append(highest + jnp.log(total))
    o_ref[0] = jnp.concatenate(outs, axis=0).astype(BF)
    logs.append(jnp.zeros((8 - len(logs), seq), F32))
    lse_ref[0] = jnp.concatenate(logs, axis=0)


def in_hbm():
    return pl.BlockSpec(memory_space=pltpu.HBM)


def table_rows(seq):
    return pl.BlockSpec((seq, D), lambda r, scalars, *_: (scalars[2], 0))


def bias_rows(shift=0):
    return pl.BlockSpec((1, VECTORS, HALF), lambda r, *_: (r + shift, 4 * QKV // VECTORS, 0))


def attention_forward(scalars, lengths, tokens, weights, pieces, tags, shards, first, carried=None):
    wide, seq = 3 * BLOCKS * QKV, tags[0].shape[1]
    count, at = pieces.shape[0], first if carried else 0
    out_shape = [
        shape_of((shards, wide, seq), BF),
        shape_of((shards, wide // 3, seq), BF),
        shape_of((shards, 8, seq), F32),
    ]
    kept = list(carried) if carried else []
    return pl.pallas_call(
        attention_forward_kernel,
        grid_spec=pltpu.PrefetchScalarGridSpec(
            num_scalar_prefetch=2,
            grid=(count,),
            in_specs=[
                table_rows(seq),
                each((weights.shape[1], D), at),
                bias_rows(),
                whole(tags[0].shape),
                whole(tags[1].shape),
            ]
            + [pl.BlockSpec(memory_space=pl.ANY)] * len(kept),
            out_specs=[each(s.shape[1:], first) for s in out_shape],
        ),
        out_shape=out_shape,
        input_output_aliases={7 + i: i for i in range(len(kept))},
        compiler_params=params(),
        cost_estimate=cost(count * 3e9, count * 3e6),
    )(scalars, lengths, tokens, weights, pieces, *tags, *kept)


def attention_backward_kernel(
    scalars, lengths, x_hbm, w_hbm, qkv_hbm, o_hbm, lse_hbm, up_hbm, start_hbm, row_ref, col_ref, dbi_ref, one_ref, two_ref,
    *refs, shard, carried,
):
    dx_ref, mine_ref, other_ref, d_ref, x_ref, w_ref, qkv_ref, o_ref, lse_ref, low_ref, start_ref, sems = refs[carried:]
    seq = x_ref.shape[0]
    at = pl.ds(shard, 1)
    copies = [
        (w_hbm.at[at], w_ref),
        (up_hbm, low_ref),
        (qkv_hbm.at[at], qkv_ref),
        (o_hbm.at[at], o_ref),
        (lse_hbm.at[at], lse_ref),
        (x_hbm.at[pl.ds(pl.multiple_of(scalars[2] * seq, 128), seq)], x_ref),
        (start_hbm, start_ref),
    ]
    started = [pltpu.make_async_copy(source, target, sems.at[i]) for i, (source, target) in enumerate(copies)]
    for copy in started:
        copy.start()
    for copy in started[:5]:
        copy.wait()
    masks = Masks(scalars, lengths, row_ref, col_ref)
    q_t, k_t, v_t = rows_of(qkv_ref, 0), rows_of(qkv_ref, 1), rows_of(qkv_ref, 2)
    grad_heads = product(output_rows(w_ref), low_ref[...], NT).astype(BF)
    heads_out = o_ref[0]
    parts = [[], [], []]
    for head in range(q_t.shape[0] // HD):
        rows = slice(HD * head, HD * (head + 1))
        queries_t, keys_t, grad_t = q_t[rows], k_t[rows], grad_heads[rows]
        scores = masks.scores(product(keys_t.T, queries_t, NN), head % 3)
        chances = jnp.exp(scores - lse_ref[0, head : head + 1])
        grad_chances = product(v_t[rows].T, grad_t, NN)
        inner = jnp.sum(grad_t.astype(F32) * heads_out[rows].astype(F32), axis=0, keepdims=True)
        grad_logits = (chances * (grad_chances - inner)).astype(BF)
        parts[2].append(product(chances.astype(BF), grad_t.T, NN).T)
        parts[1].append(product(grad_logits, queries_t.T, NN).T)
        parts[0].append(product(keys_t, grad_logits, NN) * HD**-0.5)
    for kind in range(3):
        joined = jnp.concatenate(parts[kind], axis=0).astype(BF)
        for j in range(BLOCKS):
            base = 3 * QKV * j + QKV * kind
            d_ref[base : base + QKV, :] = joined[QKV * j : QKV * (j + 1)]
    grads_low = d_ref[...]
    for copy in started[5:]:
        copy.wait()
    dx_ref[...] = (start_ref[...] + product(grads_low, projection_rows(w_ref), TN)).astype(dx_ref.dtype)
    db = product(jnp.ones((8, seq), BF), grads_low, NT)[:1]
    vectors = [dbi_ref[0, :, :HALF], dbi_ref[0, :, HALF:], db[:, :HALF]]
    vectors.append(jnp.concatenate([db[:, HALF:], jnp.zeros((1, 2 * HALF - db.shape[1]), F32)], axis=1))
    for sums_ref in (one_ref, two_ref):
        for i in range(3):
            vectors += [sums_ref[i : i + 1, :HALF], sums_ref[i : i + 1, HALF:]]
    vectors = jnp.concatenate(vectors, axis=0).astype(BF)
    c, my = scalars[0], scalars[1]
    for half, out_ref in enumerate((mine_ref, other_ref)):
        start = pl.multiple_of(jnp.where(c == half, 0, HALF), 128)
        grad_w = product(grads_low, x_ref[:, pl.ds(start, HALF)], NN).astype(BF)
        grad_wo = product(heads_out, low_ref[:, pl.ds(start, HALF)], NN).astype(BF)
        for j in range(BLOCKS):
            out_ref[j ^ my, 0, : 3 * QKV] = grad_w[3 * QKV * j : 3 * QKV * (j + 1)]
            out_ref[j ^ my, 0, 3 * QKV : 4 * QKV] = grad_wo[QKV * j : QKV * (j + 1)]
            here = jnp.where(c == half, 1.0, 0.0).astype(BF) if j == 0 else jnp.zeros((), BF)
            out_ref[j ^ my, 0, 4 * QKV :] = vectors * here


def attention_backward(
    scalars, lengths, tokens, weights, qkv, heads_out, lse, upstream, start, tags, vectors, shard, dtype, carried
):
    shards, wide, seq = qkv.shape
    rows = 4 * QKV + VECTORS
    pieces = shape_of((BLOCKS, shards, rows, HALF), BF)
    piece = pl.BlockSpec((BLOCKS, 1, rows, HALF), lambda r, *_: (0, shard, 0, 0))
    return pl.pallas_call(
        functools.partial(attention_backward_kernel, shard=shard, carried=len(carried)),
        grid_spec=pltpu.PrefetchScalarGridSpec(
            num_scalar_prefetch=2,
            grid=(1,),
            in_specs=[in_hbm()] * 7
            + [whole(tags[0].shape), whole(tags[1].shape), each(vectors[0].shape[1:], shard)]
            + [whole((8, D)), whole((8, D))]
            + [in_hbm()] * len(carried),
            out_specs=[whole((seq, D)), piece, piece],
            scratch_shapes=[
                pltpu.VMEM((wide, seq), BF),
                pltpu.VMEM((seq, D), BF),
                pltpu.VMEM((1,) + weights.shape[1:], BF),
                pltpu.VMEM((1, wide, seq), BF),
                pltpu.VMEM((1, wide // 3, seq), BF),
                pltpu.VMEM((1, 8, seq), F32),
                pltpu.VMEM((seq, D), BF),
                pltpu.VMEM((seq, D), F32),
                pltpu.SemaphoreType.DMA((7,)),
            ],
        ),
        out_shape=[shape_of((seq, D), dtype), pieces, pieces],
        input_output_aliases={14 + i: 1 + i for i in range(len(carried))},
        compiler_params=params(),
        cost_estimate=cost(5e9, 5e6),
    )(scalars, lengths, tokens, weights, qkv, heads_out, lse, upstream, start, *tags, *vectors, *carried)


def gelu_pair(x):
    bell = jnp.exp(x * x * -0.5)
    t = 1.0 / (1.0 + (0.3275911 * 0.70710678118654752) * jnp.abs(x))
    series = 0.5 * 1.061405429
    for factor in (-1.453152027, 1.421413741, -0.284496736, 0.254829592):
        series = series * t + 0.5 * factor
    tail = series * t * bell
    below = jnp.where(x < 0, tail, 1.0 - tail)
    return x * below, below + x * (bell * 0.3989422804014327)


def normalize(residual):
    centre = residual - jnp.mean(residual, axis=-1, keepdims=True)
    inv_spread = lax.rsqrt(jnp.mean(centre * centre, axis=-1, keepdims=True) + epsilon)
    return centre * inv_spread, inv_spread


def norm_back(upstream, normed, inv_spread, gain):
    scaled = upstream * gain
    return inv_spread * (
        scaled
        - jnp.mean(scaled, axis=-1, keepdims=True)
        - normed * jnp.mean(scaled * normed, axis=-1, keepdims=True)
    )


def add_sums(sums, *terms):
    return [total + jnp.sum(term, axis=0, keepdims=True) for total, term in zip(sums, terms)]


def store_sums(ref, sums):
    ref[...] = jnp.concatenate(sums + [jnp.zeros((8 - len(sums), D), F32)], axis=0)


def inner_kernel(
    scalars, o_ref, wo_ref, x_ref, vec_ref, wi_ref, own_ref, others_ref,
    normed_ref, inv_ref, hidden_ref, low_ref, act_ref, slope_ref,
):
    seq, r = x_ref.shape[0], pl.program_id(0)
    bias = jnp.where(r == 0, own_ref[0].astype(F32), others_ref[jnp.maximum(r - 1, 0)].astype(F32))
    bias = jnp.concatenate([bias[2:3], bias[3:4]], axis=1)

    @pl.when(r == 0)
    def _():
        for start in range(0, seq, CHUNK):
            rows = slice(start, start + CHUNK)
            residual = vec_ref[0:1] + x_ref[rows].astype(F32)
            for shard in range(o_ref.shape[0]):
                residual = residual + product(o_ref[shard, :, rows], output_rows(wo_ref, shard), TN)
            normed, inv_spread = normalize(residual)
            hidden = normed * vec_ref[1:2] + vec_ref[2:3]
            normed_ref[rows], inv_ref[rows], hidden_ref[rows] = normed, inv_spread, hidden
            low_ref[rows] = hidden.astype(BF)

    for start in range(0, seq, CHUNK):
        rows = slice(start, start + CHUNK)
        act, slope = gelu_pair(product(low_ref[rows], wi_ref[0], NT) + bias)
        act_ref[0, rows] = act.astype(BF)
        slope_ref[0, rows] = slope.astype(BF)


def inner_half(scalars, heads_out, w_out, tokens, vectors, w_inner, own_piece, pieces):
    shards, wide, seq = w_inner.shape[0], w_inner.shape[1], heads_out.shape[2]
    return pl.pallas_call(
        inner_kernel,
        grid_spec=pltpu.PrefetchScalarGridSpec(
            num_scalar_prefetch=1,
            grid=(shards,),
            in_specs=[
                whole(heads_out.shape),
                whole(w_out.shape),
                table_rows(seq),
                whole(vectors.shape),
                each((wide, D)),
                pl.BlockSpec((1, VECTORS, HALF), lambda r, *_: (0, 4 * QKV // VECTORS, 0)),
                pl.BlockSpec((shards - 1, VECTORS, HALF), lambda r, *_: (0, 4 * QKV // VECTORS, 0)),
            ],
            out_specs=[
                whole((seq, D)),
                whole((seq, 1)),
                whole((seq, D)),
                whole((seq, D)),
                each((seq, wide)),
                each((seq, wide)),
            ],
        ),
        out_shape=[
            shape_of((seq, D), F32),
            shape_of((seq, 1), F32),
            shape_of((seq, D), F32),
            shape_of((seq, D), BF),
            shape_of((shards, seq, wide), BF),
            shape_of((shards, seq, wide), BF),
        ],
        compiler_params=params(),
        cost_estimate=cost(12e9, 20e6),
    )(scalars, heads_out, w_out, tokens, vectors, w_inner, own_piece, pieces)


def outer_kernel(scalars, act_ref, wu_ref, hidden_ref, cot_ref, vec_ref, out_ref, grad_ref, sums_ref, acc_ref):
    r, last, seq = pl.program_id(0), pl.num_programs(0) - 1, hidden_ref.shape[0]

    @pl.when(r == 0)
    def _():
        acc_ref[...] = hidden_ref[...] + vec_ref[0:1]

    acc_ref[...] = acc_ref[...] + product(act_ref[0], wu_ref[0], NN)

    @pl.when(r == last)
    def _():
        sums = [jnp.zeros((1, D), F32)] * 3
        gain = vec_ref[1:2]
        for start in range(0, seq, CHUNK):
            rows = slice(start, start + CHUNK)
            normed, inv_spread = normalize(acc_ref[rows])
            out_ref[rows] = (normed * gain + vec_ref[2:3]).astype(BF)
            upstream = cot_ref[rows].astype(F32)
            grad = norm_back(upstream, normed, inv_spread, gain)
            grad_ref[rows] = grad
            sums = add_sums(sums, upstream * normed, upstream, grad)
        store_sums(sums_ref, sums)


def outer_half(scalars, act, w_outer, hidden, cotangent, vectors):
    shards, seq, wide = act.shape
    return pl.pallas_call(
        outer_kernel,
        grid_spec=pltpu.PrefetchScalarGridSpec(
            num_scalar_prefetch=1,
            grid=(shards,),
            in_specs=[
                each((seq, wide)),
                each((wide, D)),
                whole((seq, D)),
                table_rows(seq),
                whole(vectors.shape),
            ],
            out_specs=[whole((seq, D)), whole((seq, D)), whole((8, D))],
            scratch_shapes=[pltpu.VMEM((seq, D), F32)],
        ),
        out_shape=[shape_of((seq, D), BF), shape_of((seq, D), F32), shape_of((8, D), F32)],
        compiler_params=params(),
        cost_estimate=cost(5e9, 14e6),
    )(scalars, act, w_outer, hidden, cotangent, vectors)


def ffn_back_kernel(up_ref, start_ref, slope_ref, wu_ref, wi_ref, *refs, final):
    if final:
        normed_ref, inv_ref, vec_ref, *refs = refs[:3] + refs[5:]
        grad_ref, inner_ref, db_ref, grad_low_ref, sums_ref, acc_ref, low_ref = refs
    else:
        grad_ref, inner_ref, db_ref, acc_ref, low_ref = refs
    r, last = pl.program_id(0), pl.num_programs(0) - 1
    seq, wide = up_ref.shape[0], wi_ref.shape[1]

    @pl.when(r == 0)
    def _():
        acc_ref[...] = start_ref[...]
        low_ref[...] = up_ref[...].astype(BF)

    db = jnp.zeros((1, wide), F32)
    for start in range(0, seq, CHUNK):
        rows = slice(start, start + CHUNK)
        grad_inner = product(low_ref[rows], wu_ref[0], NT) * slope_ref[0, rows].astype(F32)
        db = db + jnp.sum(grad_inner, axis=0, keepdims=True)
        inner_ref[0, rows] = grad_inner.astype(BF)
    db_ref[0] = db
    acc_ref[...] = acc_ref[...] + product(inner_ref[0], wi_ref[0], NN)

    @pl.when(r == last)
    def _():
        if not final:
            grad_ref[...] = acc_ref[...]
            return
        sums = [jnp.zeros((1, D), F32)] * 3
        for start in range(0, seq, CHUNK):
            rows = slice(start, start + CHUNK)
            upstream, normed = acc_ref[rows], normed_ref[rows]
            grad = norm_back(upstream, normed, inv_ref[rows], vec_ref[1:2])
            grad_ref[rows] = grad
            grad_low_ref[rows] = grad.astype(BF)
            sums = add_sums(sums, upstream * normed, upstream, grad)
        store_sums(sums_ref, sums)


def ffn_back(upstream, start, slope, w_outer, w_inner, first, count, norm=(), carried=()):
    shards, seq, wide = slope.shape
    final = bool(norm)
    out_specs = [whole((seq, D)), each((seq, wide), first), each((1, wide), first)]
    out_shape = [shape_of((seq, D), F32), shape_of((shards, seq, wide), BF), shape_of((shards, 1, wide), F32)]
    if final:
        out_specs += [whole((seq, D)), whole((8, D))]
        out_shape += [shape_of((seq, D), BF), shape_of((8, D), F32)]
    return pl.pallas_call(
        functools.partial(ffn_back_kernel, final=final),
        grid=(count,),
        in_specs=[
            whole((seq, D)),
            whole((seq, D)),
            each((seq, wide), first),
            each((wide, D), first),
            each((wide, D), first),
        ]
        + [whole(array.shape) for array in norm]
        + [any_place()] * len(carried),
        out_specs=out_specs,
        out_shape=out_shape,
        input_output_aliases={8 + i: 1 + i for i in range(len(carried))},
        scratch_shapes=[pltpu.VMEM((seq, D), F32), pltpu.VMEM((seq, D), BF)],
        compiler_params=params(),
        cost_estimate=cost(count * 3e9, count * 4e6),
    )(upstream, start, slope, w_outer, w_inner, *norm, *carried)


def weight_grad_kernel(scalars, left_ref, right_ref, mine_ref, other_ref, low_ref):
    @pl.when(pl.program_id(0) == 0)
    def _():
        low_ref[...] = right_ref[...].astype(BF)

    c, my = scalars[0], scalars[1]
    rows = mine_ref.shape[2]
    for half, out_ref in enumerate((mine_ref, other_ref)):
        start = pl.multiple_of(jnp.where(c == half, 0, HALF), 128)
        grad = product(left_ref[0], low_ref[:, pl.ds(start, HALF)], TN).astype(BF)
        for j in range(BLOCKS):
            out_ref[j ^ my, 0] = grad[rows * j : rows * (j + 1)]


def weight_grad(scalars, left, right):
    shards, seq, wide = left.shape
    piece = pl.BlockSpec((BLOCKS, 1, wide // BLOCKS, HALF), lambda r, *_: (0, r, 0, 0))
    pieces = shape_of((BLOCKS, shards, wide // BLOCKS, HALF), BF)
    return pl.pallas_call(
        weight_grad_kernel,
        grid_spec=pltpu.PrefetchScalarGridSpec(
            num_scalar_prefetch=1,
            grid=(shards,),
            in_specs=[each((seq, wide)), whole((seq, D))],
            out_specs=[piece, piece],
            scratch_shapes=[pltpu.VMEM((seq, D), BF)],
        ),
        out_shape=[pieces, pieces],
        compiler_params=params(),
        cost_estimate=cost(shards * 1.5e9, shards * 2e6),
    )(scalars, left, right)


def run_copies(copies, sems):
    started = [pltpu.make_async_copy(source, target, sems.at[i]) for i, (source, target) in enumerate(copies)]
    for copy in started:
        copy.start()
    for copy in started:
        copy.wait()


def any_place():
    return pl.BlockSpec(memory_space=pl.ANY)


def slab_places(first, columns):
    col = lax.broadcasted_iota(jnp.int32, (columns, BLOCKS * QKV), 0) + first
    feature = lax.broadcasted_iota(jnp.int32, (columns, BLOCKS * QKV), 1)
    block = sum((feature >= QKV * j).astype(jnp.int32) for j in range(1, BLOCKS))
    return lambda kind: (col == feature + block * 2 * QKV + QKV * kind).astype(BF)


def attention_piece(scalars, w_query, w_key, w_value, w_out, biases):
    heads = BLOCKS * QKV

    def kernel(scalars, *refs):
        w_refs, (query_ref, value_ref, inner_ref, slab_ref, piece_ref, sems) = refs[:4], refs[4:]
        copies = []
        for j in range(BLOCKS):
            for kind, w_ref in enumerate(w_refs):
                base = QKV * (4 * j + kind)
                copies.append((w_ref.at[pl.ds(QKV * j, QKV)], slab_ref.at[0, pl.ds(base, QKV)]))
        started = [pltpu.make_async_copy(source, target, sems.at[i]) for i, (source, target) in enumerate(copies)]
        for copy in started:
            copy.start()
        every = lambda ref: jnp.broadcast_to(ref[...].astype(F32).reshape(1, -1), (16, ref.shape[0]))
        of_query, of_value, inner = every(query_ref), every(value_ref), every(inner_ref)
        low = []
        for first in (0, HALF):
            places = slab_places(first, HALF)
            low.append(product(of_query.astype(BF), places(0), NT) + product(of_value.astype(BF), places(2), NT))
        rows = [low[0], low[1], inner[:, :HALF], inner[:, HALF:]]
        at = lax.broadcasted_iota(jnp.int32, (16, HALF), 0)
        piece_ref[0, 4 * QKV :] = sum(jnp.where(at == i, row, 0.0) for i, row in enumerate(rows)).astype(BF)
        for copy in started:
            copy.wait()
        c, my = scalars[0], scalars[1]
        rows = pl.ds(pl.multiple_of(my * 4 * QKV, 16), 4 * QKV)
        piece_ref[0, : 4 * QKV] = slab_ref[0, rows, pl.ds(pl.multiple_of(c * HALF, 128), HALF)]

    weights = (w_query.T, w_key.T, w_value.T, w_out)
    return pl.pallas_call(
        kernel,
        grid_spec=pltpu.PrefetchScalarGridSpec(
            num_scalar_prefetch=1,
            grid=(1,),
            in_specs=[in_hbm()] * 4 + [whole(bias.shape) for bias in biases],
            out_specs=[whole((1, 4 * heads, D)), whole((1, 4 * QKV + VECTORS, HALF))],
            scratch_shapes=[pltpu.SemaphoreType.DMA((4 * BLOCKS,))],
        ),
        out_shape=[shape_of((1, 4 * heads, D), BF), shape_of((1, 4 * QKV + VECTORS, HALF), BF)],
        compiler_params=params(58),
        cost_estimate=cost(2e9, 0),
    )(scalars, *weights, *biases)


def ffn_pieces(scalars, w_inner, w_outer):
    wide = w_inner.shape[1]
    rows = wide // BLOCKS

    def kernel(scalars, wi_hbm, wu_hbm, wt_ref, i_ref, u_ref, wi_ref, sems):
        c, my = scalars[0], scalars[1]
        block = pl.ds(pl.multiple_of(my * rows, 16), rows)
        columns = pl.ds(pl.multiple_of(c * HALF, 128), HALF)
        run_copies([(wi_hbm, wi_ref), (wu_hbm.at[block, columns], u_ref)], sems)
        wt_ref[...] = wi_ref[...].T
        i_ref[...] = wt_ref[block, columns]

    return pl.pallas_call(
        kernel,
        grid_spec=pltpu.PrefetchScalarGridSpec(
            num_scalar_prefetch=1,
            grid=(1,),
            in_specs=[in_hbm()] * 2,
            out_specs=[whole((wide, D)), whole((rows, HALF)), whole((rows, HALF))],
            scratch_shapes=[pltpu.VMEM(w_inner.shape, BF), pltpu.SemaphoreType.DMA((2,))],
        ),
        out_shape=[shape_of((wide, D), BF), shape_of((rows, HALF), BF), shape_of((rows, HALF), BF)],
        compiler_params=params(58),
        cost_estimate=cost(2e9, 0),
    )(scalars, w_inner, w_outer)


def assemble(scalars, near, far, own, rows):
    count = near.shape[1]

    def kernel(scalars, near_ref, far_ref, own_ref, out_ref, sems):
        c, my = scalars[0], scalars[1]
        copies = [(own_ref, out_ref.at[0])]
        for m in range(BLOCKS):
            for source, side in ((near_ref, c), (far_ref, 1 - c)):
                target = out_ref.at[
                    pl.ds(1, count),
                    pl.ds(pl.multiple_of((m ^ my) * rows, 16), rows),
                    pl.ds(pl.multiple_of(side * HALF, 128), HALF),
                ]
                copies.append((source.at[m, :, pl.ds(0, rows)], target))
        run_copies(copies, sems)

    shape = (1 + count, BLOCKS * rows, D)
    return pl.pallas_call(
        kernel,
        grid_spec=pltpu.PrefetchScalarGridSpec(
            num_scalar_prefetch=1,
            grid=(1,),
            in_specs=[any_place()] * 3,
            out_specs=whole(shape),
            scratch_shapes=[pltpu.SemaphoreType.DMA((2 * BLOCKS + 1,))],
        ),
        out_shape=shape_of(shape, own.dtype),
        compiler_params=params(),
        cost_estimate=cost(2e9, 0),
    )(scalars, near, far, own)


def finish(scalars, near, far, wide, narrow):
    total, base = near.shape[1], 4 * narrow

    def kernel(scalars, near_ref, far_ref, *refs):
        *outs, held, sems = refs
        c, my = scalars[0], scalars[1]
        copies = []
        for m in range(BLOCKS):
            for source, side in ((near_ref, c), (far_ref, 1 - c)):
                copies.append((source.at[m], held.at[m ^ my, :, pl.ds(pl.multiple_of(side * HALF, 128), HALF)]))
        run_copies(copies, sems)
        for kind in range(4):
            for j in range(BLOCKS):
                outs[kind][narrow * j : narrow * (j + 1)] = held[j, narrow * kind : narrow * (kind + 1)].astype(F32)
        for j in range(BLOCKS):
            at = base + VECTORS
            outs[4][wide * j : wide * (j + 1)] = held[j, at : at + wide].astype(F32)
        last = jnp.concatenate([held[j, base + VECTORS + wide :] for j in range(BLOCKS)], axis=0)
        outs[5][...] = last.astype(F32).T
        low = held[0, base : base + VECTORS, :HALF]
        vectors = low.astype(F32)
        for out, kind in zip(outs[6:8], (0, 2)):
            halves = [product(low, slab_places(first, HALF)(kind), NN) for first in (0, HALF)]
            out[...] = (halves[0][2:3] + halves[1][3:4])[0]
        for out, i in zip(outs[8:], (0, 4, 6, 8, 10, 12, 14)):
            out[...] = jnp.concatenate([vectors[i : i + 1], vectors[i + 1 : i + 2]], axis=1)[0]

    heads = BLOCKS * narrow
    shapes = [(heads, D)] * 4 + [(BLOCKS * wide, D), (D, BLOCKS * wide)] + [(heads,)] * 2 + [(D,)] * 7
    return pl.pallas_call(
        kernel,
        grid_spec=pltpu.PrefetchScalarGridSpec(
            num_scalar_prefetch=1,
            grid=(1,),
            in_specs=[any_place()] * 2,
            out_specs=[whole(shape) for shape in shapes],
            scratch_shapes=[pltpu.VMEM((BLOCKS, total, D), BF), pltpu.SemaphoreType.DMA((2 * BLOCKS,))],
        ),
        out_shape=[shape_of(shape, F32) for shape in shapes],
        compiler_params=params(),
        cost_estimate=cost(2e9, 0),
    )(scalars, near, far)


def core_add(mine, theirs):
    _, shards, rows, columns = mine.shape
    half = shards // 2

    def kernel(mine_ref, theirs_ref, own_ref, x_ref, y_ref, first_ref, second_ref):
        r = pl.program_id(0)
        total = lambda m: (mine_ref[m, 0].astype(F32) + theirs_ref[m, 0].astype(F32)).astype(BF)
        own_ref[0], x_ref[0], y_ref[0] = total(0), total(1), total(2)

        @pl.when(r < half)
        def _():
            first_ref[0] = total(3)

        @pl.when(r >= half)
        def _():
            second_ref[0] = total(3)

    blocks = pl.BlockSpec((BLOCKS, 1, rows, columns), lambda r: (0, r, 0, 0))
    block = lambda index: pl.BlockSpec((1, rows, columns), lambda r: (index(r), 0, 0))
    return pl.pallas_call(
        kernel,
        grid=(shards,),
        in_specs=[blocks, blocks],
        out_specs=[block(lambda r: r)] * 3
        + [block(lambda r: jnp.minimum(r, half - 1)), block(lambda r: jnp.maximum(r - half, 0))],
        out_shape=[shape_of((shards, rows, columns), BF)] * 3 + [shape_of((half, rows, columns), BF)] * 2,
        compiler_params=params(),
        cost_estimate=cost(1e9, 0),
    )(mine, theirs)


def plane_add(for_x, for_y, via_y, via_x):
    half, rows, columns = via_y.shape

    def kernel(x_ref, y_ref, via_y_ref, via_x_ref, x_out, y_out):
        x_out[...] = (x_ref[...].astype(F32) + via_y_ref[...].astype(F32)).astype(BF)
        y_out[...] = (y_ref[...].astype(F32) + via_x_ref[...].astype(F32)).astype(BF)

    block = lambda shift: pl.BlockSpec((1, rows, columns), lambda r: (r + shift, 0, 0))
    return pl.pallas_call(
        kernel,
        grid=(half,),
        in_specs=[block(0), block(half), block(0), block(0)],
        out_specs=[block(0), block(half)],
        out_shape=[shape_of(for_x.shape, BF)] * 2,
        input_output_aliases={0: 0, 1: 1},
        compiler_params=params(),
        cost_estimate=cost(1e9, 0),
    )(for_x, for_y, via_y, via_x)


def tie(array, *before):
    return lax.optimization_barrier((array,) + before)[0]


def build(n_dp, n_tensor):
    flip = {bit: [(i, i ^ bit) for i in range(n_dp)] for bit in (1, 2, 4, 6)}
    f32 = lambda array: array.astype(F32)
    half = n_tensor // 2

    def across(array, bit):
        return lax.ppermute(array, "dp", flip[bit])

    def along(array, r):
        return lax.ppermute(array, "tensor", [(i, i ^ r) for i in range(n_tensor)])

    def from_all(array):
        return [along(array, r) for r in range(1, n_tensor)]

    def from_all_by_steps(array):
        two = along(array, 2)
        one, three = along(jnp.stack([array, two]), 1)
        return [one, two, three]

    def plane(array):
        return [across(array, bit) for bit in (2, 4, 6)]

    def rows_round(k, up, down):
        up = lax.ppermute(up, "tensor", [(i, i + 1) for i in range(k - 1, n_tensor - 1)])
        return up, lax.ppermute(down, "tensor", [(i + 1, i) for i in range(n_tensor - k)])

    def place_rows(z, own, ups, downs):
        seq = own.shape[0]
        rows = jnp.zeros((n_tensor * seq, D), own.dtype)
        rows = lax.dynamic_update_slice(rows, own, (z * seq, 0))
        for k in (2, 1, 3):
            got = jnp.where(z >= k, ups[k - 1], downs[n_tensor - 1 - k])
            rows = lax.dynamic_update_slice(rows, got, (((z - k) & (n_tensor - 1)) * seq, 0))
        return rows

    def add(*terms):
        return sum(f32(term) for term in terms).astype(BF)

    def plane_one(diagonal_y, diagonal_x):
        return across(diagonal_y, 4), across(diagonal_x, 2)

    def plane_two(for_x, for_y):
        return across(for_x, 2), across(for_y, 4)

    def line_sums(group):
        return sum(f32(a[:half]) for a in group), add(*[a[half:] for a in group])

    def line_one(group):
        return sum(f32(a[0::2]) for a in group), add(*[a[1::2] for a in group])

    def line_ends(far):
        return lax.ppermute(far, "tensor", [(0, 1), (3, 2)])

    def line_middle(far):
        return lax.ppermute(far, "tensor", [(1, 2), (2, 1)])

    def line_end(own, last):
        total = own + f32(last)
        step = 8
        while step < n_dp:
            total = total + lax.ppermute(total, "dp", [(i, i ^ step) for i in range(n_dp)])
            step *= 2
        return total.astype(BF)

    def body(
        tokens, w_query, b_query, w_key, w_value, b_value, w_attn_out, b_attn_out, gain_one, shift_one,
        w_inner, b_inner, w_outer, b_outer, gain_two, shift_two, cotangent, lengths, row_ids, col_ids,
    ):
        block = w_inner.shape[1] // BLOCKS
        index = lax.axis_index("dp")
        z = lax.axis_index("tensor")
        c, my = index & 1, (index >> 1) & 3
        scalars = jnp.stack([c, my, z]).astype(jnp.int32)
        tags = (row_ids, col_ids)
        vectors_one = f32(jnp.stack([b_attn_out, gain_one, shift_one]))
        vectors_two = f32(jnp.stack([b_outer, gain_two, shift_two]))

        slab, piece_a = attention_piece(
            scalars, w_query, w_key, w_value, w_attn_out, (b_query, b_value, b_inner)
        )
        with jax.named_scope("line attention weights"):
            line_a = from_all(piece_a)
        first = attention_forward(scalars, lengths, tokens, slab, piece_a, tags, n_tensor, 0)
        w_inner_t, piece_i, piece_u = ffn_pieces(tie(scalars, slab), w_inner, w_outer)

        with jax.named_scope("line inner weights"):
            line_i = from_all(tie(piece_i, *line_a, first[2]))
        own_a = jnp.concatenate([tie(line_a[0], piece_i, first[2])] + line_a[1:])
        with jax.named_scope("plane attention weights"):
            plane_a = plane(own_a)

        own_i = jnp.stack([tie(line_i[0], *plane_a)] + line_i[1:])
        near_a = jnp.stack([tie(own_a, *line_i), *plane_a])
        with jax.named_scope("core attention weights"):
            far_a = across(near_a, 1)
        with jax.named_scope("plane inner weights"):
            plane_i = plane(own_i)
        with jax.named_scope("line outer weights"):
            line_u = from_all(tie(piece_u, *line_i, far_a))

        w_attn = assemble(scalars, near_a, far_a, slab[0], 4 * QKV)
        qkv, heads_out, lse = attention_forward(scalars, lengths, tokens, w_attn, own_a, tags, n_tensor, 1, first)
        own_u = jnp.stack([tie(line_u[0], lse, *plane_i)] + line_u[1:])
        near_i = jnp.stack([tie(own_i, *line_u, lse), *plane_i])
        with jax.named_scope("core inner weights"):
            far_i = across(near_i, 1)
        with jax.named_scope("plane outer weights"):
            plane_u = plane(own_u)

        w_in = assemble(scalars, near_i, far_i, w_inner_t, block)
        normed, inv_spread, hidden, low, act, slope = inner_half(
            scalars, heads_out, w_attn, tokens, vectors_one, w_in, piece_a, own_a
        )
        near_u = jnp.stack([tie(own_u, inv_spread), *plane_u])
        with jax.named_scope("core outer weights"):
            far_u = across(near_u, 1)
        w_up = assemble(scalars, near_u, far_u, w_outer, block)
        out_rows, grad_two, sums_two = outer_half(scalars, act, w_up, hidden, cotangent, vectors_two)

        barrier = lambda *arrays: lax.optimization_barrier(arrays)
        with jax.named_scope("rows 1"):
            up_1, down_1 = rows_round(1, out_rows, out_rows)
        mine_u, other_u = weight_grad(scalars, act, grad_two)
        with jax.named_scope("core outer grad"):
            theirs_u = across(other_u, 1)
        partial, *carried = ffn_back(tie(grad_two, mine_u), grad_two, slope, w_up, w_in, 0, half)
        partial, theirs_u = barrier(partial, theirs_u)
        own_u, x_u, y_u, *via_u = core_add(mine_u, theirs_u)
        with jax.named_scope("plane one outer grad"):
            via_u = plane_one(*via_u)
        grad_one, grad_inner, db_inner, grad_one_low, sums_one = ffn_back(
            grad_two, tie(partial, own_u), slope, w_up, w_in, half, half, (normed, inv_spread, vectors_one), carried
        )
        grad_one, grad_inner, up_1, down_1, *via_u = barrier(grad_one, grad_inner, up_1, down_1, *via_u)
        with jax.named_scope("rows 2"):
            up_2, down_2 = rows_round(2, up_1, down_1)
        x_u, y_u = plane_add(x_u, y_u, *via_u)
        with jax.named_scope("plane two outer grad"):
            plane_u = plane_two(x_u, y_u)
        mine_i, other_i = weight_grad(scalars, tie(grad_inner, x_u), low)
        with jax.named_scope("core inner grad"):
            theirs_i = across(other_i, 1)
        vectors = (db_inner, sums_one, sums_two)
        pieces = ()

        def shard_back(start, r):
            dtype = F32 if r else BF
            return attention_backward(
                scalars, lengths, tokens, w_attn, qkv, heads_out, lse, grad_one_low, start, tags, vectors, r, dtype, pieces
            )

        start, *pieces = shard_back(tie(grad_one, mine_i), 3)
        start, theirs_i = barrier(start, theirs_i)
        own_i, x_i, y_i, *via_i = core_add(mine_i, theirs_i)
        start, *pieces = shard_back(tie(start, own_i), 2)
        start, *plane_u = barrier(start, *plane_u)
        with jax.named_scope("plane one inner grad"):
            via_i = plane_one(*[tie(v, *plane_u) for v in via_i])
        start, up_2, down_2 = barrier(start, up_2, down_2)
        with jax.named_scope("rows 3"):
            up_3, down_3 = rows_round(3, up_2, down_2)
        start, *pieces = shard_back(start, 1)
        start, own_u, *via_i = barrier(start, own_u, *via_i)
        near_u, far_u = line_sums((own_u, *plane_u))
        with jax.named_scope("line ends outer grad"):
            ends_u = line_ends(far_u)
        x_i, y_i = plane_add(x_i, y_i, *via_i)
        with jax.named_scope("plane two inner grad"):
            plane_i = plane_two(x_i, y_i)
        grad_rows, mine_a, other_a = shard_back(tie(start, x_i, far_u), 0)
        grad_rows, mine_a, other_a, ends_u, up_3, down_3 = barrier(grad_rows, mine_a, other_a, ends_u, up_3, down_3)

        with jax.named_scope("core attention grad"):
            theirs_a = across(other_a, 1)
        with jax.named_scope("grad rows 1"):
            go_1, back_1 = rows_round(1, grad_rows, grad_rows)
        own_a, x_a, y_a, *via_a = core_add(mine_a, theirs_a)
        far_u = add(far_u, tie(ends_u, own_a)[::-1])
        with jax.named_scope("line middle outer grad"):
            middle_u = line_middle(far_u)
        *via_a, plane_i_x, plane_i_y = barrier(*via_a, *plane_i)
        with jax.named_scope("plane one attention grad"):
            via_a = plane_one(*via_a)
        even_i, odd_i = line_one((own_i, plane_i_x, plane_i_y))
        go_1, back_1, odd_i, middle_u, *via_a = barrier(go_1, back_1, odd_i, middle_u, *via_a)
        with jax.named_scope("grad rows 2"):
            go_2, back_2 = rows_round(2, go_1, back_1)
        with jax.named_scope("line one inner grad"):
            got_i = along(odd_i, 1)
        x_a, y_a = plane_add(x_a, y_a, *via_a)
        with jax.named_scope("plane two attention grad"):
            plane_a = plane_two(x_a, y_a)
        layer_out = place_rows(z, tie(out_rows, *via_a), (up_1, up_2, up_3), (down_1, down_2, down_3))
        near_u = near_u + f32(middle_u[::-1])
        layer_out, got_i, *plane_a = barrier(layer_out, got_i, *plane_a)
        group = (own_a, *plane_a)
        low_a = [add(*[a[r] for a in group]) for r in range(1, n_tensor)]
        with jax.named_scope("line attention grad"):
            got_a = [along(a, r) for r, a in enumerate(low_a, 1)]
        even_i, near_u, go_2, back_2, *_ = barrier(even_i, near_u, go_2, back_2, *plane_a)
        even_i = even_i + f32(got_i)
        with jax.named_scope("line two inner grad"):
            last_i = along(even_i[1].astype(BF), 2)
        with jax.named_scope("line pair outer grad"):
            pair_u = along(near_u[1].astype(BF), 1)
        last_i, pair_u, *got_a = barrier(last_i, pair_u, *got_a)
        own_a = sum(f32(a[0]) for a in group) + f32(got_a[0]) + f32(got_a[1])
        done = jnp.concatenate(
            [line_end(own_a, got_a[2]), line_end(near_u[0], pair_u), line_end(even_i[0], last_i)]
        )
        with jax.named_scope("plane result"):
            found = plane(done)
        with jax.named_scope("grad rows 3"):
            go_3, back_3 = rows_round(3, go_2, back_2)
        go_3, back_3, *found = barrier(go_3, back_3, *found)
        near = jnp.stack([done, *found])
        with jax.named_scope("core result"):
            far = across(near, 1)
        grad_tokens = place_rows(z, grad_rows, (go_1, go_2, go_3), (back_1, back_2, back_3))
        grads = finish(scalars, near, far, block, QKV)
        grad_wq, grad_wk, grad_wv, grad_wo, grad_wu, grad_wi, *vectors = grads
        grad_bq, grad_bv, grad_bi, gain_1, shift_1, b_1, gain_2, shift_2, b_2 = vectors

        return (
            layer_out,
            grad_tokens,
            grad_wq.T,
            grad_bq,
            grad_wk.T,
            grad_wv.T,
            grad_bv,
            grad_wo,
            b_1,
            gain_1,
            shift_1,
            grad_wi,
            grad_bi,
            grad_wu,
            b_2,
            gain_2,
            shift_2,
        )

    return body


def solution(mesh):
    rows, columns, out = P("dp", None), P(None, "tensor"), P("tensor", None)
    one = P("tensor")
    in_specs = (
        rows, columns, one, columns, columns, one, out, P(), P(), P(), columns, one, out, P(), P(), P(),
        rows, P("dp"), rows, rows,
    )
    out_specs = (
        rows, rows, columns, one, columns, columns, one, out, P(), P(), P(), columns, one, out, P(), P(), P(),
    )
    body = build(mesh.shape["dp"], mesh.shape["tensor"])
    return jax.shard_map(body, mesh=mesh, in_specs=in_specs, out_specs=out_specs, check_vma=False)
```

```python
import functools

import jax
import jax.numpy as jnp
from jax import lax
from jax.experimental import pallas as pl
from jax.experimental.pallas import tpu as pltpu
from jax.sharding import PartitionSpec as P

F32 = jnp.float32
BF = jnp.bfloat16
HD = 64
D = 768
HALF = D // 2
BLOCKS = 4
QKV = 48
epsilon = 1e-12
masked_value = -1e30
CHUNK = 128
SCALE = 0.05
VECTORS = 16

NN = (((1,), (0,)), ((), ()))
NT = (((1,), (1,)), ((), ()))
TN = (((0,), (0,)), ((), ()))


def product(left, right, dims):
    return lax.dot_general(left, right, dims, preferred_element_type=F32)


def shape_of(shape, dtype):
    return jax.ShapeDtypeStruct(shape, dtype)


def whole(shape):
    return pl.BlockSpec(shape, lambda r, *_: (0,) * len(shape))


def each(shape, shift=0):
    return pl.BlockSpec((1,) + shape, lambda r, *_: (r + shift,) + (0,) * len(shape))


def params(mebibytes=16):
    return pltpu.CompilerParams(vmem_limit_bytes=mebibytes * 1024 * 1024)


def cost(flops, moved, exps=0):
    return pl.CostEstimate(flops=int(flops * SCALE), bytes_accessed=int(moved * SCALE), transcendentals=int(exps))


def rows_of(ref, kind):
    width = 3 * QKV
    return jnp.concatenate(
        [ref[0, width * j + QKV * kind : width * j + QKV * (kind + 1)] for j in range(BLOCKS)], axis=0
    )


class Masks:
    def __init__(self, scalars, lengths, row_ref, col_ref):
        table = scalars[2]
        length = lengths[table]
        row_q = row_ref[pl.ds(table, 1), :].astype(F32)
        col_q = col_ref[pl.ds(table, 1), :].astype(F32)
        row_k, col_k = as_column(row_q), as_column(col_q)
        position = lax.broadcasted_iota(jnp.int32, row_k.shape, 0)
        self.here = position < length
        self.leading = position == 0
        self.row_k = jnp.where(self.here, row_k, -1.0)
        self.col_k = jnp.where(self.here, col_k, -1.0)
        self.row_q, self.col_q = row_q, col_q

    def scores(self, logits, kind):
        if kind == 0:
            visible = self.here
        elif kind == 1:
            visible = (self.row_k == self.row_q) | self.leading
        else:
            visible = (self.col_k == self.col_q) | self.leading
        return jnp.where(visible, logits, masked_value)


def as_column(row):
    return jnp.broadcast_to(row, (8, row.shape[1])).T[:, 0:1]


def projection_rows(w_ref):
    return jnp.concatenate([w_ref[0, 4 * QKV * j : 4 * QKV * j + 3 * QKV] for j in range(BLOCKS)], axis=0)


def output_rows(w_ref, shard=0):
    return jnp.concatenate(
        [w_ref[shard, 4 * QKV * j + 3 * QKV : 4 * QKV * (j + 1)] for j in range(BLOCKS)], axis=0
    )


def attention_forward_kernel(scalars, lengths, x_ref, w_ref, b_ref, row_ref, col_ref, *rest):
    qkv_ref, o_ref, lse_ref = rest[-3:]
    seq = x_ref.shape[0]
    bias = b_ref[0].astype(F32)
    bias = jnp.concatenate([bias[0:1], bias[1:2, : 3 * BLOCKS * QKV - HALF]], axis=1)
    qkv = product(projection_rows(w_ref), x_ref[...], NT) + as_column(bias)
    low = qkv.astype(BF)
    is_query = lax.broadcasted_iota(jnp.int32, (qkv.shape[0], 1), 0) % (3 * QKV) < QKV
    low = jnp.where(is_query, low * jnp.asarray(HD**-0.5, BF), low)
    qkv_ref[0] = low
    masks = Masks(scalars, lengths, row_ref, col_ref)
    q_t, k_t, v_t = rows_of(qkv_ref, 0), rows_of(qkv_ref, 1), rows_of(qkv_ref, 2)
    outs, logs = [], []
    for head in range(q_t.shape[0] // HD):
        rows = slice(HD * head, HD * (head + 1))
        scores = masks.scores(product(k_t[rows].T, q_t[rows], NN), head % 3)
        highest = jnp.max(scores, axis=0, keepdims=True)
        weights = jnp.exp(scores - highest).astype(BF)
        with_ones = jnp.concatenate([v_t[rows], jnp.ones((16, seq), BF)], axis=0)
        blended = product(with_ones, weights, NN)
        total = blended[HD : HD + 1]
        outs.append(blended[:HD] * (1.0 / total))
        logs.append(highest + jnp.log(total))
    o_ref[0] = jnp.concatenate(outs, axis=0).astype(BF)
    logs.append(jnp.zeros((8 - len(logs), seq), F32))
    lse_ref[0] = jnp.concatenate(logs, axis=0)


def in_hbm():
    return pl.BlockSpec(memory_space=pltpu.HBM)


def table_rows(seq):
    return pl.BlockSpec((seq, D), lambda r, scalars, *_: (scalars[2], 0))


def bias_rows(shift=0):
    return pl.BlockSpec((1, VECTORS, HALF), lambda r, *_: (r + shift, 4 * QKV // VECTORS, 0))


def attention_forward(scalars, lengths, tokens, weights, pieces, tags, shards, first, carried=None):
    wide, seq = 3 * BLOCKS * QKV, tags[0].shape[1]
    count, at = pieces.shape[0], first if carried else 0
    out_shape = [
        shape_of((shards, wide, seq), BF),
        shape_of((shards, wide // 3, seq), BF),
        shape_of((shards, 8, seq), F32),
    ]
    kept = list(carried) if carried else []
    return pl.pallas_call(
        attention_forward_kernel,
        grid_spec=pltpu.PrefetchScalarGridSpec(
            num_scalar_prefetch=2,
            grid=(count,),
            in_specs=[
                table_rows(seq),
                each((weights.shape[1], D), at),
                bias_rows(),
                whole(tags[0].shape),
                whole(tags[1].shape),
            ]
            + [pl.BlockSpec(memory_space=pl.ANY)] * len(kept),
            out_specs=[each(s.shape[1:], first) for s in out_shape],
        ),
        out_shape=out_shape,
        input_output_aliases={7 + i: i for i in range(len(kept))},
        compiler_params=params(),
        cost_estimate=cost(count * 3e9, count * 3e6),
    )(scalars, lengths, tokens, weights, pieces, *tags, *kept)


def attention_backward_kernel(
    scalars, lengths, x_hbm, w_hbm, qkv_hbm, o_hbm, lse_hbm, up_hbm, start_hbm, row_ref, col_ref, dbi_ref, one_ref, two_ref,
    *refs, shard, carried,
):
    dx_ref, mine_ref, other_ref, d_ref, x_ref, w_ref, qkv_ref, o_ref, lse_ref, low_ref, start_ref, sems = refs[carried:]
    seq = x_ref.shape[0]
    at = pl.ds(shard, 1)
    copies = [
        (w_hbm.at[at], w_ref),
        (up_hbm, low_ref),
        (qkv_hbm.at[at], qkv_ref),
        (o_hbm.at[at], o_ref),
        (lse_hbm.at[at], lse_ref),
        (x_hbm.at[pl.ds(pl.multiple_of(scalars[2] * seq, 128), seq)], x_ref),
        (start_hbm, start_ref),
    ]
    started = [pltpu.make_async_copy(source, target, sems.at[i]) for i, (source, target) in enumerate(copies)]
    for copy in started:
        copy.start()
    for copy in started[:5]:
        copy.wait()
    masks = Masks(scalars, lengths, row_ref, col_ref)
    q_t, k_t, v_t = rows_of(qkv_ref, 0), rows_of(qkv_ref, 1), rows_of(qkv_ref, 2)
    grad_heads = product(output_rows(w_ref), low_ref[...], NT).astype(BF)
    heads_out = o_ref[0]
    parts = [[], [], []]
    for head in range(q_t.shape[0] // HD):
        rows = slice(HD * head, HD * (head + 1))
        queries_t, keys_t, grad_t = q_t[rows], k_t[rows], grad_heads[rows]
        scores = masks.scores(product(keys_t.T, queries_t, NN), head % 3)
        chances = jnp.exp(scores - lse_ref[0, head : head + 1])
        grad_chances = product(v_t[rows].T, grad_t, NN)
        inner = jnp.sum(grad_t.astype(F32) * heads_out[rows].astype(F32), axis=0, keepdims=True)
        grad_logits = (chances * (grad_chances - inner)).astype(BF)
        parts[2].append(product(chances.astype(BF), grad_t.T, NN).T)
        parts[1].append(product(grad_logits, queries_t.T, NN).T)
        parts[0].append(product(keys_t, grad_logits, NN) * HD**-0.5)
    for kind in range(3):
        joined = jnp.concatenate(parts[kind], axis=0).astype(BF)
        for j in range(BLOCKS):
            base = 3 * QKV * j + QKV * kind
            d_ref[base : base + QKV, :] = joined[QKV * j : QKV * (j + 1)]
    grads_low = d_ref[...]
    for copy in started[5:]:
        copy.wait()
    dx_ref[...] = (start_ref[...] + product(grads_low, projection_rows(w_ref), TN)).astype(dx_ref.dtype)
    db = product(jnp.ones((8, seq), BF), grads_low, NT)[:1]
    vectors = [dbi_ref[0, :, :HALF], dbi_ref[0, :, HALF:], db[:, :HALF]]
    vectors.append(jnp.concatenate([db[:, HALF:], jnp.zeros((1, 2 * HALF - db.shape[1]), F32)], axis=1))
    for sums_ref in (one_ref, two_ref):
        for i in range(3):
            vectors += [sums_ref[i : i + 1, :HALF], sums_ref[i : i + 1, HALF:]]
    vectors = jnp.concatenate(vectors, axis=0).astype(BF)
    c, my = scalars[0], scalars[1]
    for half, out_ref in enumerate((mine_ref, other_ref)):
        start = pl.multiple_of(jnp.where(c == half, 0, HALF), 128)
        grad_w = product(grads_low, x_ref[:, pl.ds(start, HALF)], NN).astype(BF)
        grad_wo = product(heads_out, low_ref[:, pl.ds(start, HALF)], NN).astype(BF)
        for j in range(BLOCKS):
            out_ref[j ^ my, 0, : 3 * QKV] = grad_w[3 * QKV * j : 3 * QKV * (j + 1)]
            out_ref[j ^ my, 0, 3 * QKV : 4 * QKV] = grad_wo[QKV * j : QKV * (j + 1)]
            here = jnp.where(c == half, 1.0, 0.0).astype(BF) if j == 0 else jnp.zeros((), BF)
            out_ref[j ^ my, 0, 4 * QKV :] = vectors * here


def attention_backward(
    scalars, lengths, tokens, weights, qkv, heads_out, lse, upstream, start, tags, vectors, shard, dtype, carried
):
    shards, wide, seq = qkv.shape
    rows = 4 * QKV + VECTORS
    pieces = shape_of((BLOCKS, shards, rows, HALF), BF)
    piece = pl.BlockSpec((BLOCKS, 1, rows, HALF), lambda r, *_: (0, shard, 0, 0))
    return pl.pallas_call(
        functools.partial(attention_backward_kernel, shard=shard, carried=len(carried)),
        grid_spec=pltpu.PrefetchScalarGridSpec(
            num_scalar_prefetch=2,
            grid=(1,),
            in_specs=[in_hbm()] * 7
            + [whole(tags[0].shape), whole(tags[1].shape), each(vectors[0].shape[1:], shard)]
            + [whole((8, D)), whole((8, D))]
            + [in_hbm()] * len(carried),
            out_specs=[whole((seq, D)), piece, piece],
            scratch_shapes=[
                pltpu.VMEM((wide, seq), BF),
                pltpu.VMEM((seq, D), BF),
                pltpu.VMEM((1,) + weights.shape[1:], BF),
                pltpu.VMEM((1, wide, seq), BF),
                pltpu.VMEM((1, wide // 3, seq), BF),
                pltpu.VMEM((1, 8, seq), F32),
                pltpu.VMEM((seq, D), BF),
                pltpu.VMEM((seq, D), F32),
                pltpu.SemaphoreType.DMA((7,)),
            ],
        ),
        out_shape=[shape_of((seq, D), dtype), pieces, pieces],
        input_output_aliases={14 + i: 1 + i for i in range(len(carried))},
        compiler_params=params(),
        cost_estimate=cost(5e9, 5e6),
    )(scalars, lengths, tokens, weights, qkv, heads_out, lse, upstream, start, *tags, *vectors, *carried)


def gelu_pair(x):
    bell = jnp.exp(x * x * -0.5)
    t = 1.0 / (1.0 + (0.3275911 * 0.70710678118654752) * jnp.abs(x))
    series = 0.5 * 1.061405429
    for factor in (-1.453152027, 1.421413741, -0.284496736, 0.254829592):
        series = series * t + 0.5 * factor
    tail = series * t * bell
    below = jnp.where(x < 0, tail, 1.0 - tail)
    return x * below, below + x * (bell * 0.3989422804014327)


def normalize(residual):
    centre = residual - jnp.mean(residual, axis=-1, keepdims=True)
    inv_spread = lax.rsqrt(jnp.mean(centre * centre, axis=-1, keepdims=True) + epsilon)
    return centre * inv_spread, inv_spread


def norm_back(upstream, normed, inv_spread, gain):
    scaled = upstream * gain
    return inv_spread * (
        scaled
        - jnp.mean(scaled, axis=-1, keepdims=True)
        - normed * jnp.mean(scaled * normed, axis=-1, keepdims=True)
    )


def add_sums(sums, *terms):
    return [total + jnp.sum(term, axis=0, keepdims=True) for total, term in zip(sums, terms)]


def store_sums(ref, sums):
    ref[...] = jnp.concatenate(sums + [jnp.zeros((8 - len(sums), D), F32)], axis=0)


def inner_kernel(
    scalars, o_ref, wo_ref, x_ref, vec_ref, wi_ref, own_ref, others_ref,
    normed_ref, inv_ref, hidden_ref, low_ref, act_ref, slope_ref,
):
    seq, r = x_ref.shape[0], pl.program_id(0)
    bias = jnp.where(r == 0, own_ref[0].astype(F32), others_ref[jnp.maximum(r - 1, 0)].astype(F32))
    bias = jnp.concatenate([bias[2:3], bias[3:4]], axis=1)

    @pl.when(r == 0)
    def _():
        for start in range(0, seq, CHUNK):
            rows = slice(start, start + CHUNK)
            residual = vec_ref[0:1] + x_ref[rows].astype(F32)
            for shard in range(o_ref.shape[0]):
                residual = residual + product(o_ref[shard, :, rows], output_rows(wo_ref, shard), TN)
            normed, inv_spread = normalize(residual)
            hidden = normed * vec_ref[1:2] + vec_ref[2:3]
            normed_ref[rows], inv_ref[rows], hidden_ref[rows] = normed, inv_spread, hidden
            low_ref[rows] = hidden.astype(BF)

    for start in range(0, seq, CHUNK):
        rows = slice(start, start + CHUNK)
        act, slope = gelu_pair(product(low_ref[rows], wi_ref[0], NT) + bias)
        act_ref[0, rows] = act.astype(BF)
        slope_ref[0, rows] = slope.astype(BF)


def inner_half(scalars, heads_out, w_out, tokens, vectors, w_inner, own_piece, pieces):
    shards, wide, seq = w_inner.shape[0], w_inner.shape[1], heads_out.shape[2]
    return pl.pallas_call(
        inner_kernel,
        grid_spec=pltpu.PrefetchScalarGridSpec(
            num_scalar_prefetch=1,
            grid=(shards,),
            in_specs=[
                whole(heads_out.shape),
                whole(w_out.shape),
                table_rows(seq),
                whole(vectors.shape),
                each((wide, D)),
                pl.BlockSpec((1, VECTORS, HALF), lambda r, *_: (0, 4 * QKV // VECTORS, 0)),
                pl.BlockSpec((shards - 1, VECTORS, HALF), lambda r, *_: (0, 4 * QKV // VECTORS, 0)),
            ],
            out_specs=[
                whole((seq, D)),
                whole((seq, 1)),
                whole((seq, D)),
                whole((seq, D)),
                each((seq, wide)),
                each((seq, wide)),
            ],
        ),
        out_shape=[
            shape_of((seq, D), F32),
            shape_of((seq, 1), F32),
            shape_of((seq, D), F32),
            shape_of((seq, D), BF),
            shape_of((shards, seq, wide), BF),
            shape_of((shards, seq, wide), BF),
        ],
        compiler_params=params(),
        cost_estimate=cost(12e9, 20e6),
    )(scalars, heads_out, w_out, tokens, vectors, w_inner, own_piece, pieces)


def outer_kernel(scalars, act_ref, wu_ref, hidden_ref, cot_ref, vec_ref, out_ref, grad_ref, sums_ref, acc_ref):
    r, last, seq = pl.program_id(0), pl.num_programs(0) - 1, hidden_ref.shape[0]

    @pl.when(r == 0)
    def _():
        acc_ref[...] = hidden_ref[...] + vec_ref[0:1]

    acc_ref[...] = acc_ref[...] + product(act_ref[0], wu_ref[0], NN)

    @pl.when(r == last)
    def _():
        sums = [jnp.zeros((1, D), F32)] * 3
        gain = vec_ref[1:2]
        for start in range(0, seq, CHUNK):
            rows = slice(start, start + CHUNK)
            normed, inv_spread = normalize(acc_ref[rows])
            out_ref[rows] = (normed * gain + vec_ref[2:3]).astype(BF)
            upstream = cot_ref[rows].astype(F32)
            grad = norm_back(upstream, normed, inv_spread, gain)
            grad_ref[rows] = grad
            sums = add_sums(sums, upstream * normed, upstream, grad)
        store_sums(sums_ref, sums)


def outer_half(scalars, act, w_outer, hidden, cotangent, vectors):
    shards, seq, wide = act.shape
    return pl.pallas_call(
        outer_kernel,
        grid_spec=pltpu.PrefetchScalarGridSpec(
            num_scalar_prefetch=1,
            grid=(shards,),
            in_specs=[
                each((seq, wide)),
                each((wide, D)),
                whole((seq, D)),
                table_rows(seq),
                whole(vectors.shape),
            ],
            out_specs=[whole((seq, D)), whole((seq, D)), whole((8, D))],
            scratch_shapes=[pltpu.VMEM((seq, D), F32)],
        ),
        out_shape=[shape_of((seq, D), BF), shape_of((seq, D), F32), shape_of((8, D), F32)],
        compiler_params=params(),
        cost_estimate=cost(5e9, 14e6),
    )(scalars, act, w_outer, hidden, cotangent, vectors)


def ffn_back_kernel(up_ref, start_ref, slope_ref, wu_ref, wi_ref, *refs, final):
    if final:
        normed_ref, inv_ref, vec_ref, *refs = refs[:3] + refs[5:]
        grad_ref, inner_ref, db_ref, grad_low_ref, sums_ref, acc_ref, low_ref = refs
    else:
        grad_ref, inner_ref, db_ref, acc_ref, low_ref = refs
    r, last = pl.program_id(0), pl.num_programs(0) - 1
    seq, wide = up_ref.shape[0], wi_ref.shape[1]

    @pl.when(r == 0)
    def _():
        acc_ref[...] = start_ref[...]
        low_ref[...] = up_ref[...].astype(BF)

    db = jnp.zeros((1, wide), F32)
    for start in range(0, seq, CHUNK):
        rows = slice(start, start + CHUNK)
        grad_inner = product(low_ref[rows], wu_ref[0], NT) * slope_ref[0, rows].astype(F32)
        db = db + jnp.sum(grad_inner, axis=0, keepdims=True)
        inner_ref[0, rows] = grad_inner.astype(BF)
    db_ref[0] = db
    acc_ref[...] = acc_ref[...] + product(inner_ref[0], wi_ref[0], NN)

    @pl.when(r == last)
    def _():
        if not final:
            grad_ref[...] = acc_ref[...]
            return
        sums = [jnp.zeros((1, D), F32)] * 3
        for start in range(0, seq, CHUNK):
            rows = slice(start, start + CHUNK)
            upstream, normed = acc_ref[rows], normed_ref[rows]
            grad = norm_back(upstream, normed, inv_ref[rows], vec_ref[1:2])
            grad_ref[rows] = grad
            grad_low_ref[rows] = grad.astype(BF)
            sums = add_sums(sums, upstream * normed, upstream, grad)
        store_sums(sums_ref, sums)


def ffn_back(upstream, start, slope, w_outer, w_inner, first, count, norm=(), carried=()):
    shards, seq, wide = slope.shape
    final = bool(norm)
    out_specs = [whole((seq, D)), each((seq, wide), first), each((1, wide), first)]
    out_shape = [shape_of((seq, D), F32), shape_of((shards, seq, wide), BF), shape_of((shards, 1, wide), F32)]
    if final:
        out_specs += [whole((seq, D)), whole((8, D))]
        out_shape += [shape_of((seq, D), BF), shape_of((8, D), F32)]
    return pl.pallas_call(
        functools.partial(ffn_back_kernel, final=final),
        grid=(count,),
        in_specs=[
            whole((seq, D)),
            whole((seq, D)),
            each((seq, wide), first),
            each((wide, D), first),
            each((wide, D), first),
        ]
        + [whole(array.shape) for array in norm]
        + [any_place()] * len(carried),
        out_specs=out_specs,
        out_shape=out_shape,
        input_output_aliases={8 + i: 1 + i for i in range(len(carried))},
        scratch_shapes=[pltpu.VMEM((seq, D), F32), pltpu.VMEM((seq, D), BF)],
        compiler_params=params(),
        cost_estimate=cost(count * 3e9, count * 4e6),
    )(upstream, start, slope, w_outer, w_inner, *norm, *carried)


def weight_grad_kernel(scalars, left_ref, right_ref, mine_ref, other_ref, low_ref):
    @pl.when(pl.program_id(0) == 0)
    def _():
        low_ref[...] = right_ref[...].astype(BF)

    c, my = scalars[0], scalars[1]
    rows = mine_ref.shape[2]
    for half, out_ref in enumerate((mine_ref, other_ref)):
        start = pl.multiple_of(jnp.where(c == half, 0, HALF), 128)
        grad = product(left_ref[0], low_ref[:, pl.ds(start, HALF)], TN).astype(BF)
        for j in range(BLOCKS):
            out_ref[j ^ my, 0] = grad[rows * j : rows * (j + 1)]


def weight_grad(scalars, left, right):
    shards, seq, wide = left.shape
    piece = pl.BlockSpec((BLOCKS, 1, wide // BLOCKS, HALF), lambda r, *_: (0, r, 0, 0))
    pieces = shape_of((BLOCKS, shards, wide // BLOCKS, HALF), BF)
    return pl.pallas_call(
        weight_grad_kernel,
        grid_spec=pltpu.PrefetchScalarGridSpec(
            num_scalar_prefetch=1,
            grid=(shards,),
            in_specs=[each((seq, wide)), whole((seq, D))],
            out_specs=[piece, piece],
            scratch_shapes=[pltpu.VMEM((seq, D), BF)],
        ),
        out_shape=[pieces, pieces],
        compiler_params=params(),
        cost_estimate=cost(shards * 1.5e9, shards * 2e6),
    )(scalars, left, right)


def run_copies(copies, sems):
    started = [pltpu.make_async_copy(source, target, sems.at[i]) for i, (source, target) in enumerate(copies)]
    for copy in started:
        copy.start()
    for copy in started:
        copy.wait()


def any_place():
    return pl.BlockSpec(memory_space=pl.ANY)


def slab_places(first, columns):
    col = lax.broadcasted_iota(jnp.int32, (columns, BLOCKS * QKV), 0) + first
    feature = lax.broadcasted_iota(jnp.int32, (columns, BLOCKS * QKV), 1)
    block = sum((feature >= QKV * j).astype(jnp.int32) for j in range(1, BLOCKS))
    return lambda kind: (col == feature + block * 2 * QKV + QKV * kind).astype(BF)


def attention_piece(scalars, w_query, w_key, w_value, w_out, biases):
    heads = BLOCKS * QKV

    def kernel(scalars, *refs):
        w_refs, (query_ref, value_ref, inner_ref, slab_ref, piece_ref, sems) = refs[:4], refs[4:]
        copies = []
        for j in range(BLOCKS):
            for kind, w_ref in enumerate(w_refs):
                base = QKV * (4 * j + kind)
                copies.append((w_ref.at[pl.ds(QKV * j, QKV)], slab_ref.at[0, pl.ds(base, QKV)]))
        started = [pltpu.make_async_copy(source, target, sems.at[i]) for i, (source, target) in enumerate(copies)]
        for copy in started:
            copy.start()
        every = lambda ref: jnp.broadcast_to(ref[...].astype(F32).reshape(1, -1), (16, ref.shape[0]))
        of_query, of_value, inner = every(query_ref), every(value_ref), every(inner_ref)
        low = []
        for first in (0, HALF):
            places = slab_places(first, HALF)
            low.append(product(of_query.astype(BF), places(0), NT) + product(of_value.astype(BF), places(2), NT))
        rows = [low[0], low[1], inner[:, :HALF], inner[:, HALF:]]
        at = lax.broadcasted_iota(jnp.int32, (16, HALF), 0)
        piece_ref[0, 4 * QKV :] = sum(jnp.where(at == i, row, 0.0) for i, row in enumerate(rows)).astype(BF)
        for copy in started:
            copy.wait()
        c, my = scalars[0], scalars[1]
        rows = pl.ds(pl.multiple_of(my * 4 * QKV, 16), 4 * QKV)
        piece_ref[0, : 4 * QKV] = slab_ref[0, rows, pl.ds(pl.multiple_of(c * HALF, 128), HALF)]

    weights = (w_query.T, w_key.T, w_value.T, w_out)
    return pl.pallas_call(
        kernel,
        grid_spec=pltpu.PrefetchScalarGridSpec(
            num_scalar_prefetch=1,
            grid=(1,),
            in_specs=[in_hbm()] * 4 + [whole(bias.shape) for bias in biases],
            out_specs=[whole((1, 4 * heads, D)), whole((1, 4 * QKV + VECTORS, HALF))],
            scratch_shapes=[pltpu.SemaphoreType.DMA((4 * BLOCKS,))],
        ),
        out_shape=[shape_of((1, 4 * heads, D), BF), shape_of((1, 4 * QKV + VECTORS, HALF), BF)],
        compiler_params=params(58),
        cost_estimate=cost(2e9, 0),
    )(scalars, *weights, *biases)


def ffn_pieces(scalars, w_inner, w_outer):
    wide = w_inner.shape[1]
    rows = wide // BLOCKS

    def kernel(scalars, wi_hbm, wu_hbm, wt_ref, i_ref, u_ref, wi_ref, sems):
        c, my = scalars[0], scalars[1]
        block = pl.ds(pl.multiple_of(my * rows, 16), rows)
        columns = pl.ds(pl.multiple_of(c * HALF, 128), HALF)
        run_copies([(wi_hbm, wi_ref), (wu_hbm.at[block, columns], u_ref)], sems)
        wt_ref[...] = wi_ref[...].T
        i_ref[...] = wt_ref[block, columns]

    return pl.pallas_call(
        kernel,
        grid_spec=pltpu.PrefetchScalarGridSpec(
            num_scalar_prefetch=1,
            grid=(1,),
            in_specs=[in_hbm()] * 2,
            out_specs=[whole((wide, D)), whole((rows, HALF)), whole((rows, HALF))],
            scratch_shapes=[pltpu.VMEM(w_inner.shape, BF), pltpu.SemaphoreType.DMA((2,))],
        ),
        out_shape=[shape_of((wide, D), BF), shape_of((rows, HALF), BF), shape_of((rows, HALF), BF)],
        compiler_params=params(58),
        cost_estimate=cost(2e9, 0),
    )(scalars, w_inner, w_outer)


def assemble(scalars, near, far, own, rows):
    count = near.shape[1]

    def kernel(scalars, near_ref, far_ref, own_ref, out_ref, sems):
        c, my = scalars[0], scalars[1]
        copies = [(own_ref, out_ref.at[0])]
        for m in range(BLOCKS):
            for source, side in ((near_ref, c), (far_ref, 1 - c)):
                target = out_ref.at[
                    pl.ds(1, count),
                    pl.ds(pl.multiple_of((m ^ my) * rows, 16), rows),
                    pl.ds(pl.multiple_of(side * HALF, 128), HALF),
                ]
                copies.append((source.at[m, :, pl.ds(0, rows)], target))
        run_copies(copies, sems)

    shape = (1 + count, BLOCKS * rows, D)
    return pl.pallas_call(
        kernel,
        grid_spec=pltpu.PrefetchScalarGridSpec(
            num_scalar_prefetch=1,
            grid=(1,),
            in_specs=[any_place()] * 3,
            out_specs=whole(shape),
            scratch_shapes=[pltpu.SemaphoreType.DMA((2 * BLOCKS + 1,))],
        ),
        out_shape=shape_of(shape, own.dtype),
        compiler_params=params(),
        cost_estimate=cost(2e9, 0),
    )(scalars, near, far, own)


def finish(scalars, near, far, wide, narrow):
    total, base = near.shape[1], 4 * narrow

    def kernel(scalars, near_ref, far_ref, *refs):
        *outs, held, sems = refs
        c, my = scalars[0], scalars[1]
        copies = []
        for m in range(BLOCKS):
            for source, side in ((near_ref, c), (far_ref, 1 - c)):
                copies.append((source.at[m], held.at[m ^ my, :, pl.ds(pl.multiple_of(side * HALF, 128), HALF)]))
        run_copies(copies, sems)
        for kind in range(4):
            for j in range(BLOCKS):
                outs[kind][narrow * j : narrow * (j + 1)] = held[j, narrow * kind : narrow * (kind + 1)].astype(F32)
        for j in range(BLOCKS):
            at = base + VECTORS
            outs[4][wide * j : wide * (j + 1)] = held[j, at : at + wide].astype(F32)
        last = jnp.concatenate([held[j, base + VECTORS + wide :] for j in range(BLOCKS)], axis=0)
        outs[5][...] = last.astype(F32).T
        low = held[0, base : base + VECTORS, :HALF]
        vectors = low.astype(F32)
        for out, kind in zip(outs[6:8], (0, 2)):
            halves = [product(low, slab_places(first, HALF)(kind), NN) for first in (0, HALF)]
            out[...] = (halves[0][2:3] + halves[1][3:4])[0]
        for out, i in zip(outs[8:], (0, 4, 6, 8, 10, 12, 14)):
            out[...] = jnp.concatenate([vectors[i : i + 1], vectors[i + 1 : i + 2]], axis=1)[0]

    heads = BLOCKS * narrow
    shapes = [(heads, D)] * 4 + [(BLOCKS * wide, D), (D, BLOCKS * wide)] + [(heads,)] * 2 + [(D,)] * 7
    return pl.pallas_call(
        kernel,
        grid_spec=pltpu.PrefetchScalarGridSpec(
            num_scalar_prefetch=1,
            grid=(1,),
            in_specs=[any_place()] * 2,
            out_specs=[whole(shape) for shape in shapes],
            scratch_shapes=[pltpu.VMEM((BLOCKS, total, D), BF), pltpu.SemaphoreType.DMA((2 * BLOCKS,))],
        ),
        out_shape=[shape_of(shape, F32) for shape in shapes],
        compiler_params=params(),
        cost_estimate=cost(2e9, 0),
    )(scalars, near, far)


def core_add(mine, theirs):
    _, shards, rows, columns = mine.shape
    half = shards // 2

    def kernel(mine_ref, theirs_ref, own_ref, x_ref, y_ref, first_ref, second_ref):
        r = pl.program_id(0)
        total = lambda m: (mine_ref[m, 0].astype(F32) + theirs_ref[m, 0].astype(F32)).astype(BF)
        own_ref[0], x_ref[0], y_ref[0] = total(0), total(1), total(2)

        @pl.when(r < half)
        def _():
            first_ref[0] = total(3)

        @pl.when(r >= half)
        def _():
            second_ref[0] = total(3)

    blocks = pl.BlockSpec((BLOCKS, 1, rows, columns), lambda r: (0, r, 0, 0))
    block = lambda index: pl.BlockSpec((1, rows, columns), lambda r: (index(r), 0, 0))
    return pl.pallas_call(
        kernel,
        grid=(shards,),
        in_specs=[blocks, blocks],
        out_specs=[block(lambda r: r)] * 3
        + [block(lambda r: jnp.minimum(r, half - 1)), block(lambda r: jnp.maximum(r - half, 0))],
        out_shape=[shape_of((shards, rows, columns), BF)] * 3 + [shape_of((half, rows, columns), BF)] * 2,
        compiler_params=params(),
        cost_estimate=cost(1e9, 0),
    )(mine, theirs)


def plane_add(for_x, for_y, via_y, via_x):
    half, rows, columns = via_y.shape

    def kernel(x_ref, y_ref, via_y_ref, via_x_ref, x_out, y_out):
        x_out[...] = (x_ref[...].astype(F32) + via_y_ref[...].astype(F32)).astype(BF)
        y_out[...] = (y_ref[...].astype(F32) + via_x_ref[...].astype(F32)).astype(BF)

    block = lambda shift: pl.BlockSpec((1, rows, columns), lambda r: (r + shift, 0, 0))
    return pl.pallas_call(
        kernel,
        grid=(half,),
        in_specs=[block(0), block(half), block(0), block(0)],
        out_specs=[block(0), block(half)],
        out_shape=[shape_of(for_x.shape, BF)] * 2,
        input_output_aliases={0: 0, 1: 1},
        compiler_params=params(),
        cost_estimate=cost(1e9, 0),
    )(for_x, for_y, via_y, via_x)


def tie(array, *before):
    return lax.optimization_barrier((array,) + before)[0]


def build(n_dp, n_tensor):
    flip = {bit: [(i, i ^ bit) for i in range(n_dp)] for bit in (1, 2, 4, 6)}
    f32 = lambda array: array.astype(F32)
    half = n_tensor // 2

    def across(array, bit):
        return lax.ppermute(array, "dp", flip[bit])

    def along(array, r):
        return lax.ppermute(array, "tensor", [(i, i ^ r) for i in range(n_tensor)])

    def from_all(array):
        return [along(array, r) for r in range(1, n_tensor)]

    def from_all_by_steps(array):
        two = along(array, 2)
        one, three = along(jnp.stack([array, two]), 1)
        return [one, two, three]

    def plane(array):
        return [across(array, bit) for bit in (2, 4, 6)]

    def rows_round(k, up, down):
        up = lax.ppermute(up, "tensor", [(i, i + 1) for i in range(k - 1, n_tensor - 1)])
        return up, lax.ppermute(down, "tensor", [(i + 1, i) for i in range(n_tensor - k)])

    def place_rows(z, own, ups, downs):
        seq = own.shape[0]
        rows = jnp.zeros((n_tensor * seq, D), own.dtype)
        rows = lax.dynamic_update_slice(rows, own, (z * seq, 0))
        for k in (2, 1, 3):
            got = jnp.where(z >= k, ups[k - 1], downs[n_tensor - 1 - k])
            rows = lax.dynamic_update_slice(rows, got, (((z - k) & (n_tensor - 1)) * seq, 0))
        return rows

    def add(*terms):
        return sum(f32(term) for term in terms).astype(BF)

    def plane_one(diagonal_y, diagonal_x):
        return across(diagonal_y, 4), across(diagonal_x, 2)

    def plane_two(for_x, for_y):
        return across(for_x, 2), across(for_y, 4)

    def line_sums(group):
        return sum(f32(a[:half]) for a in group), add(*[a[half:] for a in group])

    def line_one(group):
        return sum(f32(a[0::2]) for a in group), add(*[a[1::2] for a in group])

    def line_ends(far):
        return lax.ppermute(far, "tensor", [(0, 1), (3, 2)])

    def line_middle(far):
        return lax.ppermute(far, "tensor", [(1, 2), (2, 1)])

    def line_end(own, last):
        total = own + f32(last)
        step = 8
        while step < n_dp:
            total = total + lax.ppermute(total, "dp", [(i, i ^ step) for i in range(n_dp)])
            step *= 2
        return total.astype(BF)

    def body(
        tokens, w_query, b_query, w_key, w_value, b_value, w_attn_out, b_attn_out, gain_one, shift_one,
        w_inner, b_inner, w_outer, b_outer, gain_two, shift_two, cotangent, lengths, row_ids, col_ids,
    ):
        block = w_inner.shape[1] // BLOCKS
        index = lax.axis_index("dp")
        z = lax.axis_index("tensor")
        c, my = index & 1, (index >> 1) & 3
        scalars = jnp.stack([c, my, z]).astype(jnp.int32)
        tags = (row_ids, col_ids)
        vectors_one = f32(jnp.stack([b_attn_out, gain_one, shift_one]))
        vectors_two = f32(jnp.stack([b_outer, gain_two, shift_two]))

        slab, piece_a = attention_piece(
            scalars, w_query, w_key, w_value, w_attn_out, (b_query, b_value, b_inner)
        )
        with jax.named_scope("line attention weights"):
            line_a = from_all(piece_a)
        first = attention_forward(scalars, lengths, tokens, slab, piece_a, tags, n_tensor, 0)
        w_inner_t, piece_i, piece_u = ffn_pieces(tie(scalars, slab), w_inner, w_outer)

        with jax.named_scope("line inner weights"):
            line_i = from_all(tie(piece_i, *line_a, first[2]))
        own_a = jnp.concatenate([tie(line_a[0], piece_i, first[2])] + line_a[1:])
        with jax.named_scope("plane attention weights"):
            plane_a = plane(own_a)

        own_i = jnp.stack([tie(line_i[0], *plane_a)] + line_i[1:])
        near_a = jnp.stack([tie(own_a, *line_i), *plane_a])
        with jax.named_scope("core attention weights"):
            far_a = across(near_a, 1)
        with jax.named_scope("plane inner weights"):
            plane_i = plane(own_i)
        with jax.named_scope("line outer weights"):
            line_u = from_all(tie(piece_u, *line_i, far_a))

        w_attn = assemble(scalars, near_a, far_a, slab[0], 4 * QKV)
        qkv, heads_out, lse = attention_forward(scalars, lengths, tokens, w_attn, own_a, tags, n_tensor, 1, first)
        own_u = jnp.stack([tie(line_u[0], lse, *plane_i)] + line_u[1:])
        near_i = jnp.stack([tie(own_i, *line_u, lse), *plane_i])
        with jax.named_scope("core inner weights"):
            far_i = across(near_i, 1)
        with jax.named_scope("plane outer weights"):
            plane_u = plane(own_u)

        w_in = assemble(scalars, near_i, far_i, w_inner_t, block)
        normed, inv_spread, hidden, low, act, slope = inner_half(
            scalars, heads_out, w_attn, tokens, vectors_one, w_in, piece_a, own_a
        )
        near_u = jnp.stack([tie(own_u, inv_spread), *plane_u])
        with jax.named_scope("core outer weights"):
            far_u = across(near_u, 1)
        w_up = assemble(scalars, near_u, far_u, w_outer, block)
        out_rows, grad_two, sums_two = outer_half(scalars, act, w_up, hidden, cotangent, vectors_two)

        barrier = lambda *arrays: lax.optimization_barrier(arrays)
        with jax.named_scope("rows 1"):
            up_1, down_1 = rows_round(1, out_rows, out_rows)
        mine_u, other_u = weight_grad(scalars, act, grad_two)
        with jax.named_scope("core outer grad"):
            theirs_u = across(other_u, 1)
        partial, *carried = ffn_back(tie(grad_two, mine_u), grad_two, slope, w_up, w_in, 0, half)
        partial, theirs_u = barrier(partial, theirs_u)
        own_u, x_u, y_u, *via_u = core_add(mine_u, theirs_u)
        with jax.named_scope("plane one outer grad"):
            via_u = plane_one(*via_u)
        grad_one, grad_inner, db_inner, grad_one_low, sums_one = ffn_back(
            grad_two, tie(partial, own_u), slope, w_up, w_in, half, half, (normed, inv_spread, vectors_one), carried
        )
        mine_i, other_i = weight_grad(scalars, grad_inner, low)
        grad_one, mine_i, other_i, up_1, down_1, *via_u = barrier(grad_one, mine_i, other_i, up_1, down_1, *via_u)
        with jax.named_scope("rows 2"):
            up_2, down_2 = rows_round(2, up_1, down_1)
        x_u, y_u = plane_add(x_u, y_u, *via_u)
        with jax.named_scope("plane two outer grad"):
            plane_u = plane_two(x_u, y_u)
        with jax.named_scope("core inner grad"):
            theirs_i = across(other_i, 1)
        vectors = (db_inner, sums_one, sums_two)
        pieces = ()

        def shard_back(start, r):
            dtype = F32 if r else BF
            return attention_backward(
                scalars, lengths, tokens, w_attn, qkv, heads_out, lse, grad_one_low, start, tags, vectors, r, dtype, pieces
            )

        start, *pieces = shard_back(tie(grad_one, x_u), 3)
        start, theirs_i = barrier(start, theirs_i)
        own_i, x_i, y_i, *via_i = core_add(mine_i, theirs_i)
        start, *pieces = shard_back(tie(start, own_i), 2)
        start, *plane_u = barrier(start, *plane_u)
        with jax.named_scope("plane one inner grad"):
            via_i = plane_one(*[tie(v, *plane_u) for v in via_i])
        start, up_2, down_2 = barrier(start, up_2, down_2)
        with jax.named_scope("rows 3"):
            up_3, down_3 = rows_round(3, up_2, down_2)
        start, *pieces = shard_back(start, 1)
        start, own_u, *via_i = barrier(start, own_u, *via_i)
        near_u, far_u = line_sums((own_u, *plane_u))
        with jax.named_scope("line ends outer grad"):
            ends_u = line_ends(far_u)
        x_i, y_i = plane_add(x_i, y_i, *via_i)
        with jax.named_scope("plane two inner grad"):
            plane_i = plane_two(x_i, y_i)
        grad_rows, mine_a, other_a = shard_back(tie(start, x_i, far_u), 0)
        grad_rows, mine_a, other_a, ends_u, up_3, down_3 = barrier(grad_rows, mine_a, other_a, ends_u, up_3, down_3)

        with jax.named_scope("core attention grad"):
            theirs_a = across(other_a, 1)
        with jax.named_scope("grad rows 1"):
            go_1, back_1 = rows_round(1, grad_rows, grad_rows)
        own_a, x_a, y_a, *via_a = core_add(mine_a, theirs_a)
        far_u = add(far_u, tie(ends_u, own_a)[::-1])
        with jax.named_scope("line middle outer grad"):
            middle_u = line_middle(far_u)
        *via_a, plane_i_x, plane_i_y = barrier(*via_a, *plane_i)
        with jax.named_scope("plane one attention grad"):
            via_a = plane_one(*via_a)
        even_i, odd_i = line_one((own_i, plane_i_x, plane_i_y))
        go_1, back_1, odd_i, middle_u, *via_a = barrier(go_1, back_1, odd_i, middle_u, *via_a)
        with jax.named_scope("grad rows 2"):
            go_2, back_2 = rows_round(2, go_1, back_1)
        with jax.named_scope("line one inner grad"):
            got_i = along(odd_i, 1)
        x_a, y_a = plane_add(x_a, y_a, *via_a)
        with jax.named_scope("plane two attention grad"):
            plane_a = plane_two(x_a, y_a)
        layer_out = place_rows(z, tie(out_rows, *via_a), (up_1, up_2, up_3), (down_1, down_2, down_3))
        near_u = near_u + f32(middle_u[::-1])
        layer_out, got_i, *plane_a = barrier(layer_out, got_i, *plane_a)
        group = (own_a, *plane_a)
        low_a = [add(*[a[r] for a in group]) for r in range(1, n_tensor)]
        with jax.named_scope("line attention grad"):
            got_a = [along(a, r) for r, a in enumerate(low_a, 1)]
        even_i, near_u, go_2, back_2, *_ = barrier(even_i, near_u, go_2, back_2, *plane_a)
        even_i = even_i + f32(got_i)
        with jax.named_scope("line two inner grad"):
            last_i = along(even_i[1].astype(BF), 2)
        with jax.named_scope("line pair outer grad"):
            pair_u = along(near_u[1].astype(BF), 1)
        last_i, pair_u, *got_a = barrier(last_i, pair_u, *got_a)
        own_a = sum(f32(a[0]) for a in group) + f32(got_a[0]) + f32(got_a[1])
        done = jnp.concatenate(
            [line_end(own_a, got_a[2]), line_end(near_u[0], pair_u), line_end(even_i[0], last_i)]
        )
        with jax.named_scope("plane result"):
            found = plane(done)
        with jax.named_scope("grad rows 3"):
            go_3, back_3 = rows_round(3, go_2, back_2)
        go_3, back_3, *found = barrier(go_3, back_3, *found)
        near = jnp.stack([done, *found])
        with jax.named_scope("core result"):
            far = across(near, 1)
        grad_tokens = place_rows(z, grad_rows, (go_1, go_2, go_3), (back_1, back_2, back_3))
        grads = finish(scalars, near, far, block, QKV)
        grad_wq, grad_wk, grad_wv, grad_wo, grad_wu, grad_wi, *vectors = grads
        grad_bq, grad_bv, grad_bi, gain_1, shift_1, b_1, gain_2, shift_2, b_2 = vectors

        return (
            layer_out,
            grad_tokens,
            grad_wq.T,
            grad_bq,
            grad_wk.T,
            grad_wv.T,
            grad_bv,
            grad_wo,
            b_1,
            gain_1,
            shift_1,
            grad_wi,
            grad_bi,
            grad_wu,
            b_2,
            gain_2,
            shift_2,
        )

    return body


def solution(mesh):
    rows, columns, out = P("dp", None), P(None, "tensor"), P("tensor", None)
    one = P("tensor")
    in_specs = (
        rows, columns, one, columns, columns, one, out, P(), P(), P(), columns, one, out, P(), P(), P(),
        rows, P("dp"), rows, rows,
    )
    out_specs = (
        rows, rows, columns, one, columns, columns, one, out, P(), P(), P(), columns, one, out, P(), P(), P(),
    )
    body = build(mesh.shape["dp"], mesh.shape["tensor"])
    return jax.shard_map(body, mesh=mesh, in_specs=in_specs, out_specs=out_specs, check_vma=False)
```

```python
import functools

import jax
import jax.numpy as jnp
from jax import lax
from jax.experimental import pallas as pl
from jax.experimental.pallas import tpu as pltpu
from jax.sharding import PartitionSpec as P

F32 = jnp.float32
BF = jnp.bfloat16
HD = 64
D = 768
HALF = D // 2
BLOCKS = 4
QKV = 48
epsilon = 1e-12
masked_value = -1e30
CHUNK = 512
SCALE = 0.05
VECTORS = 16

NN = (((1,), (0,)), ((), ()))
NT = (((1,), (1,)), ((), ()))
TN = (((0,), (0,)), ((), ()))


def product(left, right, dims):
    return lax.dot_general(left, right, dims, preferred_element_type=F32)


def shape_of(shape, dtype):
    return jax.ShapeDtypeStruct(shape, dtype)


def whole(shape):
    return pl.BlockSpec(shape, lambda r, *_: (0,) * len(shape))


def each(shape, shift=0):
    return pl.BlockSpec((1,) + shape, lambda r, *_: (r + shift,) + (0,) * len(shape))


def params(mebibytes=16):
    return pltpu.CompilerParams(vmem_limit_bytes=mebibytes * 1024 * 1024)


def cost(flops, moved, exps=0):
    return pl.CostEstimate(flops=int(flops * SCALE), bytes_accessed=int(moved * SCALE), transcendentals=int(exps))


def rows_of(ref, kind):
    width = 3 * QKV
    return jnp.concatenate(
        [ref[0, width * j + QKV * kind : width * j + QKV * (kind + 1)] for j in range(BLOCKS)], axis=0
    )


class Masks:
    def __init__(self, scalars, lengths, row_ref, col_ref):
        table = scalars[2]
        length = lengths[table]
        row_q = row_ref[pl.ds(table, 1), :].astype(F32)
        col_q = col_ref[pl.ds(table, 1), :].astype(F32)
        row_k, col_k = as_column(row_q), as_column(col_q)
        position = lax.broadcasted_iota(jnp.int32, row_k.shape, 0)
        self.here = position < length
        self.leading = position == 0
        self.row_k = jnp.where(self.here, row_k, -1.0)
        self.col_k = jnp.where(self.here, col_k, -1.0)
        self.row_q, self.col_q = row_q, col_q

    def scores(self, logits, kind):
        if kind == 0:
            visible = self.here
        elif kind == 1:
            visible = (self.row_k == self.row_q) | self.leading
        else:
            visible = (self.col_k == self.col_q) | self.leading
        return jnp.where(visible, logits, masked_value)


def as_column(row):
    return jnp.broadcast_to(row, (8, row.shape[1])).T[:, 0:1]


def projection_rows(w_ref):
    return jnp.concatenate([w_ref[0, 4 * QKV * j : 4 * QKV * j + 3 * QKV] for j in range(BLOCKS)], axis=0)


def output_rows(w_ref, shard=0):
    return jnp.concatenate(
        [w_ref[shard, 4 * QKV * j + 3 * QKV : 4 * QKV * (j + 1)] for j in range(BLOCKS)], axis=0
    )


def attention_forward_kernel(scalars, lengths, x_ref, w_ref, b_ref, row_ref, col_ref, *rest):
    qkv_ref, o_ref, lse_ref = rest[-3:]
    seq = x_ref.shape[0]
    bias = b_ref[0].astype(F32)
    bias = jnp.concatenate([bias[0:1], bias[1:2, : 3 * BLOCKS * QKV - HALF]], axis=1)
    qkv = product(projection_rows(w_ref), x_ref[...], NT) + as_column(bias)
    low = qkv.astype(BF)
    is_query = lax.broadcasted_iota(jnp.int32, (qkv.shape[0], 1), 0) % (3 * QKV) < QKV
    low = jnp.where(is_query, low * jnp.asarray(HD**-0.5, BF), low)
    qkv_ref[0] = low
    masks = Masks(scalars, lengths, row_ref, col_ref)
    q_t, k_t, v_t = rows_of(qkv_ref, 0), rows_of(qkv_ref, 1), rows_of(qkv_ref, 2)
    outs, logs = [], []
    for head in range(q_t.shape[0] // HD):
        rows = slice(HD * head, HD * (head + 1))
        scores = masks.scores(product(k_t[rows].T, q_t[rows], NN), head % 3)
        highest = jnp.max(scores, axis=0, keepdims=True)
        weights = jnp.exp(scores - highest).astype(BF)
        with_ones = jnp.concatenate([v_t[rows], jnp.ones((16, seq), BF)], axis=0)
        blended = product(with_ones, weights, NN)
        total = blended[HD : HD + 1]
        outs.append(blended[:HD] * (1.0 / total))
        logs.append(highest + jnp.log(total))
    o_ref[0] = jnp.concatenate(outs, axis=0).astype(BF)
    logs.append(jnp.zeros((8 - len(logs), seq), F32))
    lse_ref[0] = jnp.concatenate(logs, axis=0)


def in_hbm():
    return pl.BlockSpec(memory_space=pltpu.HBM)


def table_rows(seq):
    return pl.BlockSpec((seq, D), lambda r, scalars, *_: (scalars[2], 0))


def bias_rows(shift=0):
    return pl.BlockSpec((1, VECTORS, HALF), lambda r, *_: (r + shift, 4 * QKV // VECTORS, 0))


def attention_forward(scalars, lengths, tokens, weights, pieces, tags, shards, first, carried=None):
    wide, seq = 3 * BLOCKS * QKV, tags[0].shape[1]
    count, at = pieces.shape[0], first if carried else 0
    out_shape = [
        shape_of((shards, wide, seq), BF),
        shape_of((shards, wide // 3, seq), BF),
        shape_of((shards, 8, seq), F32),
    ]
    kept = list(carried) if carried else []
    return pl.pallas_call(
        attention_forward_kernel,
        grid_spec=pltpu.PrefetchScalarGridSpec(
            num_scalar_prefetch=2,
            grid=(count,),
            in_specs=[
                table_rows(seq),
                each((weights.shape[1], D), at),
                bias_rows(),
                whole(tags[0].shape),
                whole(tags[1].shape),
            ]
            + [pl.BlockSpec(memory_space=pl.ANY)] * len(kept),
            out_specs=[each(s.shape[1:], first) for s in out_shape],
        ),
        out_shape=out_shape,
        input_output_aliases={7 + i: i for i in range(len(kept))},
        compiler_params=params(),
        cost_estimate=cost(count * 3e9, count * 3e6),
    )(scalars, lengths, tokens, weights, pieces, *tags, *kept)


def attention_backward_kernel(
    scalars, lengths, x_hbm, w_hbm, qkv_hbm, o_hbm, lse_hbm, up_hbm, start_hbm, row_ref, col_ref, dbi_ref, one_ref, two_ref,
    *refs, shard, carried,
):
    dx_ref, mine_ref, other_ref, d_ref, x_ref, w_ref, qkv_ref, o_ref, lse_ref, low_ref, start_ref, sems = refs[carried:]
    seq = x_ref.shape[0]
    at = pl.ds(shard, 1)
    copies = [
        (w_hbm.at[at], w_ref),
        (up_hbm, low_ref),
        (qkv_hbm.at[at], qkv_ref),
        (o_hbm.at[at], o_ref),
        (lse_hbm.at[at], lse_ref),
        (x_hbm.at[pl.ds(pl.multiple_of(scalars[2] * seq, 128), seq)], x_ref),
        (start_hbm, start_ref),
    ]
    started = [pltpu.make_async_copy(source, target, sems.at[i]) for i, (source, target) in enumerate(copies)]
    for copy in started:
        copy.start()
    for copy in started[:5]:
        copy.wait()
    masks = Masks(scalars, lengths, row_ref, col_ref)
    q_t, k_t, v_t = rows_of(qkv_ref, 0), rows_of(qkv_ref, 1), rows_of(qkv_ref, 2)
    grad_heads = product(output_rows(w_ref), low_ref[...], NT).astype(BF)
    heads_out = o_ref[0]
    parts = [[], [], []]
    for head in range(q_t.shape[0] // HD):
        rows = slice(HD * head, HD * (head + 1))
        queries_t, keys_t, grad_t = q_t[rows], k_t[rows], grad_heads[rows]
        scores = masks.scores(product(keys_t.T, queries_t, NN), head % 3)
        chances = jnp.exp(scores - lse_ref[0, head : head + 1])
        grad_chances = product(v_t[rows].T, grad_t, NN)
        inner = jnp.sum(grad_t.astype(F32) * heads_out[rows].astype(F32), axis=0, keepdims=True)
        grad_logits = (chances * (grad_chances - inner)).astype(BF)
        parts[2].append(product(chances.astype(BF), grad_t.T, NN).T)
        parts[1].append(product(grad_logits, queries_t.T, NN).T)
        parts[0].append(product(keys_t, grad_logits, NN) * HD**-0.5)
    for kind in range(3):
        joined = jnp.concatenate(parts[kind], axis=0).astype(BF)
        for j in range(BLOCKS):
            base = 3 * QKV * j + QKV * kind
            d_ref[base : base + QKV, :] = joined[QKV * j : QKV * (j + 1)]
    grads_low = d_ref[...]
    for copy in started[5:]:
        copy.wait()
    dx_ref[...] = (start_ref[...] + product(grads_low, projection_rows(w_ref), TN)).astype(dx_ref.dtype)
    db = product(jnp.ones((8, seq), BF), grads_low, NT)[:1]
    vectors = [dbi_ref[0, :, :HALF], dbi_ref[0, :, HALF:], db[:, :HALF]]
    vectors.append(jnp.concatenate([db[:, HALF:], jnp.zeros((1, 2 * HALF - db.shape[1]), F32)], axis=1))
    for sums_ref in (one_ref, two_ref):
        for i in range(3):
            vectors += [sums_ref[i : i + 1, :HALF], sums_ref[i : i + 1, HALF:]]
    vectors = jnp.concatenate(vectors, axis=0).astype(BF)
    c, my = scalars[0], scalars[1]
    for half, out_ref in enumerate((mine_ref, other_ref)):
        start = pl.multiple_of(jnp.where(c == half, 0, HALF), 128)
        grad_w = product(grads_low, x_ref[:, pl.ds(start, HALF)], NN).astype(BF)
        grad_wo = product(heads_out, low_ref[:, pl.ds(start, HALF)], NN).astype(BF)
        for j in range(BLOCKS):
            out_ref[j ^ my, 0, : 3 * QKV] = grad_w[3 * QKV * j : 3 * QKV * (j + 1)]
            out_ref[j ^ my, 0, 3 * QKV : 4 * QKV] = grad_wo[QKV * j : QKV * (j + 1)]
            here = jnp.where(c == half, 1.0, 0.0).astype(BF) if j == 0 else jnp.zeros((), BF)
            out_ref[j ^ my, 0, 4 * QKV :] = vectors * here


def attention_backward(
    scalars, lengths, tokens, weights, qkv, heads_out, lse, upstream, start, tags, vectors, shard, dtype, carried
):
    shards, wide, seq = qkv.shape
    rows = 4 * QKV + VECTORS
    pieces = shape_of((BLOCKS, shards, rows, HALF), BF)
    piece = pl.BlockSpec((BLOCKS, 1, rows, HALF), lambda r, *_: (0, shard, 0, 0))
    return pl.pallas_call(
        functools.partial(attention_backward_kernel, shard=shard, carried=len(carried)),
        grid_spec=pltpu.PrefetchScalarGridSpec(
            num_scalar_prefetch=2,
            grid=(1,),
            in_specs=[in_hbm()] * 7
            + [whole(tags[0].shape), whole(tags[1].shape), each(vectors[0].shape[1:], shard)]
            + [whole((8, D)), whole((8, D))]
            + [in_hbm()] * len(carried),
            out_specs=[whole((seq, D)), piece, piece],
            scratch_shapes=[
                pltpu.VMEM((wide, seq), BF),
                pltpu.VMEM((seq, D), BF),
                pltpu.VMEM((1,) + weights.shape[1:], BF),
                pltpu.VMEM((1, wide, seq), BF),
                pltpu.VMEM((1, wide // 3, seq), BF),
                pltpu.VMEM((1, 8, seq), F32),
                pltpu.VMEM((seq, D), BF),
                pltpu.VMEM((seq, D), F32),
                pltpu.SemaphoreType.DMA((7,)),
            ],
        ),
        out_shape=[shape_of((seq, D), dtype), pieces, pieces],
        input_output_aliases={14 + i: 1 + i for i in range(len(carried))},
        compiler_params=params(),
        cost_estimate=cost(5e9, 5e6),
    )(scalars, lengths, tokens, weights, qkv, heads_out, lse, upstream, start, *tags, *vectors, *carried)


def gelu_pair(x):
    bell = jnp.exp(x * x * -0.5)
    t = 1.0 / (1.0 + (0.3275911 * 0.70710678118654752) * jnp.abs(x))
    series = 0.5 * 1.061405429
    for factor in (-1.453152027, 1.421413741, -0.284496736, 0.254829592):
        series = series * t + 0.5 * factor
    tail = series * t * bell
    below = jnp.where(x < 0, tail, 1.0 - tail)
    return x * below, below + x * (bell * 0.3989422804014327)


def normalize(residual):
    centre = residual - jnp.mean(residual, axis=-1, keepdims=True)
    inv_spread = lax.rsqrt(jnp.mean(centre * centre, axis=-1, keepdims=True) + epsilon)
    return centre * inv_spread, inv_spread


def norm_back(upstream, normed, inv_spread, gain):
    scaled = upstream * gain
    return inv_spread * (
        scaled
        - jnp.mean(scaled, axis=-1, keepdims=True)
        - normed * jnp.mean(scaled * normed, axis=-1, keepdims=True)
    )


def add_sums(sums, *terms):
    return [total + jnp.sum(term, axis=0, keepdims=True) for total, term in zip(sums, terms)]


def store_sums(ref, sums):
    ref[...] = jnp.concatenate(sums + [jnp.zeros((8 - len(sums), D), F32)], axis=0)


def inner_kernel(
    scalars, o_ref, wo_ref, x_ref, vec_ref, wi_ref, own_ref, others_ref,
    normed_ref, inv_ref, hidden_ref, low_ref, act_ref, slope_ref,
):
    seq, r = x_ref.shape[0], pl.program_id(0)
    bias = jnp.where(r == 0, own_ref[0].astype(F32), others_ref[jnp.maximum(r - 1, 0)].astype(F32))
    bias = jnp.concatenate([bias[2:3], bias[3:4]], axis=1)

    @pl.when(r == 0)
    def _():
        for start in range(0, seq, CHUNK):
            rows = slice(start, start + CHUNK)
            residual = vec_ref[0:1] + x_ref[rows].astype(F32)
            for shard in range(o_ref.shape[0]):
                residual = residual + product(o_ref[shard, :, rows], output_rows(wo_ref, shard), TN)
            normed, inv_spread = normalize(residual)
            hidden = normed * vec_ref[1:2] + vec_ref[2:3]
            normed_ref[rows], inv_ref[rows], hidden_ref[rows] = normed, inv_spread, hidden
            low_ref[rows] = hidden.astype(BF)

    for start in range(0, seq, CHUNK):
        rows = slice(start, start + CHUNK)
        act, slope = gelu_pair(product(low_ref[rows], wi_ref[0], NT) + bias)
        act_ref[0, rows] = act.astype(BF)
        slope_ref[0, rows] = slope.astype(BF)


def inner_half(scalars, heads_out, w_out, tokens, vectors, w_inner, own_piece, pieces):
    shards, wide, seq = w_inner.shape[0], w_inner.shape[1], heads_out.shape[2]
    return pl.pallas_call(
        inner_kernel,
        grid_spec=pltpu.PrefetchScalarGridSpec(
            num_scalar_prefetch=1,
            grid=(shards,),
            in_specs=[
                whole(heads_out.shape),
                whole(w_out.shape),
                table_rows(seq),
                whole(vectors.shape),
                each((wide, D)),
                pl.BlockSpec((1, VECTORS, HALF), lambda r, *_: (0, 4 * QKV // VECTORS, 0)),
                pl.BlockSpec((shards - 1, VECTORS, HALF), lambda r, *_: (0, 4 * QKV // VECTORS, 0)),
            ],
            out_specs=[
                whole((seq, D)),
                whole((seq, 1)),
                whole((seq, D)),
                whole((seq, D)),
                each((seq, wide)),
                each((seq, wide)),
            ],
        ),
        out_shape=[
            shape_of((seq, D), F32),
            shape_of((seq, 1), F32),
            shape_of((seq, D), F32),
            shape_of((seq, D), BF),
            shape_of((shards, seq, wide), BF),
            shape_of((shards, seq, wide), BF),
        ],
        compiler_params=params(),
        cost_estimate=cost(12e9, 20e6),
    )(scalars, heads_out, w_out, tokens, vectors, w_inner, own_piece, pieces)


def outer_kernel(scalars, act_ref, wu_ref, hidden_ref, cot_ref, vec_ref, out_ref, grad_ref, sums_ref, acc_ref):
    r, last, seq = pl.program_id(0), pl.num_programs(0) - 1, hidden_ref.shape[0]

    @pl.when(r == 0)
    def _():
        acc_ref[...] = hidden_ref[...] + vec_ref[0:1]

    acc_ref[...] = acc_ref[...] + product(act_ref[0], wu_ref[0], NN)

    @pl.when(r == last)
    def _():
        sums = [jnp.zeros((1, D), F32)] * 3
        gain = vec_ref[1:2]
        for start in range(0, seq, CHUNK):
            rows = slice(start, start + CHUNK)
            normed, inv_spread = normalize(acc_ref[rows])
            out_ref[rows] = (normed * gain + vec_ref[2:3]).astype(BF)
            upstream = cot_ref[rows].astype(F32)
            grad = norm_back(upstream, normed, inv_spread, gain)
            grad_ref[rows] = grad
            sums = add_sums(sums, upstream * normed, upstream, grad)
        store_sums(sums_ref, sums)


def outer_half(scalars, act, w_outer, hidden, cotangent, vectors):
    shards, seq, wide = act.shape
    return pl.pallas_call(
        outer_kernel,
        grid_spec=pltpu.PrefetchScalarGridSpec(
            num_scalar_prefetch=1,
            grid=(shards,),
            in_specs=[
                each((seq, wide)),
                each((wide, D)),
                whole((seq, D)),
                table_rows(seq),
                whole(vectors.shape),
            ],
            out_specs=[whole((seq, D)), whole((seq, D)), whole((8, D))],
            scratch_shapes=[pltpu.VMEM((seq, D), F32)],
        ),
        out_shape=[shape_of((seq, D), BF), shape_of((seq, D), F32), shape_of((8, D), F32)],
        compiler_params=params(),
        cost_estimate=cost(5e9, 14e6),
    )(scalars, act, w_outer, hidden, cotangent, vectors)


def ffn_back_kernel(up_ref, start_ref, slope_ref, wu_ref, wi_ref, *refs, final):
    if final:
        normed_ref, inv_ref, vec_ref, *refs = refs[:3] + refs[5:]
        grad_ref, inner_ref, db_ref, grad_low_ref, sums_ref, acc_ref, low_ref = refs
    else:
        grad_ref, inner_ref, db_ref, acc_ref, low_ref = refs
    r, last = pl.program_id(0), pl.num_programs(0) - 1
    seq, wide = up_ref.shape[0], wi_ref.shape[1]

    @pl.when(r == 0)
    def _():
        acc_ref[...] = start_ref[...]
        low_ref[...] = up_ref[...].astype(BF)

    db = jnp.zeros((1, wide), F32)
    for start in range(0, seq, CHUNK):
        rows = slice(start, start + CHUNK)
        grad_inner = product(low_ref[rows], wu_ref[0], NT) * slope_ref[0, rows].astype(F32)
        db = db + jnp.sum(grad_inner, axis=0, keepdims=True)
        inner_ref[0, rows] = grad_inner.astype(BF)
    db_ref[0] = db
    acc_ref[...] = acc_ref[...] + product(inner_ref[0], wi_ref[0], NN)

    @pl.when(r == last)
    def _():
        if not final:
            grad_ref[...] = acc_ref[...]
            return
        sums = [jnp.zeros((1, D), F32)] * 3
        for start in range(0, seq, CHUNK):
            rows = slice(start, start + CHUNK)
            upstream, normed = acc_ref[rows], normed_ref[rows]
            grad = norm_back(upstream, normed, inv_ref[rows], vec_ref[1:2])
            grad_ref[rows] = grad
            grad_low_ref[rows] = grad.astype(BF)
            sums = add_sums(sums, upstream * normed, upstream, grad)
        store_sums(sums_ref, sums)


def ffn_back(upstream, start, slope, w_outer, w_inner, first, count, norm=(), carried=()):
    shards, seq, wide = slope.shape
    final = bool(norm)
    out_specs = [whole((seq, D)), each((seq, wide), first), each((1, wide), first)]
    out_shape = [shape_of((seq, D), F32), shape_of((shards, seq, wide), BF), shape_of((shards, 1, wide), F32)]
    if final:
        out_specs += [whole((seq, D)), whole((8, D))]
        out_shape += [shape_of((seq, D), BF), shape_of((8, D), F32)]
    return pl.pallas_call(
        functools.partial(ffn_back_kernel, final=final),
        grid=(count,),
        in_specs=[
            whole((seq, D)),
            whole((seq, D)),
            each((seq, wide), first),
            each((wide, D), first),
            each((wide, D), first),
        ]
        + [whole(array.shape) for array in norm]
        + [any_place()] * len(carried),
        out_specs=out_specs,
        out_shape=out_shape,
        input_output_aliases={8 + i: 1 + i for i in range(len(carried))},
        scratch_shapes=[pltpu.VMEM((seq, D), F32), pltpu.VMEM((seq, D), BF)],
        compiler_params=params(),
        cost_estimate=cost(count * 3e9, count * 4e6),
    )(upstream, start, slope, w_outer, w_inner, *norm, *carried)


def weight_grad_kernel(scalars, left_ref, right_ref, mine_ref, other_ref, low_ref):
    @pl.when(pl.program_id(0) == 0)
    def _():
        low_ref[...] = right_ref[...].astype(BF)

    c, my = scalars[0], scalars[1]
    rows = mine_ref.shape[2]
    for half, out_ref in enumerate((mine_ref, other_ref)):
        start = pl.multiple_of(jnp.where(c == half, 0, HALF), 128)
        grad = product(left_ref[0], low_ref[:, pl.ds(start, HALF)], TN).astype(BF)
        for j in range(BLOCKS):
            out_ref[j ^ my, 0] = grad[rows * j : rows * (j + 1)]


def weight_grad(scalars, left, right):
    shards, seq, wide = left.shape
    piece = pl.BlockSpec((BLOCKS, 1, wide // BLOCKS, HALF), lambda r, *_: (0, r, 0, 0))
    pieces = shape_of((BLOCKS, shards, wide // BLOCKS, HALF), BF)
    return pl.pallas_call(
        weight_grad_kernel,
        grid_spec=pltpu.PrefetchScalarGridSpec(
            num_scalar_prefetch=1,
            grid=(shards,),
            in_specs=[each((seq, wide)), whole((seq, D))],
            out_specs=[piece, piece],
            scratch_shapes=[pltpu.VMEM((seq, D), BF)],
        ),
        out_shape=[pieces, pieces],
        compiler_params=params(),
        cost_estimate=cost(shards * 1.5e9, shards * 2e6),
    )(scalars, left, right)


def run_copies(copies, sems):
    started = [pltpu.make_async_copy(source, target, sems.at[i]) for i, (source, target) in enumerate(copies)]
    for copy in started:
        copy.start()
    for copy in started:
        copy.wait()


def any_place():
    return pl.BlockSpec(memory_space=pl.ANY)


def slab_places(first, columns):
    col = lax.broadcasted_iota(jnp.int32, (columns, BLOCKS * QKV), 0) + first
    feature = lax.broadcasted_iota(jnp.int32, (columns, BLOCKS * QKV), 1)
    block = sum((feature >= QKV * j).astype(jnp.int32) for j in range(1, BLOCKS))
    return lambda kind: (col == feature + block * 2 * QKV + QKV * kind).astype(BF)


def attention_piece(scalars, w_query, w_key, w_value, w_out, biases):
    heads = BLOCKS * QKV

    def kernel(scalars, *refs):
        w_refs, (query_ref, value_ref, inner_ref, slab_ref, piece_ref, sems) = refs[:4], refs[4:]
        copies = []
        for j in range(BLOCKS):
            for kind, w_ref in enumerate(w_refs):
                base = QKV * (4 * j + kind)
                copies.append((w_ref.at[pl.ds(QKV * j, QKV)], slab_ref.at[0, pl.ds(base, QKV)]))
        started = [pltpu.make_async_copy(source, target, sems.at[i]) for i, (source, target) in enumerate(copies)]
        for copy in started:
            copy.start()
        every = lambda ref: jnp.broadcast_to(ref[...].astype(F32).reshape(1, -1), (16, ref.shape[0]))
        of_query, of_value, inner = every(query_ref), every(value_ref), every(inner_ref)
        low = []
        for first in (0, HALF):
            places = slab_places(first, HALF)
            low.append(product(of_query.astype(BF), places(0), NT) + product(of_value.astype(BF), places(2), NT))
        rows = [low[0], low[1], inner[:, :HALF], inner[:, HALF:]]
        at = lax.broadcasted_iota(jnp.int32, (16, HALF), 0)
        piece_ref[0, 4 * QKV :] = sum(jnp.where(at == i, row, 0.0) for i, row in enumerate(rows)).astype(BF)
        for copy in started:
            copy.wait()
        c, my = scalars[0], scalars[1]
        rows = pl.ds(pl.multiple_of(my * 4 * QKV, 16), 4 * QKV)
        piece_ref[0, : 4 * QKV] = slab_ref[0, rows, pl.ds(pl.multiple_of(c * HALF, 128), HALF)]

    weights = (w_query.T, w_key.T, w_value.T, w_out)
    return pl.pallas_call(
        kernel,
        grid_spec=pltpu.PrefetchScalarGridSpec(
            num_scalar_prefetch=1,
            grid=(1,),
            in_specs=[in_hbm()] * 4 + [whole(bias.shape) for bias in biases],
            out_specs=[whole((1, 4 * heads, D)), whole((1, 4 * QKV + VECTORS, HALF))],
            scratch_shapes=[pltpu.SemaphoreType.DMA((4 * BLOCKS,))],
        ),
        out_shape=[shape_of((1, 4 * heads, D), BF), shape_of((1, 4 * QKV + VECTORS, HALF), BF)],
        compiler_params=params(58),
        cost_estimate=cost(2e9, 0),
    )(scalars, *weights, *biases)


def ffn_pieces(scalars, w_inner, w_outer):
    wide = w_inner.shape[1]
    rows = wide // BLOCKS

    def kernel(scalars, wi_hbm, wu_hbm, wt_ref, i_ref, u_ref, wi_ref, sems):
        c, my = scalars[0], scalars[1]
        block = pl.ds(pl.multiple_of(my * rows, 16), rows)
        columns = pl.ds(pl.multiple_of(c * HALF, 128), HALF)
        run_copies([(wi_hbm, wi_ref), (wu_hbm.at[block, columns], u_ref)], sems)
        wt_ref[...] = wi_ref[...].T
        i_ref[...] = wt_ref[block, columns]

    return pl.pallas_call(
        kernel,
        grid_spec=pltpu.PrefetchScalarGridSpec(
            num_scalar_prefetch=1,
            grid=(1,),
            in_specs=[in_hbm()] * 2,
            out_specs=[whole((wide, D)), whole((rows, HALF)), whole((rows, HALF))],
            scratch_shapes=[pltpu.VMEM(w_inner.shape, BF), pltpu.SemaphoreType.DMA((2,))],
        ),
        out_shape=[shape_of((wide, D), BF), shape_of((rows, HALF), BF), shape_of((rows, HALF), BF)],
        compiler_params=params(58),
        cost_estimate=cost(2e9, 0),
    )(scalars, w_inner, w_outer)


def assemble(scalars, near, far, own, rows):
    count = near.shape[1]

    def kernel(scalars, near_ref, far_ref, own_ref, out_ref, sems):
        c, my = scalars[0], scalars[1]
        copies = [(own_ref, out_ref.at[0])]
        for m in range(BLOCKS):
            for source, side in ((near_ref, c), (far_ref, 1 - c)):
                target = out_ref.at[
                    pl.ds(1, count),
                    pl.ds(pl.multiple_of((m ^ my) * rows, 16), rows),
                    pl.ds(pl.multiple_of(side * HALF, 128), HALF),
                ]
                copies.append((source.at[m, :, pl.ds(0, rows)], target))
        run_copies(copies, sems)

    shape = (1 + count, BLOCKS * rows, D)
    return pl.pallas_call(
        kernel,
        grid_spec=pltpu.PrefetchScalarGridSpec(
            num_scalar_prefetch=1,
            grid=(1,),
            in_specs=[any_place()] * 3,
            out_specs=whole(shape),
            scratch_shapes=[pltpu.SemaphoreType.DMA((2 * BLOCKS + 1,))],
        ),
        out_shape=shape_of(shape, own.dtype),
        compiler_params=params(),
        cost_estimate=cost(2e9, 0),
    )(scalars, near, far, own)


def finish(scalars, near, far, wide, narrow):
    total, base = near.shape[1], 4 * narrow

    def kernel(scalars, near_ref, far_ref, *refs):
        *outs, held, sems = refs
        c, my = scalars[0], scalars[1]
        copies = []
        for m in range(BLOCKS):
            for source, side in ((near_ref, c), (far_ref, 1 - c)):
                copies.append((source.at[m], held.at[m ^ my, :, pl.ds(pl.multiple_of(side * HALF, 128), HALF)]))
        run_copies(copies, sems)
        for kind in range(4):
            for j in range(BLOCKS):
                outs[kind][narrow * j : narrow * (j + 1)] = held[j, narrow * kind : narrow * (kind + 1)].astype(F32)
        for j in range(BLOCKS):
            at = base + VECTORS
            outs[4][wide * j : wide * (j + 1)] = held[j, at : at + wide].astype(F32)
        last = jnp.concatenate([held[j, base + VECTORS + wide :] for j in range(BLOCKS)], axis=0)
        outs[5][...] = last.astype(F32).T
        low = held[0, base : base + VECTORS, :HALF]
        vectors = low.astype(F32)
        for out, kind in zip(outs[6:8], (0, 2)):
            halves = [product(low, slab_places(first, HALF)(kind), NN) for first in (0, HALF)]
            out[...] = (halves[0][2:3] + halves[1][3:4])[0]
        for out, i in zip(outs[8:], (0, 4, 6, 8, 10, 12, 14)):
            out[...] = jnp.concatenate([vectors[i : i + 1], vectors[i + 1 : i + 2]], axis=1)[0]

    heads = BLOCKS * narrow
    shapes = [(heads, D)] * 4 + [(BLOCKS * wide, D), (D, BLOCKS * wide)] + [(heads,)] * 2 + [(D,)] * 7
    return pl.pallas_call(
        kernel,
        grid_spec=pltpu.PrefetchScalarGridSpec(
            num_scalar_prefetch=1,
            grid=(1,),
            in_specs=[any_place()] * 2,
            out_specs=[whole(shape) for shape in shapes],
            scratch_shapes=[pltpu.VMEM((BLOCKS, total, D), BF), pltpu.SemaphoreType.DMA((2 * BLOCKS,))],
        ),
        out_shape=[shape_of(shape, F32) for shape in shapes],
        compiler_params=params(),
        cost_estimate=cost(2e9, 0),
    )(scalars, near, far)


def core_add(mine, theirs):
    _, shards, rows, columns = mine.shape
    half = shards // 2

    def kernel(mine_ref, theirs_ref, own_ref, x_ref, y_ref, first_ref, second_ref):
        r = pl.program_id(0)
        total = lambda m: (mine_ref[m, 0].astype(F32) + theirs_ref[m, 0].astype(F32)).astype(BF)
        own_ref[0], x_ref[0], y_ref[0] = total(0), total(1), total(2)

        @pl.when(r < half)
        def _():
            first_ref[0] = total(3)

        @pl.when(r >= half)
        def _():
            second_ref[0] = total(3)

    blocks = pl.BlockSpec((BLOCKS, 1, rows, columns), lambda r: (0, r, 0, 0))
    block = lambda index: pl.BlockSpec((1, rows, columns), lambda r: (index(r), 0, 0))
    return pl.pallas_call(
        kernel,
        grid=(shards,),
        in_specs=[blocks, blocks],
        out_specs=[block(lambda r: r)] * 3
        + [block(lambda r: jnp.minimum(r, half - 1)), block(lambda r: jnp.maximum(r - half, 0))],
        out_shape=[shape_of((shards, rows, columns), BF)] * 3 + [shape_of((half, rows, columns), BF)] * 2,
        compiler_params=params(),
        cost_estimate=cost(1e9, 0),
    )(mine, theirs)


def plane_add(for_x, for_y, via_y, via_x):
    half, rows, columns = via_y.shape

    def kernel(x_ref, y_ref, via_y_ref, via_x_ref, x_out, y_out):
        x_out[...] = (x_ref[...].astype(F32) + via_y_ref[...].astype(F32)).astype(BF)
        y_out[...] = (y_ref[...].astype(F32) + via_x_ref[...].astype(F32)).astype(BF)

    block = lambda shift: pl.BlockSpec((1, rows, columns), lambda r: (r + shift, 0, 0))
    return pl.pallas_call(
        kernel,
        grid=(half,),
        in_specs=[block(0), block(half), block(0), block(0)],
        out_specs=[block(0), block(half)],
        out_shape=[shape_of(for_x.shape, BF)] * 2,
        input_output_aliases={0: 0, 1: 1},
        compiler_params=params(),
        cost_estimate=cost(1e9, 0),
    )(for_x, for_y, via_y, via_x)


def tie(array, *before):
    return lax.optimization_barrier((array,) + before)[0]


def build(n_dp, n_tensor):
    flip = {bit: [(i, i ^ bit) for i in range(n_dp)] for bit in (1, 2, 4, 6)}
    f32 = lambda array: array.astype(F32)
    half = n_tensor // 2

    def across(array, bit):
        return lax.ppermute(array, "dp", flip[bit])

    def along(array, r):
        return lax.ppermute(array, "tensor", [(i, i ^ r) for i in range(n_tensor)])

    def from_all(array):
        return [along(array, r) for r in range(1, n_tensor)]

    def from_all_by_steps(array):
        two = along(array, 2)
        one, three = along(jnp.stack([array, two]), 1)
        return [one, two, three]

    def plane(array):
        return [across(array, bit) for bit in (2, 4, 6)]

    def rows_round(k, up, down):
        up = lax.ppermute(up, "tensor", [(i, i + 1) for i in range(k - 1, n_tensor - 1)])
        return up, lax.ppermute(down, "tensor", [(i + 1, i) for i in range(n_tensor - k)])

    def place_rows(z, own, ups, downs):
        seq = own.shape[0]
        rows = jnp.zeros((n_tensor * seq, D), own.dtype)
        rows = lax.dynamic_update_slice(rows, own, (z * seq, 0))
        for k in (2, 1, 3):
            got = jnp.where(z >= k, ups[k - 1], downs[n_tensor - 1 - k])
            rows = lax.dynamic_update_slice(rows, got, (((z - k) & (n_tensor - 1)) * seq, 0))
        return rows

    def add(*terms):
        return sum(f32(term) for term in terms).astype(BF)

    def plane_one(diagonal_y, diagonal_x):
        return across(diagonal_y, 4), across(diagonal_x, 2)

    def plane_two(for_x, for_y):
        return across(for_x, 2), across(for_y, 4)

    def line_sums(group):
        return sum(f32(a[:half]) for a in group), add(*[a[half:] for a in group])

    def line_one(group):
        return sum(f32(a[0::2]) for a in group), add(*[a[1::2] for a in group])

    def line_ends(far):
        return lax.ppermute(far, "tensor", [(0, 1), (3, 2)])

    def line_middle(far):
        return lax.ppermute(far, "tensor", [(1, 2), (2, 1)])

    def line_end(own, last):
        total = own + f32(last)
        step = 8
        while step < n_dp:
            total = total + lax.ppermute(total, "dp", [(i, i ^ step) for i in range(n_dp)])
            step *= 2
        return total.astype(BF)

    def body(
        tokens, w_query, b_query, w_key, w_value, b_value, w_attn_out, b_attn_out, gain_one, shift_one,
        w_inner, b_inner, w_outer, b_outer, gain_two, shift_two, cotangent, lengths, row_ids, col_ids,
    ):
        block = w_inner.shape[1] // BLOCKS
        index = lax.axis_index("dp")
        z = lax.axis_index("tensor")
        c, my = index & 1, (index >> 1) & 3
        scalars = jnp.stack([c, my, z]).astype(jnp.int32)
        tags = (row_ids, col_ids)
        vectors_one = f32(jnp.stack([b_attn_out, gain_one, shift_one]))
        vectors_two = f32(jnp.stack([b_outer, gain_two, shift_two]))

        slab, piece_a = attention_piece(
            scalars, w_query, w_key, w_value, w_attn_out, (b_query, b_value, b_inner)
        )
        with jax.named_scope("line attention weights"):
            line_a = from_all(piece_a)
        first = attention_forward(scalars, lengths, tokens, slab, piece_a, tags, n_tensor, 0)
        w_inner_t, piece_i, piece_u = ffn_pieces(tie(scalars, slab), w_inner, w_outer)

        with jax.named_scope("line inner weights"):
            line_i = from_all(tie(piece_i, *line_a, first[2]))
        own_a = jnp.concatenate([tie(line_a[0], piece_i, first[2])] + line_a[1:])
        with jax.named_scope("plane attention weights"):
            plane_a = plane(own_a)

        own_i = jnp.stack([tie(line_i[0], *plane_a)] + line_i[1:])
        near_a = jnp.stack([tie(own_a, *line_i), *plane_a])
        with jax.named_scope("core attention weights"):
            far_a = across(near_a, 1)
        with jax.named_scope("plane inner weights"):
            plane_i = plane(own_i)
        with jax.named_scope("line outer weights"):
            line_u = from_all(tie(piece_u, *line_i, far_a))

        w_attn = assemble(scalars, near_a, far_a, slab[0], 4 * QKV)
        qkv, heads_out, lse = attention_forward(scalars, lengths, tokens, w_attn, own_a, tags, n_tensor, 1, first)
        own_u = jnp.stack([tie(line_u[0], lse, *plane_i)] + line_u[1:])
        near_i = jnp.stack([tie(own_i, *line_u, lse), *plane_i])
        with jax.named_scope("core inner weights"):
            far_i = across(near_i, 1)
        with jax.named_scope("plane outer weights"):
            plane_u = plane(own_u)

        w_in = assemble(scalars, near_i, far_i, w_inner_t, block)
        normed, inv_spread, hidden, low, act, slope = inner_half(
            scalars, heads_out, w_attn, tokens, vectors_one, w_in, piece_a, own_a
        )
        near_u = jnp.stack([tie(own_u, inv_spread), *plane_u])
        with jax.named_scope("core outer weights"):
            far_u = across(near_u, 1)
        w_up = assemble(scalars, near_u, far_u, w_outer, block)
        out_rows, grad_two, sums_two = outer_half(scalars, act, w_up, hidden, cotangent, vectors_two)

        barrier = lambda *arrays: lax.optimization_barrier(arrays)
        with jax.named_scope("rows 1"):
            up_1, down_1 = rows_round(1, out_rows, out_rows)
        mine_u, other_u = weight_grad(scalars, act, grad_two)
        with jax.named_scope("core outer grad"):
            theirs_u = across(other_u, 1)
        partial, *carried = ffn_back(tie(grad_two, mine_u), grad_two, slope, w_up, w_in, 0, half)
        partial, theirs_u = barrier(partial, theirs_u)
        own_u, x_u, y_u, *via_u = core_add(mine_u, theirs_u)
        with jax.named_scope("plane one outer grad"):
            via_u = plane_one(*via_u)
        grad_one, grad_inner, db_inner, grad_one_low, sums_one = ffn_back(
            grad_two, tie(partial, own_u), slope, w_up, w_in, half, half, (normed, inv_spread, vectors_one), carried
        )
        mine_i, other_i = weight_grad(scalars, grad_inner, low)
        grad_one, mine_i, other_i, up_1, down_1, *via_u = barrier(grad_one, mine_i, other_i, up_1, down_1, *via_u)
        with jax.named_scope("rows 2"):
            up_2, down_2 = rows_round(2, up_1, down_1)
        x_u, y_u = plane_add(x_u, y_u, *via_u)
        with jax.named_scope("plane two outer grad"):
            plane_u = plane_two(x_u, y_u)
        with jax.named_scope("core inner grad"):
            theirs_i = across(other_i, 1)
        vectors = (db_inner, sums_one, sums_two)
        pieces = ()

        def shard_back(start, r):
            dtype = F32 if r else BF
            return attention_backward(
                scalars, lengths, tokens, w_attn, qkv, heads_out, lse, grad_one_low, start, tags, vectors, r, dtype, pieces
            )

        start, *pieces = shard_back(tie(grad_one, x_u), 3)
        start, theirs_i = barrier(start, theirs_i)
        own_i, x_i, y_i, *via_i = core_add(mine_i, theirs_i)
        start, *pieces = shard_back(tie(start, own_i), 2)
        start, *plane_u = barrier(start, *plane_u)
        with jax.named_scope("plane one inner grad"):
            via_i = plane_one(*[tie(v, *plane_u) for v in via_i])
        start, up_2, down_2 = barrier(start, up_2, down_2)
        with jax.named_scope("rows 3"):
            up_3, down_3 = rows_round(3, up_2, down_2)
        start, *pieces = shard_back(start, 1)
        start, own_u, *via_i = barrier(start, own_u, *via_i)
        near_u, far_u = line_sums((own_u, *plane_u))
        with jax.named_scope("line ends outer grad"):
            ends_u = line_ends(far_u)
        x_i, y_i = plane_add(x_i, y_i, *via_i)
        with jax.named_scope("plane two inner grad"):
            plane_i = plane_two(x_i, y_i)
        grad_rows, mine_a, other_a = shard_back(tie(start, x_i, far_u), 0)
        grad_rows, mine_a, other_a, ends_u, up_3, down_3 = barrier(grad_rows, mine_a, other_a, ends_u, up_3, down_3)

        with jax.named_scope("core attention grad"):
            theirs_a = across(other_a, 1)
        with jax.named_scope("grad rows 1"):
            go_1, back_1 = rows_round(1, grad_rows, grad_rows)
        own_a, x_a, y_a, *via_a = core_add(mine_a, theirs_a)
        far_u = add(far_u, tie(ends_u, own_a)[::-1])
        with jax.named_scope("line middle outer grad"):
            middle_u = line_middle(far_u)
        *via_a, plane_i_x, plane_i_y = barrier(*via_a, *plane_i)
        with jax.named_scope("plane one attention grad"):
            via_a = plane_one(*via_a)
        even_i, odd_i = line_one((own_i, plane_i_x, plane_i_y))
        go_1, back_1, odd_i, middle_u, *via_a = barrier(go_1, back_1, odd_i, middle_u, *via_a)
        with jax.named_scope("grad rows 2"):
            go_2, back_2 = rows_round(2, go_1, back_1)
        with jax.named_scope("line one inner grad"):
            got_i = along(odd_i, 1)
        x_a, y_a = plane_add(x_a, y_a, *via_a)
        with jax.named_scope("plane two attention grad"):
            plane_a = plane_two(x_a, y_a)
        layer_out = place_rows(z, tie(out_rows, *via_a), (up_1, up_2, up_3), (down_1, down_2, down_3))
        near_u = near_u + f32(middle_u[::-1])
        layer_out, got_i, *plane_a = barrier(layer_out, got_i, *plane_a)
        group = (own_a, *plane_a)
        low_a = [add(*[a[r] for a in group]) for r in range(1, n_tensor)]
        with jax.named_scope("line attention grad"):
            got_a = [along(a, r) for r, a in enumerate(low_a, 1)]
        even_i, near_u, go_2, back_2, *_ = barrier(even_i, near_u, go_2, back_2, *plane_a)
        even_i = even_i + f32(got_i)
        with jax.named_scope("line two inner grad"):
            last_i = along(even_i[1].astype(BF), 2)
        with jax.named_scope("line pair outer grad"):
            pair_u = along(near_u[1].astype(BF), 1)
        last_i, pair_u, *got_a = barrier(last_i, pair_u, *got_a)
        own_a = sum(f32(a[0]) for a in group) + f32(got_a[0]) + f32(got_a[1])
        done = jnp.concatenate(
            [line_end(own_a, got_a[2]), line_end(near_u[0], pair_u), line_end(even_i[0], last_i)]
        )
        with jax.named_scope("plane result"):
            found = plane(done)
        with jax.named_scope("grad rows 3"):
            go_3, back_3 = rows_round(3, go_2, back_2)
        go_3, back_3, *found = barrier(go_3, back_3, *found)
        near = jnp.stack([done, *found])
        with jax.named_scope("core result"):
            far = across(near, 1)
        grad_tokens = place_rows(z, grad_rows, (go_1, go_2, go_3), (back_1, back_2, back_3))
        grads = finish(scalars, near, far, block, QKV)
        grad_wq, grad_wk, grad_wv, grad_wo, grad_wu, grad_wi, *vectors = grads
        grad_bq, grad_bv, grad_bi, gain_1, shift_1, b_1, gain_2, shift_2, b_2 = vectors

        return (
            layer_out,
            grad_tokens,
            grad_wq.T,
            grad_bq,
            grad_wk.T,
            grad_wv.T,
            grad_bv,
            grad_wo,
            b_1,
            gain_1,
            shift_1,
            grad_wi,
            grad_bi,
            grad_wu,
            b_2,
            gain_2,
            shift_2,
        )

    return body


def solution(mesh):
    rows, columns, out = P("dp", None), P(None, "tensor"), P("tensor", None)
    one = P("tensor")
    in_specs = (
        rows, columns, one, columns, columns, one, out, P(), P(), P(), columns, one, out, P(), P(), P(),
        rows, P("dp"), rows, rows,
    )
    out_specs = (
        rows, rows, columns, one, columns, columns, one, out, P(), P(), P(), columns, one, out, P(), P(), P(),
    )
    body = build(mesh.shape["dp"], mesh.shape["tensor"])
    return jax.shard_map(body, mesh=mesh, in_specs=in_specs, out_specs=out_specs, check_vma=False)
```
